128 devices in a mesh: clip: 4 (over x), owner: 32 (over z, y, core).
Axes of the slice: x: 4, y: 4, z: 4, core: 2. Of those that a mesh axis runs over, the one named last changes fastest.
Arguments:
- mask_tiles: bfloat16 [2048, 16384], P('owner'), may hold values from 0 to 1
- correlation: int32 [256, 4], replicated, may hold values from 0 to 2047, as said below
- target: bfloat16 [256, 65536], P(('clip', 'owner')), may hold values from 0 to 1
- socs_kernels: float32 [2, 12, 15, 15], replicated, may hold values from -0.375 to 0.375
- socs_weights: float32 [12], replicated, may hold values from 0.2 to 1
Outputs:
- mask_grad: float32 [2048, 16384], P('owner', 'clip')
- clip_loss: float32 [256], P(('clip', 'owner'))
The draws below stay inside these ranges and needn't reach their ends.
Inputs may be any that keep to these rules, and one draw needn't show every extreme that they name: `correlation`: tile t lies in row t // 64 and column t % 64 of the mask's tile grid and belongs to owner t // 64. Each clip's ids are the 2 x 2 neighbouring tiles at grid positions (r, c), (r, c+1), (r+1, c), (r+1, c+1), in that order, with r even. The clips of one device (aligned blocks of 2 clips) lie in distinct grid rows, so at most 2 of its 8 ids belong to one owner, and one pair of owners, the same for every block, gets exactly 2 from every block.
All inputs are finite; a program needn't handle non-finite values.
Results may differ from the reference program's by a relative error of at most 0.013.
Values may be sent and summed in bfloat16 or wider, within the bound.
A program may use at most 128 MiB of HBM per device.

```python
import math
import jax
import jax.numpy as jnp
from jax import lax

TS = 128
NKER = 12
KS = 15
CLIP_DEV = 2
TILE_OWN = 64
TILES = 2048
CLIPS = 256
N_OWNER = 32


def draw_correlation(key, part):
    key = jax.random.fold_in(key, 7)
    block_count = CLIPS // CLIP_DEV
    row_pairs = N_OWNER // 2
    hot_pair = jax.random.randint(jax.random.fold_in(key, 1), (), 0, row_pairs)
    block_keys = jax.random.split(jax.random.fold_in(key, 2), block_count)

    def draw_block(block_key):
        key_rank, key_shuffle, key_column = jax.random.split(block_key, 3)
        ranking = jax.random.permutation(key_rank, row_pairs).astype(jnp.int32)
        pair_ids = jnp.arange(row_pairs, dtype=jnp.int32)
        scores = ranking + jnp.where(pair_ids == hot_pair, -row_pairs, 0)
        picked = jnp.argsort(scores)[:CLIP_DEV].astype(jnp.int32)
        picked = picked[jax.random.permutation(key_shuffle, CLIP_DEV)]
        grid_rows = 2 * picked
        columns = jax.random.randint(key_column, (CLIP_DEV,), 0, TILE_OWN - 1).astype(jnp.int32)
        upper = grid_rows * TILE_OWN + columns
        lower = upper + TILE_OWN
        return jnp.stack([upper, upper + 1, lower, lower + 1], axis=1).astype(jnp.int32)
    tile_ids = jax.vmap(draw_block)(block_keys)
    return tile_ids.reshape(CLIPS, 4)


def block_levels(rng, dims, cuts, least, high):
    loudness, own = 1.0, jax.random.fold_in(rng, 6)
    for axis_at, shards_of in cuts:
        steps = jnp.exp(jax.random.uniform(jax.random.fold_in(own, axis_at), (shards_of,), jnp.float32, least / len(cuts), high / len(cuts)))
        loudness = loudness * jnp.repeat(steps, dims[axis_at] // shards_of).reshape([-1 if axis == axis_at else 1 for axis in range(len(dims))])
    return loudness


def scatter_about(rng, shape, scale, most, kind=jnp.bfloat16):
    return jnp.clip(scale * jax.random.normal(rng, shape, jnp.float32), -most, most).astype(kind)


def setup_inputs(seed: int = 0) -> dict:
    streams_of = jax.random.split(jax.random.key(seed), 6)
    return {
        "mask_tiles": jnp.clip(1.0 * jax.random.uniform(streams_of[0], (TILES, TS * TS), jnp.float32) ** block_levels(streams_of[0], (TILES, TS * TS), ((0, 32),), -0.2, 0.2), 0.0, 1.0).astype(jnp.bfloat16),
        "correlation": draw_correlation(jax.random.fold_in(streams_of[5], 71), 0),
        "target": jnp.clip(1.0 * jax.random.uniform(streams_of[2], (CLIPS, 4 * TS * TS), jnp.float32) ** block_levels(streams_of[2], (CLIPS, 4 * TS * TS), ((0, 128),), -0.2, 0.2), 0.0, 1.0).astype(jnp.bfloat16),
        "socs_kernels": scatter_about(streams_of[3], (2, NKER, KS, KS), (KS * KS) ** -0.5, 0.375, jnp.float32),
        "socs_weights": jnp.clip(jnp.exp(jax.random.uniform(streams_of[4], (NKER,), jnp.float32, math.log(0.2), math.log(1.0))), 0.2, 1.0),
    }


steepness = 10.0
threshold = 0.3


def matmul(former, latter):
    return jnp.dot(former, latter, preferred_element_type=jnp.float32)


def dft_tables(extent):
    positions = jnp.arange(extent, dtype=jnp.int32)
    phases = (positions[:, None] * positions[None, :]) % extent
    angles = phases.astype(jnp.float32) * (2.0 * math.pi / extent)
    fwd_re = jnp.cos(angles).astype(jnp.bfloat16)
    fwd_im = (-jnp.sin(angles)).astype(jnp.bfloat16)
    inv_re = (jnp.cos(angles) / extent).astype(jnp.bfloat16)
    inv_im = (jnp.sin(angles) / extent).astype(jnp.bfloat16)
    return fwd_re, fwd_im, inv_re, inv_im


def kernel_spectra(socs_kernels, extent):
    kernel_span = socs_kernels.shape[-1]
    frequency = jnp.arange(extent, dtype=jnp.int32)
    offsets = jnp.arange(kernel_span, dtype=jnp.int32) - kernel_span // 2
    phases = (frequency[:, None] * offsets[None, :]) % extent
    angles = phases.astype(jnp.float32) * (2.0 * math.pi / extent)
    wave_re = jnp.cos(angles)
    wave_im = -jnp.sin(angles)
    highest = lax.Precision.HIGHEST
    ker_re = socs_kernels[0]
    ker_im = socs_kernels[1]
    mid_re = jnp.einsum("kab,vb->kav", ker_re, wave_re, precision=highest) - jnp.einsum("kab,vb->kav", ker_im, wave_im, precision=highest)
    mid_im = jnp.einsum("kab,vb->kav", ker_re, wave_im, precision=highest) + jnp.einsum("kab,vb->kav", ker_im, wave_re, precision=highest)
    spec_re = jnp.einsum("ua,kav->kuv", wave_re, mid_re, precision=highest) - jnp.einsum("ua,kav->kuv", wave_im, mid_im, precision=highest)
    spec_im = jnp.einsum("ua,kav->kuv", wave_re, mid_im, precision=highest) + jnp.einsum("ua,kav->kuv", wave_im, mid_re, precision=highest)
    return spec_re, spec_im


def clip_pass(window, target_row, spec_re, spec_im, socs_weights, tables, ambit):
    fwd_re, fwd_im, inv_re, inv_im = tables
    extent = window.shape[0]
    kernel_count = spec_re.shape[0]
    left_re = matmul(fwd_re, window).astype(jnp.bfloat16)
    left_im = matmul(fwd_im, window).astype(jnp.bfloat16)
    spec_real = matmul(left_re, fwd_re) - matmul(left_im, fwd_im)
    spec_imag = matmul(left_re, fwd_im) + matmul(left_im, fwd_re)
    intensity = jnp.zeros((extent, extent), jnp.float32)
    fields = []
    for kernel in range(kernel_count):
        prod_re = (spec_real * spec_re[kernel] - spec_imag * spec_im[kernel]).astype(jnp.bfloat16)
        prod_im = (spec_real * spec_im[kernel] + spec_imag * spec_re[kernel]).astype(jnp.bfloat16)
        half_re = (matmul(inv_re, prod_re) - matmul(inv_im, prod_im)).astype(jnp.bfloat16)
        half_im = (matmul(inv_re, prod_im) + matmul(inv_im, prod_re)).astype(jnp.bfloat16)
        field_re = matmul(half_re, inv_re) - matmul(half_im, inv_im)
        field_im = matmul(half_re, inv_im) + matmul(half_im, inv_re)
        scaled = socs_weights[kernel] / kernel_count
        intensity = intensity + scaled * (field_re * field_re + field_im * field_im)
        fields.append((field_re, field_im))
    resist = jax.nn.sigmoid(steepness * (intensity - threshold))
    positions = jnp.arange(extent, dtype=jnp.int32)
    inner = ((positions >= ambit) & (positions < extent - ambit)).astype(jnp.float32)
    interior = inner[:, None] * inner[None, :]
    mismatch = (resist - target_row.astype(jnp.float32).reshape(extent, extent)) * interior
    clip_error = jnp.sum(mismatch * mismatch) / float((extent - 2 * ambit) ** 2)
    sensitivity = 2.0 * mismatch * resist * (1.0 - resist) * steepness
    summed_re = jnp.zeros((extent, extent), jnp.float32)
    summed_im = jnp.zeros((extent, extent), jnp.float32)
    for kernel in range(kernel_count):
        field_re, field_im = fields[kernel]
        factor = sensitivity * (2.0 * socs_weights[kernel] / kernel_count)
        grad_re = (factor * field_re).astype(jnp.bfloat16)
        grad_im = (factor * field_im).astype(jnp.bfloat16)
        back_re = (matmul(fwd_re, grad_re) - matmul(fwd_im, grad_im)).astype(jnp.bfloat16)
        back_im = (matmul(fwd_re, grad_im) + matmul(fwd_im, grad_re)).astype(jnp.bfloat16)
        turn_re = matmul(back_re, fwd_re) - matmul(back_im, fwd_im)
        turn_im = matmul(back_re, fwd_im) + matmul(back_im, fwd_re)
        summed_re = summed_re + spec_re[kernel] * turn_re + spec_im[kernel] * turn_im
        summed_im = summed_im + spec_re[kernel] * turn_im - spec_im[kernel] * turn_re
    summed_re = summed_re.astype(jnp.bfloat16)
    summed_im = summed_im.astype(jnp.bfloat16)
    out_re = (matmul(inv_re, summed_re) - matmul(inv_im, summed_im)).astype(jnp.bfloat16)
    out_im = (matmul(inv_re, summed_im) + matmul(inv_im, summed_re)).astype(jnp.bfloat16)
    window_grad = matmul(out_re, inv_re) - matmul(out_im, inv_im)
    return window_grad, clip_error


def assemble(tile_rows, edge):
    return tile_rows.reshape(2, 2, edge, edge).transpose(0, 2, 1, 3).reshape(2 * edge, 2 * edge)


def split_window(window_grad, edge):
    return window_grad.reshape(2, edge, 2, edge).transpose(0, 2, 1, 3).reshape(4, edge * edge)


def reference(mask_tiles, correlation, target, socs_kernels, socs_weights):
    extent = 2 * TS
    ambit = socs_kernels.shape[-1] // 2
    tables = dft_tables(extent)
    spec_re, spec_im = kernel_spectra(socs_kernels, extent)

    def per_clip(clip_args):
        tile_ids, target_row = clip_args
        window = assemble(mask_tiles[tile_ids], TS)
        window_grad, clip_error = clip_pass(window, target_row, spec_re, spec_im, socs_weights, tables, ambit)
        return split_window(window_grad, TS), clip_error

    pieces, losses = lax.map(per_clip, (correlation, target))
    mask_grad = jnp.zeros((TILES, TS * TS), jnp.float32).at[correlation.reshape(-1)].add(pieces.reshape(-1, TS * TS))
    return mask_grad, losses
```

```python
import functools

import jax
import jax.numpy as jnp
import ml_dtypes
import numpy as np
from jax import lax
from jax.experimental import pallas as pl
from jax.experimental.pallas import tpu as pltpu
from jax.sharding import PartitionSpec as P

TS=128; W=256; HF=128; KS=15; AM=7; NK=12; CH=24
f32=jnp.float32; bf16=jnp.bfloat16

def tables():
    u = np.arange(HF) + 0.5
    y = np.arange(W)
    ang = 2*np.pi*u[:,None]*y[None,:]/W
    R = np.concatenate([np.cos(ang), np.sin(ang)], 0)
    b = np.arange(KS)-AM
    ang2 = 2*np.pi*u[:,None]*b[None,:]/W
    T = np.concatenate([np.cos(ang2), np.sin(ang2)], 0)
    T16 = np.zeros((W,16)); T16[:,:KS]=T
    hi = T16.astype(np.float32).astype(ml_dtypes.bfloat16)
    lo = (T16-hi.astype(np.float64)).astype(np.float32).astype(ml_dtypes.bfloat16)
    T3 = np.concatenate([hi,hi,lo],1)
    TB = np.zeros((W, 128)); TB[:,:KS]=T
    TB = TB.T.astype(np.float32)
    Rb = R.astype(np.float32).astype(ml_dtypes.bfloat16)
    return Rb, np.ascontiguousarray(Rb.T), T3, TB

def dot(a,b):
    return jnp.dot(a,b,preferred_element_type=f32)

def gen_spectra(taps_ref, sw_ref, t3_ref, tb_ref, pad, mid, spec, level, su):
    pad[...] = jnp.zeros(pad.shape, f32)
    for c in range(CH):
        pad[c,:KS,:KS] = taps_ref[c]*jnp.sqrt(sw_ref[c % NK]*(1.0/NK))
    level[...] = jnp.broadcast_to(jnp.sum(jnp.sum(pad[...],axis=1,keepdims=True),axis=2,keepdims=True)*0.5,level.shape)
    m = jnp.dot(pad[...].reshape(CH*16,128), tb_ref[...], precision=lax.Precision.HIGHEST, preferred_element_type=f32).reshape(CH,16,W)
    hi = m.astype(bf16)
    lo = (m-hi.astype(f32)).astype(bf16)
    mid[:,0:16,:]=hi
    mid[:,16:32,:]=lo
    mid[:,32:48,:]=hi
    def body(c,_):
        q = dot(t3_ref[...], mid[c])
        cc=q[:HF,:HF]; cs=q[:HF,HF:]; sc=q[HF:,:HF]; ss=q[HF:,HF:]
        spec[c,0]=cc-ss; spec[c,1]=sc+cs; spec[c,2]=cc+ss; spec[c,3]=sc-cs
        return 0
    lax.fori_loop(0,CH,body,0,unroll=su)

def compute(n, window, target, spec, r_ref, rt_ref, sfreq, acc, field, inten, put, loss_ref, level, rsum_ref, fu, bu):
    R=r_ref[...]; RT=rt_ref[...]
    for i in range(n):
        x = window(i)
        t = (dot(R, x)-rsum_ref[...]).astype(bf16)
        s = dot(t, RT)*(0.5/(HF*HF))
        cc=s[:HF,:HF]; cs=s[:HF,HF:]; sc=s[HF:,:HF]; ss=s[HF:,HF:]
        sfreq[i,0]=cc-ss; sfreq[i,1]=sc+cs; sfreq[i,2]=cc+ss; sfreq[i,3]=sc-cs
        inten[i]=jnp.zeros((W,W),f32)
    def fwd(c,_):
        for i in range(n):
            p,q,p2,q2 = (sfreq[i,j] for j in range(4))
            m,nn,m2,n2 = (spec[c,j] for j in range(4))
            a=p*m-q*nn; b=p*nn+q*m; a2=p2*m2-q2*n2; b2=p2*n2+q2*m2
            P=jnp.concatenate([jnp.concatenate([a+a2,b-b2],1),jnp.concatenate([b+b2,a2-a],1)],0).astype(bf16)
            U=dot(P,r_ref[...]).astype(bf16)
            E=dot(rt_ref[...],U)+level[c]
            field[c,i]=E
            inten[i]=inten[i]+E*E
        return 0
    lax.fori_loop(0,CH,fwd,0,unroll=fu)
    row=lax.broadcasted_iota(jnp.int32,(W,W),0); col=lax.broadcasted_iota(jnp.int32,(W,W),1)
    inside=(row>=AM)&(row<W-AM)&(col>=AM)&(col<W-AM)
    for i in range(n):
        I=inten[i]
        Rs=1.0/(1.0+jnp.exp(-10.0*(I-0.3)))
        Z=jnp.where(inside,Rs-target(i).astype(f32),0.0)
        loss_ref[i]=jnp.sum(Z*Z)*(1.0/((W-2*AM)**2))
        inten[i]=40.0*Z*Rs*(1.0-Rs)
        acc[i]=jnp.zeros((4,HF,HF),f32)
    def bwd(c,_):
        for i in range(n):
            g=(inten[i]*field[c,i]).astype(bf16)
            V=dot(g,rt_ref[...]).astype(bf16)
            s=dot(r_ref[...],V)
            cc=s[:HF,:HF]; cs=s[:HF,HF:]; sc=s[HF:,:HF]; ss=s[HF:,HF:]
            p=cc-ss; q=sc+cs; p2=cc+ss; q2=sc-cs
            m,nn,m2,n2 = (spec[c,j] for j in range(4))
            acc[i,0]+=p*m+q*nn
            acc[i,1]+=q*m-p*nn
            acc[i,2]+=p2*m2+q2*n2
            acc[i,3]+=q2*m2-p2*n2
        return 0
    lax.fori_loop(0,CH,bwd,0,unroll=bu)
    for i in range(n):
        a,b,a2,b2=(acc[i,j] for j in range(4))
        P=(jnp.concatenate([jnp.concatenate([a+a2,b-b2],1),jnp.concatenate([b+b2,a2-a],1)],0)*(0.5/(HF*HF))).astype(bf16)
        U=dot(P,r_ref[...]).astype(bf16)
        put(i,dot(rt_ref[...],U))

def clip_kernel(su, fu, bu, idx_ref, sw_ref, tiles_ref, target_ref, taps_ref, r_ref, rt_ref, t3_ref, tb_ref, rsum_ref, grad_ref, loss_ref, pad, mid, spec, sfreq, acc, field, inten, level):
    gen_spectra(taps_ref, sw_ref, t3_ref, tb_ref, pad, mid, spec, level, su)
    def window(i):
        t=[tiles_ref[idx_ref[4*i+j]] for j in range(4)]
        return jnp.concatenate([jnp.concatenate(t[:2],1),jnp.concatenate(t[2:],1)],0)
    def put(i,d):
        d=d.astype(bf16)
        for j in range(4):
            r,c=divmod(j,2)
            grad_ref[4*i+j]=d[r*HF:(r+1)*HF,c*HF:(c+1)*HF]
    compute(2, window, lambda i: target_ref[i], spec, r_ref, rt_ref, sfreq, acc, field, inten, put, loss_ref, level, rsum_ref, fu, bu)


def clip_grads(idx, sw, tiles, target, taps):
    Rb,RTb,T3,TB=tables()
    V=pl.BlockSpec(memory_space=pltpu.VMEM); S=pl.BlockSpec(memory_space=pltpu.SMEM)
    rsum=np.broadcast_to(0.5*Rb.astype(np.float32).sum(1,keepdims=True),(W,W)).copy()
    return pl.pallas_call(functools.partial(clip_kernel,8,4,4),
        out_shape=(jax.ShapeDtypeStruct((8,TS,TS),bf16), jax.ShapeDtypeStruct((2,),f32)),
        in_specs=[S,S]+[V]*8, out_specs=(V,S),
        scratch_shapes=[pltpu.VMEM((CH,16,128),f32), pltpu.VMEM((CH,48,W),bf16), pltpu.VMEM((CH,4,HF,HF),f32),
            pltpu.VMEM((2,4,HF,HF),f32), pltpu.VMEM((2,4,HF,HF),f32), pltpu.VMEM((CH,2,W,W),f32), pltpu.VMEM((2,W,W),f32), pltpu.VMEM((CH,1,W),f32)],
        compiler_params=pltpu.CompilerParams(vmem_limit_bytes=56*2**20),
    )(idx, sw, tiles, target, taps, jnp.asarray(Rb), jnp.asarray(RTb), jnp.asarray(T3), jnp.asarray(TB), jnp.asarray(rsum))


def sum_kernel(first_ref, got_ref, out_ref, total):
    chip = lax.axis_index("owner") // 2
    total[...] = jnp.zeros(total.shape, f32)

    def step(s, _):
        for i in range(2):
            first = first_ref[2 * s + i]

            @pl.when(first // 128 == chip)
            def _():
                at = pl.multiple_of(first % 64 * 32, 32)
                total[pl.ds(at, 32), :] += got_ref[s, 0].astype(f32)
                total[pl.ds(at + 32, 32), :] += got_ref[s, 1].astype(f32)
        return 0

    lax.fori_loop(0, 128, step, 0)
    for t in range(8):
        for j in range(32):
            out_ref[8 * t : 8 * t + 8, 128 * j : 128 * j + 128] = total[pl.ds(256 * t + j, 8, stride=32), :]


def body(mask_tiles, correlation, target, socs_kernels, socs_weights):
    plane = lax.axis_index("clip")
    owner = lax.axis_index("owner")
    first = correlation[:, 0]
    near = lax.dynamic_slice(first, (plane * 64,), (64,)).reshape(32, 2)
    hit = near // 128 == owner // 2
    column = jnp.where(hit[:, 0], near[:, 0], near[:, 1]) % 64
    column = jnp.minimum(column, 62)
    outgoing = mask_tiles.reshape(64, TS, TS)[column[:, None] + jnp.arange(2)]
    incoming = lax.all_to_all(outgoing, "owner", split_axis=0, concat_axis=0, tiled=True).reshape(64, TS, TS)
    own = near[owner]
    idx = (own[:, None] // 128 * 4 + jnp.arange(4)).reshape(8)
    grads, losses = clip_grads(idx, socs_weights, incoming, target.reshape(2, W, W), socs_kernels.reshape(CH, KS, KS))
    which = (jnp.arange(16) == own[1] // 128).astype(jnp.int32)
    back = grads.reshape(2, 2, 2, 4, 32, TS)[which]
    back = back.transpose(3, 0, 1, 2, 4, 5).reshape(128, 2, 32, TS)
    got = lax.all_to_all(back, ("clip", "owner"), split_axis=0, concat_axis=0, tiled=True)
    V=pl.BlockSpec(memory_space=pltpu.VMEM); S=pl.BlockSpec(memory_space=pltpu.SMEM)
    mask_grad = pl.pallas_call(sum_kernel, out_shape=jax.ShapeDtypeStruct((64, 4096), f32),
        in_specs=[S, V], out_specs=V, scratch_shapes=[pltpu.VMEM((2048, 128), f32)],
    )(first, got)
    return mask_grad, losses


def solution(mesh):
    placed = (P("owner", None), P(), P(("clip", "owner"), None), P(), P())
    return jax.shard_map(body, mesh=mesh, in_specs=placed,
        out_specs=(P("owner", "clip"), P(("clip", "owner"))), check_vma=False)
```

```python
import functools

import jax
import jax.numpy as jnp
import ml_dtypes
import numpy as np
from jax import lax
from jax.experimental import pallas as pl
from jax.experimental.pallas import tpu as pltpu
from jax.sharding import PartitionSpec as P

TS=128; W=256; HF=128; KS=15; AM=7; NK=12; CH=24
MESH = pl.DeviceIdType.MESH
f32=jnp.float32; bf16=jnp.bfloat16

def tables():
    u = np.arange(HF) + 0.5
    y = np.arange(W)
    ang = 2*np.pi*u[:,None]*y[None,:]/W
    R = np.concatenate([np.cos(ang), np.sin(ang)], 0)
    b = np.arange(KS)-AM
    ang2 = 2*np.pi*u[:,None]*b[None,:]/W
    T = np.concatenate([np.cos(ang2), np.sin(ang2)], 0)
    T16 = np.zeros((W,16)); T16[:,:KS]=T
    hi = T16.astype(np.float32).astype(ml_dtypes.bfloat16)
    lo = (T16-hi.astype(np.float64)).astype(np.float32).astype(ml_dtypes.bfloat16)
    T3 = np.concatenate([hi,hi,lo],1)
    TB = np.zeros((W, 128)); TB[:,:KS]=T
    TB = TB.T.astype(np.float32)
    Rb = R.astype(np.float32).astype(ml_dtypes.bfloat16)
    return Rb, np.ascontiguousarray(Rb.T), T3, TB

def dot(a,b):
    return jnp.dot(a,b,preferred_element_type=f32)

def gen_spectra(taps_ref, sw_ref, t3_ref, tb_ref, pad, mid, spec, level, su):
    pad[...] = jnp.zeros(pad.shape, f32)
    for c in range(CH):
        pad[c,:KS,:KS] = taps_ref[c]*jnp.sqrt(sw_ref[c % NK]*(1.0/NK))
    level[...] = jnp.broadcast_to(jnp.sum(jnp.sum(pad[...],axis=1,keepdims=True),axis=2,keepdims=True)*0.5,level.shape)
    m = jnp.dot(pad[...].reshape(CH*16,128), tb_ref[...], precision=lax.Precision.HIGHEST, preferred_element_type=f32).reshape(CH,16,W)
    hi = m.astype(bf16)
    lo = (m-hi.astype(f32)).astype(bf16)
    mid[:,0:16,:]=hi
    mid[:,16:32,:]=lo
    mid[:,32:48,:]=hi
    def body(c,_):
        q = dot(t3_ref[...], mid[c])
        cc=q[:HF,:HF]; cs=q[:HF,HF:]; sc=q[HF:,:HF]; ss=q[HF:,HF:]
        spec[c,0]=cc-ss; spec[c,1]=sc+cs; spec[c,2]=cc+ss; spec[c,3]=sc-cs
        return 0
    lax.fori_loop(0,CH,body,0,unroll=su)

def compute(n, window, target, spec, r_ref, rt_ref, sfreq, acc, field, inten, put, loss_ref, level, rsum_ref, fu, bu):
    R=r_ref[...]; RT=rt_ref[...]
    for i in range(n):
        x = window(i)
        t = (dot(R, x)-rsum_ref[...]).astype(bf16)
        s = dot(t, RT)*(0.5/(HF*HF))
        cc=s[:HF,:HF]; cs=s[:HF,HF:]; sc=s[HF:,:HF]; ss=s[HF:,HF:]
        sfreq[i,0]=cc-ss; sfreq[i,1]=sc+cs; sfreq[i,2]=cc+ss; sfreq[i,3]=sc-cs
        inten[i]=jnp.zeros((W,W),f32)
    def fwd(c,_):
        for i in range(n):
            p,q,p2,q2 = (sfreq[i,j] for j in range(4))
            m,nn,m2,n2 = (spec[c,j] for j in range(4))
            a=p*m-q*nn; b=p*nn+q*m; a2=p2*m2-q2*n2; b2=p2*n2+q2*m2
            P=jnp.concatenate([jnp.concatenate([a+a2,b-b2],1),jnp.concatenate([b+b2,a2-a],1)],0).astype(bf16)
            U=dot(P,r_ref[...]).astype(bf16)
            E=dot(rt_ref[...],U)+level[c]
            field[c,i]=E
            inten[i]=inten[i]+E*E
        return 0
    lax.fori_loop(0,CH,fwd,0,unroll=fu)
    row=lax.broadcasted_iota(jnp.int32,(W,W),0); col=lax.broadcasted_iota(jnp.int32,(W,W),1)
    inside=(row>=AM)&(row<W-AM)&(col>=AM)&(col<W-AM)
    for i in range(n):
        I=inten[i]
        Rs=1.0/(1.0+jnp.exp(-10.0*(I-0.3)))
        Z=jnp.where(inside,Rs-target(i).astype(f32),0.0)
        loss_ref[i]=jnp.sum(Z*Z)*(1.0/((W-2*AM)**2))
        inten[i]=40.0*Z*Rs*(1.0-Rs)
        acc[i]=jnp.zeros((4,HF,HF),f32)
    def bwd(c,_):
        for i in range(n):
            g=(inten[i]*field[c,i]).astype(bf16)
            V=dot(g,rt_ref[...]).astype(bf16)
            s=dot(r_ref[...],V)
            cc=s[:HF,:HF]; cs=s[:HF,HF:]; sc=s[HF:,:HF]; ss=s[HF:,HF:]
            p=cc-ss; q=sc+cs; p2=cc+ss; q2=sc-cs
            m,nn,m2,n2 = (spec[c,j] for j in range(4))
            acc[i,0]+=p*m+q*nn
            acc[i,1]+=q*m-p*nn
            acc[i,2]+=p2*m2+q2*n2
            acc[i,3]+=q2*m2-p2*n2
        return 0
    lax.fori_loop(0,CH,bwd,0,unroll=bu)
    for i in range(n):
        a,b,a2,b2=(acc[i,j] for j in range(4))
        P=(jnp.concatenate([jnp.concatenate([a+a2,b-b2],1),jnp.concatenate([b+b2,a2-a],1)],0)*(0.5/(HF*HF))).astype(bf16)
        U=dot(P,r_ref[...]).astype(bf16)
        put(i,dot(rt_ref[...],U))


def partner(k, plane, owner):
    y = (owner // 2 + k // 2) % 4
    z = (owner // 8 + k // 8) % 4
    return (plane + k // 32) % 4, z * 8 + y * 2 + (owner + k) % 2


def step_kernel(first, sw, mask, target, taps, r, rt, t3, tb, rsum, got, loss,
        out, recv, back, grads, pad, mid, spec, sfreq, acc, field, inten, level, fs, fr, bs, br, ls):
    plane = lax.axis_index("clip")
    owner = lax.axis_index("owner")
    me = plane * 32 + owner
    chip = owner // 2
    barrier = pltpu.get_barrier_semaphore()

    def greet(k, _):
        pl.semaphore_signal(barrier, inc=1, device_id=partner(k, plane, owner), device_id_type=MESH)
        return 0

    lax.fori_loop(1, 128, greet, 0)

    def pick(d, _):
        near = first[plane * 64 + 2 * d]
        far = first[plane * 64 + 2 * d + 1]
        column = jnp.minimum(lax.rem(jnp.where(near // 128 == chip, near, far), 64), 62)
        out[d, 0] = mask[column]
        out[d, 1] = mask[column + 1]
        return 0

    lax.fori_loop(0, 32, pick, 0)
    pl.semaphore_wait(barrier, 127)

    def fetch(k, _):
        _, to = partner(k, plane, owner)
        pltpu.make_async_remote_copy(src_ref=out.at[to], dst_ref=recv.at[owner], send_sem=fs, recv_sem=fr,
            device_id=(plane, to), device_id_type=MESH).start()
        return 0

    lax.fori_loop(1, 32, fetch, 0)
    recv[owner] = out[owner]
    gen_spectra(taps, sw, t3, tb, pad, mid, spec, level, 8)
    pltpu.make_async_copy(recv.at[pl.ds(0, 31)], recv.at[pl.ds(0, 31)], fr).wait()

    def window(i):
        pair = first[2 * me + i] // 128
        t = [recv[2 * pair + j // 2, j % 2] for j in range(4)]
        return jnp.concatenate([jnp.concatenate(t[:2], 1), jnp.concatenate(t[2:], 1)], 0)

    def put(i, d):
        d = d.astype(bf16)
        for core in range(2):
            for q in range(4):
                for slot in range(2):
                    row = core * TS + q * 32
                    grads[i, q, core, slot] = d[row : row + 32, slot * TS : slot * TS + TS]

    compute(2, window, lambda i: target[i], spec, r, rt, sfreq, acc, field, inten, put, loss, level, rsum, 4, 4)
    last = first[2 * me + 1] // 128

    def stage(d, _):
        which = jnp.where(last == d, 1, 0)
        for q in range(4):
            for core in range(2):
                back[q * 32 + 2 * d + core] = grads[which, q, core]
        return 0

    lax.fori_loop(0, 16, stage, 0)

    def send(k, _):
        p, to = partner(k, plane, owner)
        pltpu.make_async_remote_copy(src_ref=back.at[p * 32 + to], dst_ref=got.at[me], send_sem=bs, recv_sem=br,
            device_id=(p, to), device_id_type=MESH).start()
        return 0

    lax.fori_loop(1, 128, send, 0)
    own = pltpu.make_async_copy(back.at[me], got.at[me], ls)
    own.start()
    own.wait()
    pltpu.make_async_copy(out.at[pl.ds(0, 31)], out.at[pl.ds(0, 31)], fs).wait()
    pltpu.make_async_copy(back.at[pl.ds(0, 127)], back.at[pl.ds(0, 127)], bs).wait()
    pltpu.make_async_copy(got.at[pl.ds(0, 127)], got.at[pl.ds(0, 127)], br).wait()


def sum_kernel(first, got, out, total):
    chip = lax.axis_index("owner") // 2
    total[...] = jnp.zeros(total.shape, f32)

    def step(s, _):
        near = first[2 * s]
        far = first[2 * s + 1]
        mine = jnp.where(near // 128 == chip, near, far)
        column = jnp.where(mine // 128 == chip, jnp.minimum(lax.rem(mine, 64), 62), 64)
        at = pl.ds(pl.multiple_of(column * 32, 32), 64)
        total[at, :] += got[s].reshape(64, TS).astype(f32)
        return 0

    lax.fori_loop(0, 128, step, 0, unroll=4)
    for t in range(8):
        for j in range(32):
            out[8 * t : 8 * t + 8, 128 * j : 128 * j + 128] = total[pl.ds(256 * t + j, 8, stride=32), :]


def body(mask_tiles, correlation, target, socs_kernels, socs_weights):
    first = correlation[:, 0]
    Rb, RTb, T3, TB = tables()
    rsum = np.broadcast_to(0.5 * Rb.astype(np.float32).sum(1, keepdims=True), (W, W)).copy()
    V = pl.BlockSpec(memory_space=pltpu.VMEM)
    S = pl.BlockSpec(memory_space=pltpu.SMEM)
    A = pl.BlockSpec(memory_space=pl.ANY)
    got, losses = pl.pallas_call(
        step_kernel,
        out_shape=(jax.ShapeDtypeStruct((128, 2, 32, TS), bf16), jax.ShapeDtypeStruct((2,), f32)),
        in_specs=[S, S] + [V] * 8,
        out_specs=(A, S),
        scratch_shapes=[
            pltpu.VMEM((32, 2, TS, TS), bf16),
            pltpu.VMEM((32, 2, TS, TS), bf16),
            pltpu.VMEM((128, 2, 32, TS), bf16),
            pltpu.VMEM((2, 4, 2, 2, 32, TS), bf16),
            pltpu.VMEM((CH, 16, 128), f32),
            pltpu.VMEM((CH, 48, W), bf16),
            pltpu.VMEM((CH, 4, HF, HF), f32),
            pltpu.VMEM((2, 4, HF, HF), f32),
            pltpu.VMEM((2, 4, HF, HF), f32),
            pltpu.VMEM((CH, 2, W, W), f32),
            pltpu.VMEM((2, W, W), f32),
            pltpu.VMEM((CH, 1, W), f32),
        ]
        + [pltpu.SemaphoreType.DMA] * 5,
        compiler_params=pltpu.CompilerParams(vmem_limit_bytes=56 * 2**20, collective_id=0, has_side_effects=True),
    )(first, socs_weights, mask_tiles.reshape(64, TS, TS), target.reshape(2, W, W), socs_kernels.reshape(CH, KS, KS),
        jnp.asarray(Rb), jnp.asarray(RTb), jnp.asarray(T3), jnp.asarray(TB), jnp.asarray(rsum))
    mask_grad = pl.pallas_call(sum_kernel, out_shape=jax.ShapeDtypeStruct((64, 4096), f32),
        in_specs=[S, V], out_specs=V, scratch_shapes=[pltpu.VMEM((66 * 32, TS), f32)],
    )(first, got)
    return mask_grad, losses


def solution(mesh):
    placed = (P("owner", None), P(), P(("clip", "owner"), None), P(), P())
    return jax.shard_map(body, mesh=mesh, in_specs=placed,
        out_specs=(P("owner", "clip"), P(("clip", "owner"))), check_vma=False)
```

```python
import functools

import jax
import jax.numpy as jnp
import ml_dtypes
import numpy as np
from jax import lax
from jax.experimental import pallas as pl
from jax.experimental.pallas import tpu as pltpu
from jax.sharding import PartitionSpec as P

TS=128; W=256; HF=128; KS=15; AM=7; NK=12; CH=24
MESH = pl.DeviceIdType.MESH
f32=jnp.float32; bf16=jnp.bfloat16

def tables():
    u = np.arange(HF) + 0.5
    y = np.arange(W)
    ang = 2*np.pi*u[:,None]*y[None,:]/W
    R = np.concatenate([np.cos(ang), np.sin(ang)], 0)
    b = np.arange(KS)-AM
    ang2 = 2*np.pi*u[:,None]*b[None,:]/W
    T = np.concatenate([np.cos(ang2), np.sin(ang2)], 0)
    T16 = np.zeros((W,16)); T16[:,:KS]=T
    hi = T16.astype(np.float32).astype(ml_dtypes.bfloat16)
    lo = (T16-hi.astype(np.float64)).astype(np.float32).astype(ml_dtypes.bfloat16)
    T3 = np.concatenate([hi,hi,lo],1)
    TB = np.zeros((W, 128)); TB[:,:KS]=T
    TB = TB.T.astype(np.float32)
    Rb = R.astype(np.float32).astype(ml_dtypes.bfloat16)
    return Rb, np.ascontiguousarray(Rb.T), T3, TB

def dot(a,b):
    return jnp.dot(a,b,preferred_element_type=f32)


def quarters(s):
    return s[:HF, :HF], s[:HF, HF:], s[HF:, :HF], s[HF:, HF:]


def whole(cc, cs, sc, ss):
    return jnp.concatenate([jnp.concatenate([cc, cs], 1), jnp.concatenate([sc, ss], 1)], 0)


def step_kernel(unroll, first, sw, mask, target, taps, r, rt, t3, tb, rsum, got, loss,
        out, held0, held1, held2, held3, mid, recv0, recv1, grads, across, lines, back, pad, taph, spec, sfreq, acc, field, inten, level,
        s1s, s1r, s2s, s2r, xs, xr, gs, gr, bs, br, ls):
    held = (held0, held1, held2, held3)
    recv = (recv0, recv1)
    plane = lax.axis_index("clip")
    owner = lax.axis_index("owner")
    me = plane * 32 + owner
    chip = owner // 2
    core = owner % 2
    y = chip % 4
    z = chip // 4

    def at(route, a, b, c):
        return a * (8 - 6 * route) + b * (2 + 6 * route) + c

    def drain(ref, count, sem):
        part = ref.at[pl.ds(0, count)]
        pltpu.make_async_copy(part, part, sem).wait()

    def send(src, dst, send_sem, recv_sem, p, to):
        pltpu.make_async_remote_copy(src_ref=src, dst_ref=dst, send_sem=send_sem, recv_sem=recv_sem,
            device_id=(p, to), device_id_type=MESH).start()

    barrier = pltpu.get_barrier_semaphore()
    partners = [(plane, owner + 1 - 2 * core)]
    for j in (1, 2, 3):
        partners.append(((plane + j) % 4, owner))
        for c in range(2):
            partners.append((plane, at(0, (z + j) % 4, y, c)))
            partners.append((plane, at(0, z, (y + j) % 4, c)))
    for to in partners:
        pl.semaphore_signal(barrier, inc=1, device_id=to, device_id_type=MESH)

    a = z + core * (y - z)
    b = y + core * (z - y)

    def pick(k):
        b2 = (b + 1 + k) % 4

        def one(n, _):
            a2 = (a + n // 2) % 4
            c = n % 2
            dest = plane * 32 + at(core, a2, b2, c)
            near = first[2 * dest]
            far = first[2 * dest + 1]
            column = jnp.minimum(jnp.where(near >> 7 == chip, near, far) & 63, 62)
            slot = a2 * 8 + b2 * 2 + c
            out[slot, 0] = mask[column]
            out[slot, 1] = mask[column + 1]
            return 0

        lax.fori_loop(0, 8, one, 0)

    def first_stage(k):
        b2 = (b + 1 + k) % 4
        for j in (2, 1, 3):
            a2 = (a + j) % 4
            send(out.at[pl.ds(a2 * 8 + b2 * 2, 2)], held[k].at[pl.ds(a * 2, 2)], s1s, s1r.at[k],
                plane, at(core, a2, b, core))
        for c in range(2):
            held[k][a * 2 + c] = out[a * 8 + b2 * 2 + c]

    def second_stage(k):
        drain(held[k], 6, s1r.at[k])
        b2 = (b + 1 + k) % 4
        for i in range(2):
            for c in range(2):
                dest = plane * 32 + at(core, a, b2, c)
                pair = first[2 * dest + i] >> 7
                from_z = pair >> 2
                from_a = from_z + core * ((pair & 3) - from_z)
                mid[b2 * 4 + c * 2 + i] = held[k][from_a * 2 + c]
            if k < 3:
                for c in range(2):
                    send(mid.at[b2 * 4 + c * 2 + i], recv[i].at[core * 4 + b], s2s, s2r.at[i],
                        plane, at(core, a, b2, c))
            else:
                send(mid.at[b2 * 4 + (1 - core) * 2 + i], recv[i].at[core * 4 + b], s2s, s2r.at[i],
                    plane, owner + 1 - 2 * core)
                recv[i][core * 4 + b] = mid[b2 * 4 + core * 2 + i]

    pick(0)
    pl.semaphore_wait(barrier, len(partners))
    first_stage(0)
    for k in (1, 2, 3):
        pick(k)
        first_stage(k)

    pad[...] = jnp.zeros(pad.shape, f32)
    for c in range(CH):
        pad[c, :KS, :KS] = taps[c] * jnp.sqrt(sw[c % NK] * (1.0 / NK))
    level[...] = jnp.broadcast_to(
        jnp.sum(jnp.sum(pad[...], axis=1, keepdims=True), axis=2, keepdims=True) * 0.5, level.shape)
    m = jnp.dot(pad[...].reshape(CH * 16, 128), tb[...], precision=lax.Precision.HIGHEST,
        preferred_element_type=f32).reshape(CH, 16, W)
    high = m.astype(bf16)
    taph[:, 0:16, :] = high
    taph[:, 16:32, :] = (m - high.astype(f32)).astype(bf16)
    taph[:, 32:48, :] = high

    def spectrum(c, _):
        cc, cs, sc, ss = quarters(dot(t3[...], taph[c]))
        spec[c, 0] = cc - ss
        spec[c, 1] = sc + cs
        spec[c, 2] = cc + ss
        spec[c, 3] = sc - cs
        return 0

    for k in range(4):
        second_stage(k)
        if k < 3:
            lax.fori_loop(8 * k, 8 * k + 8, spectrum, 0, unroll=8)

    def transform(i):
        pair = first[2 * me + i] >> 7
        top = recv[i][pair & 3]
        low = recv[i][4 + (pair >> 2)]
        x = whole(top[0], top[1], low[0], low[1])
        t = (dot(r[...], x) - rsum[...]).astype(bf16)
        cc, cs, sc, ss = quarters(dot(t, rt[...]) * (0.5 / (HF * HF)))
        sfreq[0] = cc - ss
        sfreq[1] = sc + cs
        sfreq[2] = cc + ss
        sfreq[3] = sc - cs

    def back_to_pixels(aa, bb, a2, b2):
        u = dot(whole(aa + a2, bb - b2, bb + b2, a2 - aa).astype(bf16), r[...]).astype(bf16)
        return dot(rt[...], u)

    def forward():
        inten[...] = jnp.zeros((W, W), f32)

        def channel(c, _):
            p, q, p2, q2 = (sfreq[j] for j in range(4))
            m, n, m2, n2 = (spec[c, j] for j in range(4))
            e = back_to_pixels(p * m - q * n, p * n + q * m, p2 * m2 - q2 * n2, p2 * n2 + q2 * m2) + level[c]
            field[c] = e
            inten[...] = inten[...] + e * e
            return 0

        lax.fori_loop(0, CH, channel, 0, unroll=unroll)

    def resist(i):
        row = lax.broadcasted_iota(jnp.int32, (W, W), 0)
        col = lax.broadcasted_iota(jnp.int32, (W, W), 1)
        inside = (row >= AM) & (row < W - AM) & (col >= AM) & (col < W - AM)
        level_at = 1.0 / (1.0 + jnp.exp(-10.0 * (inten[...] - 0.3)))
        miss = jnp.where(inside, level_at - target[i].astype(f32), 0.0)
        loss[i] = jnp.sum(miss * miss) * (1.0 / ((W - 2 * AM) ** 2))
        inten[...] = 40.0 * miss * level_at * (1.0 - level_at)

    def backward():
        acc[...] = jnp.zeros(acc.shape, f32)

        def channel(c, _):
            g = (inten[...] * field[c]).astype(bf16)
            v = dot(g, rt[...]).astype(bf16)
            cc, cs, sc, ss = quarters(dot(r[...], v))
            p, q, p2, q2 = cc - ss, sc + cs, cc + ss, sc - cs
            m, n, m2, n2 = (spec[c, j] for j in range(4))
            acc[0] += p * m + q * n
            acc[1] += q * m - p * n
            acc[2] += p2 * m2 + q2 * n2
            acc[3] += q2 * m2 - p2 * n2
            return 0

        lax.fori_loop(0, CH, channel, 0, unroll=unroll)

    def finish(i):
        d = back_to_pixels(*(acc[j] * (0.5 / (HF * HF)) for j in range(4))).astype(bf16)
        for q in range(4):
            for part in range(2):
                for slot in range(2):
                    row = part * TS + q * 32
                    grads[i * 8 + q * 2 + part, slot] = d[row : row + 32, slot * TS : slot * TS + TS]

    def to_planes(i):
        for j in (1, 2, 3):
            p = (plane + j) % 4
            for part in range(2):
                send(grads.at[i * 8 + p * 2 + part], across.at[i * 8 + part * 4 + plane], xs, xr.at[i], p, owner)
        for part in range(2):
            across[i * 8 + part * 4 + plane] = grads[i * 8 + plane * 2 + part]

    def to_line(i):
        drain(across, 6, xr.at[i])
        for j in (2, 1, 3):
            for part in range(2):
                pa, pb = (z, y) if part == 0 else (y, z)
                here = across.at[pl.ds(i * 8 + part * 4, 4)]
                send(here, lines.at[pl.ds(part * 32 + pa * 8 + i * 4, 4)], gs, gr.at[i],
                    plane, at(part, (pa + j) % 4, pb, core))
        for part in range(2):
            pa = z if part == 0 else y
            lines[pl.ds(part * 32 + pa * 8 + i * 4, 4)] = across[pl.ds(i * 8 + part * 4, 4)]

    def to_owners(j, part):
        pa, pb = (z, y) if part == 0 else (y, z)
        b2 = (pb + j) % 4
        goal = pa * 4 + b2 if part == 0 else b2 * 4 + pa

        def one(n, _):
            a_src = n // 4
            x_src = n % 4
            source = x_src * 32 + at(part, a_src, pb, core)
            which = jnp.where(first[2 * source + 1] >> 7 == goal, 1, 0)
            back[part * 64 + b2 * 16 + n] = lines[part * 32 + a_src * 8 + which * 4 + x_src]
            return 0

        lax.fori_loop(0, 16, one, 0, unroll=2)
        src = back.at[pl.ds(part * 64 + b2 * 16, 16)]
        dst = got.at[pl.ds((pb * 2 + core) * 16, 16)]
        if j:
            send(src, dst, bs, br, plane, at(part, pa, b2, part))
        else:

            @pl.when(core == part)
            def _():
                pltpu.make_async_copy(src, dst, ls).start()

            @pl.when(core != part)
            def _():
                send(src, dst, bs, br, plane, owner + 1 - 2 * core)

    drain(recv[0], 7, s2r.at[0])
    transform(0)
    forward()
    resist(0)
    backward()
    finish(0)
    to_planes(0)
    drain(recv[1], 7, s2r.at[1])
    transform(1)
    forward()
    to_line(0)
    resist(1)
    backward()
    finish(1)
    to_planes(1)
    to_line(1)
    drain(lines, 24, gr.at[0])
    drain(lines, 24, gr.at[1])
    for j in (2, 1, 3, 0):
        for part in range(2):
            to_owners(j, part)
    drain(out, 24, s1s)
    drain(mid, 14, s2s)
    drain(grads, 12, xs)
    drain(lines, 48, gs)
    drain(back, 112, bs)
    drain(got, 16, ls)
    drain(got, 112, br)


def sum_kernel(first, losses, got, out, loss, total):
    owner = lax.axis_index("owner")
    chip = owner // 2
    core = owner % 2
    total[...] = jnp.zeros(total.shape, f32)

    def step(s, _):
        source = (s & 3) * 32 + ((s >> 2) & 3) * (8 - 6 * core) + (s >> 5) * (2 + 6 * core) + ((s >> 4) & 1)
        near = first[2 * source]
        far = first[2 * source + 1]
        mine = jnp.where(near >> 7 == chip, near, far)
        column = jnp.where(mine >> 7 == chip, jnp.minimum(mine & 63, 62), 64)
        at = pl.ds(pl.multiple_of(column * 32, 32), 64)
        total[at, :] += got[s].reshape(64, TS).astype(f32)
        return 0

    lax.fori_loop(0, 128, step, 0, unroll=4)
    for t in range(8):
        for j in range(32):
            out[8 * t : 8 * t + 8, 128 * j : 128 * j + 128] = total[pl.ds(256 * t + j, 8, stride=32), :]
    for i in range(2):
        loss[i] = losses[i]


def body(mask_tiles, correlation, target, socs_kernels, socs_weights):
    first = correlation[:, 0]
    Rb, RTb, T3, TB = tables()
    rsum = np.broadcast_to(0.5 * Rb.astype(np.float32).sum(1, keepdims=True), (W, W)).copy()
    V = pl.BlockSpec(memory_space=pltpu.VMEM)
    S = pl.BlockSpec(memory_space=pltpu.SMEM)
    A = pl.BlockSpec(memory_space=pl.ANY)
    D = pltpu.SemaphoreType.DMA
    got, losses = pl.pallas_call(
        functools.partial(step_kernel, 8),
        out_shape=(jax.ShapeDtypeStruct((128, 2, 32, TS), bf16), jax.ShapeDtypeStruct((2,), f32)),
        in_specs=[S, S] + [V] * 8,
        out_specs=(A, S),
        scratch_shapes=[
            pltpu.VMEM((32, 2, TS, TS), bf16),
            *[pltpu.VMEM((8, 2, TS, TS), bf16)] * 4,
            pltpu.VMEM((16, 2, TS, TS), bf16),
            *[pltpu.VMEM((8, 2, TS, TS), bf16)] * 2,
            pltpu.VMEM((16, 2, 32, TS), bf16),
            pltpu.VMEM((16, 2, 32, TS), bf16),
            pltpu.VMEM((64, 2, 32, TS), bf16),
            pltpu.VMEM((128, 2, 32, TS), bf16),
            pltpu.VMEM((CH, 16, 128), f32),
            pltpu.VMEM((CH, 48, W), bf16),
            pltpu.VMEM((CH, 4, HF, HF), f32),
            pltpu.VMEM((4, HF, HF), f32),
            pltpu.VMEM((4, HF, HF), f32),
            pltpu.VMEM((CH, W, W), f32),
            pltpu.VMEM((W, W), f32),
            pltpu.VMEM((CH, 1, W), f32),
            D, D((4,)), D, D((2,)), D, D((2,)), D, D((2,)), D, D, D,
        ],
        compiler_params=pltpu.CompilerParams(vmem_limit_bytes=56 * 2**20, collective_id=0, has_side_effects=True),
    )(first, socs_weights, mask_tiles.reshape(64, TS, TS), target.reshape(2, W, W), socs_kernels.reshape(CH, KS, KS),
        jnp.asarray(Rb), jnp.asarray(RTb), jnp.asarray(T3), jnp.asarray(TB), jnp.asarray(rsum))
    return pl.pallas_call(sum_kernel,
        out_shape=(jax.ShapeDtypeStruct((64, 4096), f32), jax.ShapeDtypeStruct((2,), f32)),
        in_specs=[S, S, V], out_specs=(V, S), scratch_shapes=[pltpu.VMEM((66 * 32, TS), f32)],
    )(first, losses, got)


def solution(mesh):
    placed = (P("owner", None), P(), P(("clip", "owner"), None), P(), P())
    return jax.shard_map(body, mesh=mesh, in_specs=placed,
        out_specs=(P("owner", "clip"), P(("clip", "owner"))), check_vma=False)
```

```python
import functools

import jax
import jax.numpy as jnp
import ml_dtypes
import numpy as np
from jax import lax
from jax.experimental import pallas as pl
from jax.experimental.pallas import tpu as pltpu
from jax.sharding import PartitionSpec as P

TS=128; W=256; HF=128; KS=15; AM=7; NK=12; CH=24
MESH = pl.DeviceIdType.MESH
f32=jnp.float32; bf16=jnp.bfloat16

def tables():
    u = np.arange(HF) + 0.5
    y = np.arange(W)
    ang = 2*np.pi*u[:,None]*y[None,:]/W
    R = np.concatenate([np.cos(ang), np.sin(ang)], 0)
    b = np.arange(KS)-AM
    ang2 = 2*np.pi*u[:,None]*b[None,:]/W
    T = np.concatenate([np.cos(ang2), np.sin(ang2)], 0)
    T16 = np.zeros((W,16)); T16[:,:KS]=T
    hi = T16.astype(np.float32).astype(ml_dtypes.bfloat16)
    lo = (T16-hi.astype(np.float64)).astype(np.float32).astype(ml_dtypes.bfloat16)
    T3 = np.concatenate([hi,hi,lo],1)
    TB = np.zeros((W, 128)); TB[:,:KS]=T
    TB = TB.T.astype(np.float32)
    Rb = R.astype(np.float32).astype(ml_dtypes.bfloat16)
    return Rb, np.ascontiguousarray(Rb.T), T3, TB

def dot(a,b):
    return jnp.dot(a,b,preferred_element_type=f32)


def quarters(s):
    return s[:HF, :HF], s[:HF, HF:], s[HF:, :HF], s[HF:, HF:]


def whole(cc, cs, sc, ss):
    return jnp.concatenate([jnp.concatenate([cc, cs], 1), jnp.concatenate([sc, ss], 1)], 0)


def step_kernel(unroll, first, sw, mask_in, target_in, taps_in, r_in, rt_in, t3_in, tb_in, got, loss,
        raw, mask, wide, target, taps, r, rt, t3, tb, rsum, out, held0, held1, held2, held3, mid, recv0, recv1, grads, across, lines, back, pad, taph, spec, sfreq, acc, field, inten, level,
        ins, s1s, s1r, s2s, s2r, xs, xr, gs, gr, bs, br, ls):
    held = (held0, held1, held2, held3)
    recv = (recv0, recv1)
    plane = lax.axis_index("clip")
    owner = lax.axis_index("owner")
    me = plane * 32 + owner
    chip = owner // 2
    core = owner % 2
    y = chip % 4
    z = chip // 4

    def at(route, a, b, c):
        return a * (8 - 6 * route) + b * (2 + 6 * route) + c

    def drain(ref, count, sem):
        part = ref.at[pl.ds(0, count)]
        pltpu.make_async_copy(part, part, sem).wait()

    def send(src, dst, send_sem, recv_sem, p, to):
        pltpu.make_async_remote_copy(src_ref=src, dst_ref=dst, send_sem=send_sem, recv_sem=recv_sem,
            device_id=(p, to), device_id_type=MESH).start()

    barrier = pltpu.get_barrier_semaphore()
    partners = [(plane, owner + 1 - 2 * core)]
    for j in (1, 2, 3):
        partners.append(((plane + j) % 4, owner))
        for c in range(2):
            partners.append((plane, at(0, (z + j) % 4, y, c)))
            partners.append((plane, at(0, z, (y + j) % 4, c)))
    for to in partners:
        pl.semaphore_signal(barrier, inc=1, device_id=to, device_id_type=MESH)

    loads = [pltpu.make_async_copy(mask_in.at[pl.ds(16 * n, 16)], raw.at[pl.ds(16 * n, 16)], ins.at[n]) for n in range(4)]
    loads += [
        pltpu.make_async_copy(src, dst, ins.at[4 + n])
        for n, (src, dst) in enumerate(((taps_in, taps), (tb_in, tb), (t3_in, t3), (target_in, wide), (r_in, r), (rt_in, rt)))
    ]
    for load in loads:
        load.start()

    a = z + core * (y - z)
    b = y + core * (z - y)

    def pick(k):
        b2 = (b + 1 + k) % 4

        def one(n, _):
            a2 = (a + n // 2) % 4
            c = n % 2
            dest = plane * 32 + at(core, a2, b2, c)
            near = first[0, 2 * dest]
            far = first[0, 2 * dest + 1]
            column = jnp.minimum(jnp.where(near >> 7 == chip, near, far) & 63, 62)
            slot = a2 * 8 + b2 * 2 + c
            for n2 in range(2):
                out[slot, n2] = mask[column + n2].astype(bf16)
            return 0

        lax.fori_loop(0, 8, one, 0)

    def first_stage(k):
        b2 = (b + 1 + k) % 4
        for j in (2, 1, 3):
            a2 = (a + j) % 4
            send(out.at[pl.ds(a2 * 8 + b2 * 2, 2)], held[k].at[pl.ds(a * 2, 2)], s1s, s1r.at[k],
                plane, at(core, a2, b, core))
        for c in range(2):
            held[k][a * 2 + c] = out[a * 8 + b2 * 2 + c]

    def second_stage(k, i):
        if i == 0:
            drain(held[k], 6, s1r.at[k])
        b2 = (b + 1 + k) % 4
        if True:
            for c in range(2):
                dest = plane * 32 + at(core, a, b2, c)
                pair = first[0, 2 * dest + i] >> 7
                from_z = pair >> 2
                from_a = from_z + core * ((pair & 3) - from_z)
                mid[b2 * 4 + c * 2 + i] = held[k][from_a * 2 + c]
            if k < 3:
                for c in range(2):
                    send(mid.at[b2 * 4 + c * 2 + i], recv[i].at[core * 4 + b], s2s, s2r.at[i],
                        plane, at(core, a, b2, c))
            else:
                send(mid.at[b2 * 4 + (1 - core) * 2 + i], recv[i].at[core * 4 + b], s2s, s2r.at[i],
                    plane, owner + 1 - 2 * core)
                recv[i][core * 4 + b] = mid[b2 * 4 + core * 2 + i]

    flat = mask.reshape(64 * TS, TS)
    for n in range(4):
        loads[n].wait()

        def rows(j, _):
            v = raw[16 * n : 16 * n + 16, pl.ds(pl.multiple_of(j * TS, TS), TS)].astype(f32)
            flat[pl.ds(16 * n * TS + j, 8, stride=TS), :] = v[:8]
            flat[pl.ds((16 * n + 8) * TS + j, 8, stride=TS), :] = v[8:]
            return 0

        lax.fori_loop(0, TS, rows, 0, unroll=8)

    pick(0)
    pl.semaphore_wait(barrier, len(partners))
    first_stage(0)
    for k in (1, 2, 3):
        pick(k)
        first_stage(k)

    for load in loads[4:7]:
        load.wait()
    pad[...] = jnp.zeros(pad.shape, f32)
    for c in range(CH):
        pad[c, :KS, :KS] = taps[c % NK, :, c // NK, :] * jnp.sqrt(sw[c % NK] * (1.0 / NK))
    level[...] = jnp.broadcast_to(
        jnp.sum(jnp.sum(pad[...], axis=1, keepdims=True), axis=2, keepdims=True) * 0.5, level.shape)
    m = jnp.dot(pad[...].reshape(CH * 16, 128), tb[...], precision=lax.Precision.HIGHEST,
        preferred_element_type=f32).reshape(CH, 16, W)
    high = m.astype(bf16)
    taph[:, 0:16, :] = high
    taph[:, 16:32, :] = (m - high.astype(f32)).astype(bf16)
    taph[:, 32:48, :] = high

    def spectrum(c, _):
        cc, cs, sc, ss = quarters(dot(t3[...], taph[c]))
        spec[c, 0] = cc - ss
        spec[c, 1] = sc + cs
        spec[c, 2] = cc + ss
        spec[c, 3] = sc - cs
        return 0

    for k in range(4):
        second_stage(k, 0)
        if k < 3:
            lax.fori_loop(8 * k, 8 * k + 8, spectrum, 0, unroll=8)

    for k in range(4):
        second_stage(k, 1)
    for load in loads[7:]:
        load.wait()

    def widen(n, _):
        target[pl.ds(n, 2, stride=2 * W), :] = wide[:, pl.ds(pl.multiple_of(n * TS, TS), TS)].astype(f32)
        return 0

    lax.fori_loop(0, 2 * W, widen, 0, unroll=8)
    rsum[...] = dot(r[...], jnp.full((W, W), 0.5, bf16))

    def transform(i):
        pair = first[0, 2 * me + i] >> 7
        top = recv[i][pair & 3]
        low = recv[i][4 + (pair >> 2)]
        x = whole(top[0], top[1], low[0], low[1])
        t = (dot(r[...], x) - rsum[...]).astype(bf16)
        cc, cs, sc, ss = quarters(dot(t, rt[...]) * (0.5 / (HF * HF)))
        sfreq[0] = cc - ss
        sfreq[1] = sc + cs
        sfreq[2] = cc + ss
        sfreq[3] = sc - cs

    def back_to_pixels(aa, bb, a2, b2):
        u = dot(whole(aa + a2, bb - b2, bb + b2, a2 - aa).astype(bf16), r[...]).astype(bf16)
        return dot(rt[...], u)

    def forward():
        inten[...] = jnp.zeros((W, W), f32)

        def channel(c, _):
            p, q, p2, q2 = (sfreq[j] for j in range(4))
            m, n, m2, n2 = (spec[c, j] for j in range(4))
            e = back_to_pixels(p * m - q * n, p * n + q * m, p2 * m2 - q2 * n2, p2 * n2 + q2 * m2) + level[c]
            field[c] = e
            inten[...] = inten[...] + e * e
            return 0

        lax.fori_loop(0, CH, channel, 0, unroll=unroll)

    def resist(i):
        row = lax.broadcasted_iota(jnp.int32, (W, W), 0)
        col = lax.broadcasted_iota(jnp.int32, (W, W), 1)
        inside = (row >= AM) & (row < W - AM) & (col >= AM) & (col < W - AM)
        level_at = 1.0 / (1.0 + jnp.exp(-10.0 * (inten[...] - 0.3)))
        goal = jnp.concatenate([target[pl.ds(i * 2 * W + n, W, stride=2), :] for n in range(2)], 1)
        miss = jnp.where(inside, level_at - goal, 0.0)
        loss[i] = jnp.sum(miss * miss) * (1.0 / ((W - 2 * AM) ** 2))
        inten[...] = 40.0 * miss * level_at * (1.0 - level_at)

    def backward():
        acc[...] = jnp.zeros(acc.shape, f32)

        def channel(c, _):
            g = (inten[...] * field[c]).astype(bf16)
            v = dot(g, rt[...]).astype(bf16)
            cc, cs, sc, ss = quarters(dot(r[...], v))
            p, q, p2, q2 = cc - ss, sc + cs, cc + ss, sc - cs
            m, n, m2, n2 = (spec[c, j] for j in range(4))
            acc[0] += p * m + q * n
            acc[1] += q * m - p * n
            acc[2] += p2 * m2 + q2 * n2
            acc[3] += q2 * m2 - p2 * n2
            return 0

        lax.fori_loop(0, CH, channel, 0, unroll=unroll)

    def finish(i):
        d = back_to_pixels(*(acc[j] * (0.5 / (HF * HF)) for j in range(4))).astype(bf16)
        for q in range(4):
            for part in range(2):
                for slot in range(2):
                    row = part * TS + q * 32
                    grads[i * 8 + q * 2 + part, slot] = d[row : row + 32, slot * TS : slot * TS + TS]

    def to_planes(i):
        for j in (1, 2, 3):
            p = (plane + j) % 4
            for part in range(2):
                send(grads.at[i * 8 + p * 2 + part], across.at[i * 8 + part * 4 + plane], xs, xr.at[i], p, owner)
        for part in range(2):
            across[i * 8 + part * 4 + plane] = grads[i * 8 + plane * 2 + part]

    def to_line(i):
        drain(across, 6, xr.at[i])
        for j in (2, 1, 3):
            for part in range(2):
                pa, pb = (z, y) if part == 0 else (y, z)
                here = across.at[pl.ds(i * 8 + part * 4, 4)]
                send(here, lines.at[pl.ds(part * 32 + pa * 8 + i * 4, 4)], gs, gr.at[i],
                    plane, at(part, (pa + j) % 4, pb, core))
        for part in range(2):
            pa = z if part == 0 else y
            lines[pl.ds(part * 32 + pa * 8 + i * 4, 4)] = across[pl.ds(i * 8 + part * 4, 4)]

    def to_owners(j, part):
        pa, pb = (z, y) if part == 0 else (y, z)
        b2 = (pb + j) % 4
        goal = pa * 4 + b2 if part == 0 else b2 * 4 + pa

        def one(n, _):
            a_src = n // 4
            x_src = n % 4
            source = x_src * 32 + at(part, a_src, pb, core)
            which = jnp.where(first[0, 2 * source + 1] >> 7 == goal, 1, 0)
            back[part * 64 + b2 * 16 + n] = lines[part * 32 + a_src * 8 + which * 4 + x_src]
            return 0

        lax.fori_loop(0, 16, one, 0, unroll=2)
        src = back.at[pl.ds(part * 64 + b2 * 16, 16)]
        dst = got.at[pl.ds((pb * 2 + core) * 16, 16)]
        if j:
            send(src, dst, bs, br, plane, at(part, pa, b2, part))
        else:

            @pl.when(core == part)
            def _():
                pltpu.make_async_copy(src, dst, ls).start()

            @pl.when(core != part)
            def _():
                send(src, dst, bs, br, plane, owner + 1 - 2 * core)

    drain(recv[0], 7, s2r.at[0])
    transform(0)
    forward()
    resist(0)
    backward()
    finish(0)
    to_planes(0)
    drain(recv[1], 7, s2r.at[1])
    transform(1)
    forward()
    to_line(0)
    resist(1)
    backward()
    finish(1)
    to_planes(1)
    to_line(1)
    drain(lines, 24, gr.at[0])
    drain(lines, 24, gr.at[1])
    for j in (2, 1, 3, 0):
        for part in range(2):
            to_owners(j, part)
    drain(out, 24, s1s)
    drain(mid, 14, s2s)
    drain(grads, 12, xs)
    drain(lines, 48, gs)
    drain(back, 112, bs)
    drain(got, 16, ls)
    drain(got, 112, br)


def sum_kernel(first, losses, got, out, loss, total):
    owner = lax.axis_index("owner")
    chip = owner // 2
    core = owner % 2
    total[...] = jnp.zeros(total.shape, f32)

    def step(s, _):
        source = (s & 3) * 32 + ((s >> 2) & 3) * (8 - 6 * core) + (s >> 5) * (2 + 6 * core) + ((s >> 4) & 1)
        near = first[0, 2 * source]
        far = first[0, 2 * source + 1]
        mine = jnp.where(near >> 7 == chip, near, far)
        column = jnp.where(mine >> 7 == chip, jnp.minimum(mine & 63, 62), 64)
        at = pl.ds(pl.multiple_of(column * 32, 32), 64)
        total[at, :] += got[s].reshape(64, TS).astype(f32)
        return 0

    lax.fori_loop(0, 128, step, 0, unroll=4)
    for t in range(8):
        for j in range(32):
            out[8 * t : 8 * t + 8, 128 * j : 128 * j + 128] = total[pl.ds(256 * t + j, 8, stride=32), :]
    for i in range(2):
        loss[i] = losses[i]


def body(mask_tiles, correlation, target, socs_kernels, socs_weights):
    first = correlation.T
    Rb, RTb, T3, TB = tables()
    V = pl.BlockSpec(memory_space=pltpu.VMEM)
    S = pl.BlockSpec(memory_space=pltpu.SMEM)
    A = pl.BlockSpec(memory_space=pl.ANY)
    D = pltpu.SemaphoreType.DMA
    got, losses = pl.pallas_call(
        functools.partial(step_kernel, 8),
        out_shape=(jax.ShapeDtypeStruct((128, 2, 32, TS), bf16), jax.ShapeDtypeStruct((2,), f32)),
        in_specs=[S, S] + [A] * 7,
        out_specs=(A, S),
        scratch_shapes=[
            pltpu.VMEM((64, TS * TS), bf16),
            pltpu.VMEM((64, TS, TS), f32),
            pltpu.VMEM((2, W * W), bf16),
            pltpu.VMEM((4 * W, TS), f32),
            pltpu.VMEM((NK, KS, 2, KS), f32),
            pltpu.VMEM((W, W), bf16),
            pltpu.VMEM((W, W), bf16),
            pltpu.VMEM((W, 48), bf16),
            pltpu.VMEM((128, W), f32),
            pltpu.VMEM((W, W), f32),
            pltpu.VMEM((32, 2, TS, TS), bf16),
            *[pltpu.VMEM((8, 2, TS, TS), bf16)] * 4,
            pltpu.VMEM((16, 2, TS, TS), bf16),
            *[pltpu.VMEM((8, 2, TS, TS), bf16)] * 2,
            pltpu.VMEM((16, 2, 32, TS), bf16),
            pltpu.VMEM((16, 2, 32, TS), bf16),
            pltpu.VMEM((64, 2, 32, TS), bf16),
            pltpu.VMEM((128, 2, 32, TS), bf16),
            pltpu.VMEM((CH, 16, 128), f32),
            pltpu.VMEM((CH, 48, W), bf16),
            pltpu.VMEM((CH, 4, HF, HF), f32),
            pltpu.VMEM((4, HF, HF), f32),
            pltpu.VMEM((4, HF, HF), f32),
            pltpu.VMEM((CH, W, W), f32),
            pltpu.VMEM((W, W), f32),
            pltpu.VMEM((CH, 1, W), f32),
            D((10,)), D, D((4,)), D, D((2,)), D, D((2,)), D, D((2,)), D, D, D,
        ],
        compiler_params=pltpu.CompilerParams(vmem_limit_bytes=56 * 2**20, collective_id=0, has_side_effects=True),
    )(first, socs_weights, mask_tiles, target, socs_kernels.transpose(1, 2, 0, 3),
        jnp.asarray(Rb), jnp.asarray(RTb), jnp.asarray(T3), jnp.asarray(TB))
    return pl.pallas_call(sum_kernel,
        out_shape=(jax.ShapeDtypeStruct((64, 4096), f32), jax.ShapeDtypeStruct((2,), f32)),
        in_specs=[S, S, V], out_specs=(V, S), scratch_shapes=[pltpu.VMEM((66 * 32, TS), f32)],
    )(first, losses, got)


def solution(mesh):
    placed = (P("owner", None), P(), P(("clip", "owner"), None), P(), P())
    return jax.shard_map(body, mesh=mesh, in_specs=placed,
        out_specs=(P("owner", "clip"), P(("clip", "owner"))), check_vma=False)
```

```python
import functools

import jax
import jax.numpy as jnp
import ml_dtypes
import numpy as np
from jax import lax
from jax.experimental import pallas as pl
from jax.experimental.pallas import tpu as pltpu
from jax.sharding import PartitionSpec as P

TS=128; W=256; HF=128; KS=15; AM=7; NK=12; CH=24
PITCH = 136
MESH = pl.DeviceIdType.MESH
f32=jnp.float32; bf16=jnp.bfloat16

def tables():
    u = np.arange(HF) + 0.5
    y = np.arange(W)
    ang = 2*np.pi*u[:,None]*y[None,:]/W
    R = np.concatenate([np.cos(ang), np.sin(ang)], 0)
    b = np.arange(KS)-AM
    ang2 = 2*np.pi*u[:,None]*b[None,:]/W
    T = np.concatenate([np.cos(ang2), np.sin(ang2)], 0)
    T16 = np.zeros((W,16)); T16[:,:KS]=T
    hi = T16.astype(np.float32).astype(ml_dtypes.bfloat16)
    lo = (T16-hi.astype(np.float64)).astype(np.float32).astype(ml_dtypes.bfloat16)
    T3 = np.concatenate([hi,hi,lo],1)
    TB = np.zeros((W, 128)); TB[:,:KS]=T
    TB = TB.T.astype(np.float32)
    Rb = R.astype(np.float32).astype(ml_dtypes.bfloat16)
    return Rb, np.ascontiguousarray(Rb.T), T3, TB

def dot(a,b):
    return jnp.dot(a,b,preferred_element_type=f32)


def quarters(s):
    return s[:HF, :HF], s[:HF, HF:], s[HF:, :HF], s[HF:, HF:]


def whole(cc, cs, sc, ss):
    return jnp.concatenate([jnp.concatenate([cc, cs], 1), jnp.concatenate([sc, ss], 1)], 0)


def step_kernel(unroll, first, sw, mask_in, target_in, taps_in, r_in, rt_in, t3_in, tb_in, got, loss,
        raw, mask, wide, target, taps, r, rt, t3, tb, rsum, out, held0, held1, held2, held3, mid, recv0, recv1, grads, across, lines, back, pad, taph, spec, sfreq, acc, field, inten, level, flow, amp,
        ins, s1s, s1r, s2s, s2r, xs, xr, gs, gr, bs, br, ls):
    held = (held0, held1, held2, held3)
    recv = (recv0, recv1)
    plane = lax.axis_index("clip")
    owner = lax.axis_index("owner")
    me = plane * 32 + owner
    chip = owner // 2
    core = owner % 2
    y = chip % 4
    z = chip // 4

    def at(route, a, b, c):
        return a * (8 - 6 * route) + b * (2 + 6 * route) + c

    def drain(ref, count, sem):
        part = ref.at[pl.ds(0, count)]
        pltpu.make_async_copy(part, part, sem).wait()

    def send(src, dst, send_sem, recv_sem, p, to):
        pltpu.make_async_remote_copy(src_ref=src, dst_ref=dst, send_sem=send_sem, recv_sem=recv_sem,
            device_id=(p, to), device_id_type=MESH).start()

    barrier = pltpu.get_barrier_semaphore()
    partners = [(plane, owner + 1 - 2 * core)]
    for j in (1, 2, 3):
        partners.append(((plane + j) % 4, owner))
        for c in range(2):
            partners.append((plane, at(0, (z + j) % 4, y, c)))
            partners.append((plane, at(0, z, (y + j) % 4, c)))
    for to in partners:
        pl.semaphore_signal(barrier, inc=1, device_id=to, device_id_type=MESH)

    loads = [pltpu.make_async_copy(mask_in.at[pl.ds(16 * n, 16)], raw.at[pl.ds(16 * n, 16)], ins.at[n]) for n in range(4)]
    loads += [
        pltpu.make_async_copy(src, dst, ins.at[4 + n])
        for n, (src, dst) in enumerate(((taps_in, taps), (tb_in, tb), (t3_in, t3), (target_in, wide), (r_in, r), (rt_in, rt)))
    ]
    for load in loads:
        load.start()

    a = z + core * (y - z)
    b = y + core * (z - y)

    def pick(k):
        b2 = (b + 1 + k) % 4

        def one(n, _):
            a2 = (a + n // 2) % 4
            c = n % 2
            dest = plane * 32 + at(core, a2, b2, c)
            near = first[0, 2 * dest]
            far = first[0, 2 * dest + 1]
            column = jnp.minimum(jnp.where(near >> 7 == chip, near, far) & 63, 62)
            slot = a2 * 8 + b2 * 2 + c
            for n2 in range(2):
                out[slot, n2] = mask[column + n2, :TS].astype(bf16)
            return 0

        lax.fori_loop(0, 8, one, 0)

    def first_stage(k):
        b2 = (b + 1 + k) % 4
        for j in (2, 1, 3):
            a2 = (a + j) % 4
            send(out.at[pl.ds(a2 * 8 + b2 * 2, 2)], held[k].at[pl.ds(a * 2, 2)], s1s, s1r.at[k],
                plane, at(core, a2, b, core))
        for c in range(2):
            held[k][a * 2 + c] = out[a * 8 + b2 * 2 + c]

    def second_stage(k, i):
        if i == 0:
            drain(held[k], 6, s1r.at[k])
        b2 = (b + 1 + k) % 4
        if True:
            for c in range(2):
                dest = plane * 32 + at(core, a, b2, c)
                pair = first[0, 2 * dest + i] >> 7
                from_z = pair >> 2
                from_a = from_z + core * ((pair & 3) - from_z)
                mid[b2 * 4 + c * 2 + i] = held[k][from_a * 2 + c]
            if k < 3:
                for c in range(2):
                    send(mid.at[b2 * 4 + c * 2 + i], recv[i].at[core * 4 + b], s2s, s2r.at[i],
                        plane, at(core, a, b2, c))
            else:
                send(mid.at[b2 * 4 + (1 - core) * 2 + i], recv[i].at[core * 4 + b], s2s, s2r.at[i],
                    plane, owner + 1 - 2 * core)
                recv[i][core * 4 + b] = mid[b2 * 4 + core * 2 + i]

    flat = mask.reshape(64 * PITCH, TS)
    for n in range(4):
        loads[n].wait()

        def rows(j, _):
            v = raw[16 * n : 16 * n + 16, pl.ds(pl.multiple_of(j * TS, TS), TS)].astype(f32)
            flat[pl.ds(16 * n * PITCH + j, 8, stride=PITCH), :] = v[:8]
            flat[pl.ds((16 * n + 8) * PITCH + j, 8, stride=PITCH), :] = v[8:]
            return 0

        lax.fori_loop(0, TS, rows, 0, unroll=8)

    pick(0)
    pl.semaphore_wait(barrier, len(partners))
    first_stage(0)
    for k in (1, 2, 3):
        pick(k)
        first_stage(k)

    for load in loads[4:7]:
        load.wait()
    pad[...] = jnp.zeros(pad.shape, f32)
    for c in range(CH):
        pad[c, :KS, :KS] = taps[c % NK, :, c // NK, :]
        amp[c] = jnp.full((1, W), jnp.sqrt(sw[c % NK] * (1.0 / NK)))
    flow[...] = jnp.broadcast_to(
        jnp.sum(jnp.sum(pad[...], axis=1, keepdims=True), axis=2, keepdims=True), flow.shape)
    m = jnp.dot((pad[...] * amp[:, :, :128]).reshape(CH * 16, 128), tb[...], precision=lax.Precision.HIGHEST,
        preferred_element_type=f32).reshape(CH, 16, W)
    high = m.astype(bf16)
    taph[:, 0:16, :] = high
    taph[:, 16:32, :] = (m - high.astype(f32)).astype(bf16)
    taph[:, 32:48, :] = high

    def spectrum(c, _):
        cc, cs, sc, ss = quarters(dot(t3[...], taph[c]))
        spec[c, 0] = cc - ss
        spec[c, 1] = sc + cs
        spec[c, 2] = cc + ss
        spec[c, 3] = sc - cs
        return 0

    for k in range(4):
        second_stage(k, 0)
        if k < 3:
            lax.fori_loop(8 * k, 8 * k + 8, spectrum, 0, unroll=8)

    for k in range(4):
        second_stage(k, 1)
    for load in loads[7:]:
        load.wait()

    def widen(n, _):
        target[pl.ds(n, 2, stride=2 * W), :] = wide[:, pl.ds(pl.multiple_of(n * TS, TS), TS)].astype(f32)
        return 0

    lax.fori_loop(0, 2 * W, widen, 0, unroll=8)
    rsum[...] = dot(r[...], jnp.full((W, W), 1.0, bf16))

    def transform(i):
        pair = first[0, 2 * me + i] >> 7
        top = recv[i][pair & 3]
        low = recv[i][4 + (pair >> 2)]
        x = whole(top[0], top[1], low[0], low[1])
        sums = jnp.sum(x.astype(f32), axis=0, keepdims=True)
        rounded = sums.astype(bf16).astype(f32)
        t = (dot(r[...], x) - rsum[...] * (0.5 - (rounded - sums) * (1.0 / W))).astype(bf16)
        zero = flow[...] * jnp.sum(rounded)
        level[...] = amp[...] * (0.5 * flow[...] + (zero.astype(bf16).astype(f32) - zero) * (1.0 / (W * W)))
        cc, cs, sc, ss = quarters(dot(t, rt[...]) * (0.5 / (HF * HF)))
        sfreq[0] = cc - ss
        sfreq[1] = sc + cs
        sfreq[2] = cc + ss
        sfreq[3] = sc - cs

    def back_to_pixels(aa, bb, a2, b2):
        u = dot(whole(aa + a2, bb - b2, bb + b2, a2 - aa).astype(bf16), r[...]).astype(bf16)
        return dot(rt[...], u)

    def forward():
        inten[...] = jnp.zeros((W, W), f32)

        def channel(c, _):
            p, q, p2, q2 = (sfreq[j] for j in range(4))
            m, n, m2, n2 = (spec[c, j] for j in range(4))
            e = back_to_pixels(p * m - q * n, p * n + q * m, p2 * m2 - q2 * n2, p2 * n2 + q2 * m2) + level[c]
            field[c] = e
            inten[...] = inten[...] + e * e
            return 0

        lax.fori_loop(0, CH, channel, 0, unroll=unroll)

    def resist(i):
        row = lax.broadcasted_iota(jnp.int32, (W, W), 0)
        col = lax.broadcasted_iota(jnp.int32, (W, W), 1)
        inside = (row >= AM) & (row < W - AM) & (col >= AM) & (col < W - AM)
        level_at = 1.0 / (1.0 + jnp.exp(-10.0 * (inten[...] - 0.3)))
        goal = jnp.concatenate([target[pl.ds(i * 2 * W + n, W, stride=2), :] for n in range(2)], 1)
        miss = jnp.where(inside, level_at - goal, 0.0)
        loss[i] = jnp.sum(miss * miss) * (1.0 / ((W - 2 * AM) ** 2))
        inten[...] = 40.0 * miss * level_at * (1.0 - level_at)

    def backward():
        acc[...] = jnp.zeros(acc.shape, f32)

        def channel(c, _):
            g = (inten[...] * field[c]).astype(bf16)
            v = dot(g, rt[...]).astype(bf16)
            cc, cs, sc, ss = quarters(dot(r[...], v))
            p, q, p2, q2 = cc - ss, sc + cs, cc + ss, sc - cs
            m, n, m2, n2 = (spec[c, j] for j in range(4))
            acc[0] += p * m + q * n
            acc[1] += q * m - p * n
            acc[2] += p2 * m2 + q2 * n2
            acc[3] += q2 * m2 - p2 * n2
            return 0

        lax.fori_loop(0, CH, channel, 0, unroll=unroll)

    def finish(i):
        d = back_to_pixels(*(acc[j] * (0.5 / (HF * HF)) for j in range(4))).astype(bf16)
        for q in range(4):
            for part in range(2):
                for slot in range(2):
                    row = part * TS + q * 32
                    grads[i * 8 + q * 2 + part, slot] = d[row : row + 32, slot * TS : slot * TS + TS]

    def to_planes(i):
        for j in (1, 2, 3):
            p = (plane + j) % 4
            for part in range(2):
                send(grads.at[i * 8 + p * 2 + part], across.at[i * 8 + part * 4 + plane], xs, xr.at[i], p, owner)
        for part in range(2):
            across[i * 8 + part * 4 + plane] = grads[i * 8 + plane * 2 + part]

    def to_line(i):
        drain(across, 6, xr.at[i])
        for j in (2, 1, 3):
            for part in range(2):
                pa, pb = (z, y) if part == 0 else (y, z)
                here = across.at[pl.ds(i * 8 + part * 4, 4)]
                send(here, lines.at[pl.ds(part * 32 + pa * 8 + i * 4, 4)], gs, gr.at[i],
                    plane, at(part, (pa + j) % 4, pb, core))
        for part in range(2):
            pa = z if part == 0 else y
            lines[pl.ds(part * 32 + pa * 8 + i * 4, 4)] = across[pl.ds(i * 8 + part * 4, 4)]

    def to_owners(j, part):
        pa, pb = (z, y) if part == 0 else (y, z)
        b2 = (pb + j) % 4
        goal = pa * 4 + b2 if part == 0 else b2 * 4 + pa

        def one(n, _):
            a_src = n // 4
            x_src = n % 4
            source = x_src * 32 + at(part, a_src, pb, core)
            which = jnp.where(first[0, 2 * source + 1] >> 7 == goal, 1, 0)
            back[part * 64 + b2 * 16 + n] = lines[part * 32 + a_src * 8 + which * 4 + x_src]
            return 0

        lax.fori_loop(0, 16, one, 0, unroll=2)
        src = back.at[pl.ds(part * 64 + b2 * 16, 16)]
        dst = got.at[pl.ds((pb * 2 + core) * 16, 16)]
        if j:
            send(src, dst, bs, br, plane, at(part, pa, b2, part))
        else:

            @pl.when(core == part)
            def _():
                pltpu.make_async_copy(src, dst, ls).start()

            @pl.when(core != part)
            def _():
                send(src, dst, bs, br, plane, owner + 1 - 2 * core)

    drain(recv[0], 7, s2r.at[0])
    transform(0)
    forward()
    resist(0)
    backward()
    finish(0)
    to_planes(0)
    drain(recv[1], 7, s2r.at[1])
    transform(1)
    forward()
    to_line(0)
    resist(1)
    backward()
    finish(1)
    to_planes(1)
    to_line(1)
    drain(lines, 24, gr.at[0])
    drain(lines, 24, gr.at[1])
    for j in (2, 1, 3, 0):
        for part in range(2):
            to_owners(j, part)
    drain(out, 24, s1s)
    drain(mid, 14, s2s)
    drain(grads, 12, xs)
    drain(lines, 48, gs)
    drain(back, 112, bs)
    drain(got, 16, ls)
    drain(got, 112, br)


def sum_kernel(first, losses, got, out, loss, held, total, rows, ins, outs):
    owner = lax.axis_index("owner")
    chip = owner // 2
    core = owner % 2
    loads = [pltpu.make_async_copy(got.at[pl.ds(16 * n, 16)], held.at[pl.ds(16 * n, 16)], ins.at[n]) for n in range(8)]
    for load in loads:
        load.start()
    total[...] = jnp.zeros(total.shape, f32)

    def step(s, _):
        source = (s & 3) * 32 + ((s >> 2) & 3) * (8 - 6 * core) + (s >> 5) * (2 + 6 * core) + ((s >> 4) & 1)
        near = first[0, 2 * source]
        far = first[0, 2 * source + 1]
        mine = jnp.where(near >> 7 == chip, near, far)
        column = jnp.where(mine >> 7 == chip, jnp.minimum(mine & 63, 62), 64)
        for n in range(2):
            total[pl.ds(pl.multiple_of((column + n) * 40, 8), 32), :] += held[s, n].astype(f32)
        return 0

    for n in range(8):
        loads[n].wait()
        lax.fori_loop(16 * n, 16 * n + 16, step, 0, unroll=4)
    stores = []
    for t in range(8):
        for j in range(32):
            rows[8 * t : 8 * t + 8, 128 * j : 128 * j + 128] = total[pl.ds(320 * t + j, 8, stride=40), :]
        store = pltpu.make_async_copy(rows.at[pl.ds(8 * t, 8)], out.at[pl.ds(8 * t, 8)], outs.at[t])
        store.start()
        stores.append(store)
    for i in range(2):
        loss[i] = losses[i]
    for store in stores:
        store.wait()


def body(mask_tiles, correlation, target, socs_kernels, socs_weights):
    first = correlation.T
    Rb, RTb, T3, TB = tables()
    S = pl.BlockSpec(memory_space=pltpu.SMEM)
    A = pl.BlockSpec(memory_space=pl.ANY)
    D = pltpu.SemaphoreType.DMA
    got, losses = pl.pallas_call(
        functools.partial(step_kernel, 8),
        out_shape=(jax.ShapeDtypeStruct((128, 2, 32, TS), bf16), jax.ShapeDtypeStruct((2,), f32)),
        in_specs=[S, S] + [A] * 7,
        out_specs=(A, S),
        scratch_shapes=[
            pltpu.VMEM((64, TS * TS), bf16),
            pltpu.VMEM((64, PITCH, TS), f32),
            pltpu.VMEM((2, W * W), bf16),
            pltpu.VMEM((4 * W, TS), f32),
            pltpu.VMEM((NK, KS, 2, KS), f32),
            pltpu.VMEM((W, W), bf16),
            pltpu.VMEM((W, W), bf16),
            pltpu.VMEM((W, 48), bf16),
            pltpu.VMEM((128, W), f32),
            pltpu.VMEM((W, W), f32),
            pltpu.VMEM((32, 2, TS, TS), bf16),
            *[pltpu.VMEM((8, 2, TS, TS), bf16)] * 4,
            pltpu.VMEM((16, 2, TS, TS), bf16),
            *[pltpu.VMEM((8, 2, TS, TS), bf16)] * 2,
            pltpu.VMEM((16, 2, 32, TS), bf16),
            pltpu.VMEM((16, 2, 32, TS), bf16),
            pltpu.VMEM((64, 2, 32, TS), bf16),
            pltpu.VMEM((128, 2, 32, TS), bf16),
            pltpu.VMEM((CH, 16, 128), f32),
            pltpu.VMEM((CH, 48, W), bf16),
            pltpu.VMEM((CH, 4, HF, HF), f32),
            pltpu.VMEM((4, HF, HF), f32),
            pltpu.VMEM((4, HF, HF), f32),
            pltpu.VMEM((CH, W, W), f32),
            pltpu.VMEM((W, W), f32),
            *[pltpu.VMEM((CH, 1, W), f32)] * 3,
            D((10,)), D, D((4,)), D, D((2,)), D, D((2,)), D, D((2,)), D, D, D,
        ],
        compiler_params=pltpu.CompilerParams(vmem_limit_bytes=56 * 2**20, collective_id=0, has_side_effects=True),
    )(first, socs_weights, mask_tiles, target, socs_kernels.transpose(1, 2, 0, 3),
        jnp.asarray(Rb), jnp.asarray(RTb), jnp.asarray(T3), jnp.asarray(TB))
    return pl.pallas_call(sum_kernel,
        out_shape=(jax.ShapeDtypeStruct((64, 4096), f32), jax.ShapeDtypeStruct((2,), f32)),
        in_specs=[S, S, A], out_specs=(A, S),
        scratch_shapes=[pltpu.VMEM((128, 2, 32, TS), bf16), pltpu.VMEM((66 * 40, TS), f32), pltpu.VMEM((64, 4096), f32), D((8,)), D((8,))],
    )(first, losses, got)


def solution(mesh):
    placed = (P("owner", None), P(), P(("clip", "owner"), None), P(), P())
    return jax.shard_map(body, mesh=mesh, in_specs=placed,
        out_specs=(P("owner", "clip"), P(("clip", "owner"))), check_vma=False)
```

```python
import functools

import jax
import jax.numpy as jnp
import ml_dtypes
import numpy as np
from jax import lax
from jax.experimental import pallas as pl
from jax.experimental.pallas import tpu as pltpu
from jax.sharding import PartitionSpec as P

TS=128; W=256; HF=128; KS=15; AM=7; NK=12; CH=24
PITCH = 136
MESH = pl.DeviceIdType.MESH
f32=jnp.float32; bf16=jnp.bfloat16

def tables():
    u = np.arange(HF) + 0.5
    y = np.arange(W)
    ang = 2*np.pi*u[:,None]*y[None,:]/W
    R = np.concatenate([np.cos(ang), np.sin(ang)], 0)
    b = np.arange(KS)-AM
    ang2 = 2*np.pi*u[:,None]*b[None,:]/W
    T = np.concatenate([np.cos(ang2), np.sin(ang2)], 0)
    T16 = np.zeros((W,16)); T16[:,:KS]=T
    hi = T16.astype(np.float32).astype(ml_dtypes.bfloat16)
    lo = (T16-hi.astype(np.float64)).astype(np.float32).astype(ml_dtypes.bfloat16)
    T3 = np.concatenate([hi,hi,lo],1)
    TB = np.zeros((W, 128)); TB[:,:KS]=T
    TB = TB.T.astype(np.float32)
    Rb = R.astype(np.float32).astype(ml_dtypes.bfloat16)
    return Rb, np.ascontiguousarray(Rb.T), T3, TB

def dot(a,b):
    return jnp.dot(a,b,preferred_element_type=f32)


def quarters(s):
    return s[:HF, :HF], s[:HF, HF:], s[HF:, :HF], s[HF:, HF:]


def whole(cc, cs, sc, ss):
    return jnp.concatenate([jnp.concatenate([cc, cs], 1), jnp.concatenate([sc, ss], 1)], 0)


def step_kernel(unroll, first, sw, mask_in, target_in, taps_in, r_in, rt_in, t3_in, tb_in, got, loss,
        raw, mask, wide, target, taps, r, rt, t3, tb, rsum, out, held0, held1, held2, held3, mid, recv0, recv1, grads, across, lines, back, pad, taph, spec, sfreq, acc, field, inten, level, flow, amp,
        ins, s1s, s1r, s2s, s2r, xs, xr, gs, gr, bs, br, ls):
    held = (held0, held1, held2, held3)
    recv = (recv0, recv1)
    plane = lax.axis_index("clip")
    owner = lax.axis_index("owner")
    me = plane * 32 + owner
    chip = owner // 2
    core = owner % 2
    y = chip % 4
    z = chip // 4

    def at(route, a, b, c):
        return a * (8 - 6 * route) + b * (2 + 6 * route) + c

    def drain(ref, count, sem):
        part = ref.at[pl.ds(0, count)]
        pltpu.make_async_copy(part, part, sem).wait()

    def send(src, dst, send_sem, recv_sem, p, to):
        pltpu.make_async_remote_copy(src_ref=src, dst_ref=dst, send_sem=send_sem, recv_sem=recv_sem,
            device_id=(p, to), device_id_type=MESH).start()

    barrier = pltpu.get_barrier_semaphore()
    partners = [(plane, owner + 1 - 2 * core)]
    for j in (1, 2, 3):
        partners.append(((plane + j) % 4, owner))
        for c in range(2):
            partners.append((plane, at(0, (z + j) % 4, y, c)))
            partners.append((plane, at(0, z, (y + j) % 4, c)))
    for to in partners:
        pl.semaphore_signal(barrier, inc=1, device_id=to, device_id_type=MESH)

    loads = [pltpu.make_async_copy(mask_in.at[pl.ds(16 * n, 16)], raw.at[pl.ds(16 * n, 16)], ins.at[n]) for n in range(4)]
    loads += [
        pltpu.make_async_copy(src, dst, ins.at[4 + n])
        for n, (src, dst) in enumerate(((taps_in, taps), (tb_in, tb), (t3_in, t3), (target_in, wide), (r_in, r), (rt_in, rt)))
    ]
    for load in loads:
        load.start()

    a = z + core * (y - z)
    b = y + core * (z - y)

    def pick(k):
        b2 = (b + 1 + k) % 4

        def one(n, _):
            a2 = (a + n // 2) % 4
            c = n % 2
            dest = plane * 32 + at(core, a2, b2, c)
            near = first[0, 2 * dest]
            far = first[0, 2 * dest + 1]
            column = jnp.minimum(jnp.where(near >> 7 == chip, near, far) & 63, 62)
            slot = a2 * 8 + b2 * 2 + c
            for n2 in range(2):
                out[slot, n2] = mask[column + n2, :TS].astype(bf16)
            return 0

        lax.fori_loop(0, 8, one, 0)

    def first_stage(k):
        b2 = (b + 1 + k) % 4
        for j in (2, 1, 3):
            a2 = (a + j) % 4
            send(out.at[pl.ds(a2 * 8 + b2 * 2, 2)], held[k].at[pl.ds(a * 2, 2)], s1s, s1r.at[k],
                plane, at(core, a2, b, core))
        for c in range(2):
            held[k][a * 2 + c] = out[a * 8 + b2 * 2 + c]

    def second_stage(k, i):
        if i == 0:
            drain(held[k], 6, s1r.at[k])
        b2 = (b + 1 + k) % 4
        if True:
            for c in range(2):
                dest = plane * 32 + at(core, a, b2, c)
                pair = first[0, 2 * dest + i] >> 7
                from_z = pair >> 2
                from_a = from_z + core * ((pair & 3) - from_z)
                mid[b2 * 4 + c * 2 + i] = held[k][from_a * 2 + c]
            if k < 3:
                for c in range(2):
                    send(mid.at[b2 * 4 + c * 2 + i], recv[i].at[core * 4 + b], s2s, s2r.at[i],
                        plane, at(core, a, b2, c))
            else:
                send(mid.at[b2 * 4 + (1 - core) * 2 + i], recv[i].at[core * 4 + b], s2s, s2r.at[i],
                    plane, owner + 1 - 2 * core)
                recv[i][core * 4 + b] = mid[b2 * 4 + core * 2 + i]

    flat = mask.reshape(64 * PITCH, TS)
    for n in range(4):
        loads[n].wait()

        def rows(j, _):
            v = raw[16 * n : 16 * n + 16, pl.ds(pl.multiple_of(j * TS, TS), TS)].astype(f32)
            flat[pl.ds(16 * n * PITCH + j, 8, stride=PITCH), :] = v[:8]
            flat[pl.ds((16 * n + 8) * PITCH + j, 8, stride=PITCH), :] = v[8:]
            return 0

        lax.fori_loop(0, TS, rows, 0, unroll=8)

    pick(0)
    pl.semaphore_wait(barrier, len(partners))
    first_stage(0)
    for k in (1, 2, 3):
        pick(k)
        first_stage(k)

    for load in loads[4:7]:
        load.wait()
    pad[...] = jnp.zeros(pad.shape, f32)
    for c in range(CH):
        pad[c, :KS, :KS] = taps[c % NK, :, c // NK, :]
        amp[c] = jnp.full((1, W), jnp.sqrt(sw[c % NK] * (1.0 / NK)))
    flow[...] = jnp.broadcast_to(
        jnp.sum(jnp.sum(pad[...], axis=1, keepdims=True), axis=2, keepdims=True), flow.shape)
    m = jnp.dot((pad[...] * amp[:, :, :128]).reshape(CH * 16, 128), tb[...], precision=lax.Precision.HIGHEST,
        preferred_element_type=f32).reshape(CH, 16, W)
    high = m.astype(bf16)
    taph[:, 0:16, :] = high
    taph[:, 16:32, :] = (m - high.astype(f32)).astype(bf16)
    taph[:, 32:48, :] = high

    def spectrum(c, _):
        cc, cs, sc, ss = quarters(dot(t3[...], taph[c]))
        spec[c, 0] = cc - ss
        spec[c, 1] = sc + cs
        spec[c, 2] = cc + ss
        spec[c, 3] = sc - cs
        return 0

    for k in range(4):
        second_stage(k, 0)
        if k < 3:
            lax.fori_loop(8 * k, 8 * k + 8, spectrum, 0, unroll=8)

    for k in range(4):
        second_stage(k, 1)
    for load in loads[7:]:
        load.wait()

    def widen(n, _):
        target[pl.ds(n, 2, stride=2 * W), :] = wide[:, pl.ds(pl.multiple_of(n * TS, TS), TS)].astype(f32)
        return 0

    lax.fori_loop(0, 2 * W, widen, 0, unroll=8)
    rsum[...] = dot(r[...], jnp.full((W, W), 1.0, bf16))

    def transform(i):
        pair = first[0, 2 * me + i] >> 7
        top = recv[i][pair & 3]
        low = recv[i][4 + (pair >> 2)]
        x = whole(top[0], top[1], low[0], low[1])
        sums = jnp.sum(x.astype(f32), axis=0, keepdims=True)
        rounded = sums.astype(bf16).astype(f32)
        t = (dot(r[...], x) - rsum[...] * (0.5 - (rounded - sums) * (1.0 / W))).astype(bf16)
        zero = flow[...] * jnp.sum(rounded)
        level[...] = amp[...] * (0.5 * flow[...] + (zero.astype(bf16).astype(f32) - zero) * (1.0 / (W * W)))
        cc, cs, sc, ss = quarters(dot(t, rt[...]) * (0.5 / (HF * HF)))
        sfreq[0] = cc - ss
        sfreq[1] = sc + cs
        sfreq[2] = cc + ss
        sfreq[3] = sc - cs

    def back_to_pixels(aa, bb, a2, b2):
        u = dot(whole(aa + a2, bb - b2, bb + b2, a2 - aa).astype(bf16), r[...]).astype(bf16)
        return dot(rt[...], u)

    def forward():
        inten[...] = jnp.zeros((W, W), f32)

        def channel(c, _):
            p, q, p2, q2 = (sfreq[j] for j in range(4))
            m, n, m2, n2 = (spec[c, j] for j in range(4))
            e = back_to_pixels(p * m - q * n, p * n + q * m, p2 * m2 - q2 * n2, p2 * n2 + q2 * m2) + level[c]
            field[c] = e
            inten[...] = inten[...] + e * e
            return 0

        lax.fori_loop(0, CH, channel, 0, unroll=unroll)

    def resist(i):
        row = lax.broadcasted_iota(jnp.int32, (W, W), 0)
        col = lax.broadcasted_iota(jnp.int32, (W, W), 1)
        inside = (row >= AM) & (row < W - AM) & (col >= AM) & (col < W - AM)
        level_at = 1.0 / (1.0 + jnp.exp(-10.0 * (inten[...] - 0.3)))
        goal = jnp.concatenate([target[pl.ds(i * 2 * W + n, W, stride=2), :] for n in range(2)], 1)
        miss = jnp.where(inside, level_at - goal, 0.0)
        loss[i] = jnp.sum(miss * miss) * (1.0 / ((W - 2 * AM) ** 2))
        inten[...] = 40.0 * miss * level_at * (1.0 - level_at)

    def backward():
        acc[...] = jnp.zeros(acc.shape, f32)

        def channel(c, _):
            g = (inten[...] * field[c]).astype(bf16)
            v = dot(g, rt[...]).astype(bf16)
            cc, cs, sc, ss = quarters(dot(r[...], v))
            p, q, p2, q2 = cc - ss, sc + cs, cc + ss, sc - cs
            m, n, m2, n2 = (spec[c, j] for j in range(4))
            acc[0] += p * m + q * n
            acc[1] += q * m - p * n
            acc[2] += p2 * m2 + q2 * n2
            acc[3] += q2 * m2 - p2 * n2
            return 0

        lax.fori_loop(0, CH, channel, 0, unroll=unroll)

    def finish(i):
        d = back_to_pixels(*(acc[j] * (0.5 / (HF * HF)) for j in range(4))).astype(bf16)
        for q in range(4):
            for part in range(2):
                for slot in range(2):
                    row = part * TS + q * 32
                    grads[i * 8 + q * 2 + part, slot] = d[row : row + 32, slot * TS : slot * TS + TS]

    def to_planes(i):
        for j in (1, 2, 3):
            p = (plane + j) % 4
            for part in range(2):
                send(grads.at[i * 8 + p * 2 + part], across.at[i * 8 + part * 4 + plane], xs, xr.at[i], p, owner)
        for part in range(2):
            across[i * 8 + part * 4 + plane] = grads[i * 8 + plane * 2 + part]

    def to_line(i):
        drain(across, 6, xr.at[i])
        for j in (2, 1, 3):
            for part in range(2):
                pa, pb = (z, y) if part == 0 else (y, z)
                here = across.at[pl.ds(i * 8 + part * 4, 4)]
                send(here, lines.at[pl.ds(part * 32 + pa * 8 + i * 4, 4)], gs, gr.at[i],
                    plane, at(part, (pa + j) % 4, pb, core))

    def to_owners(j, part, begin, end):
        pa, pb = (z, y) if part == 0 else (y, z)
        b2 = (pb + j) % 4
        goal = pa * 4 + b2 if part == 0 else b2 * 4 + pa

        def one(n, _):
            a_src = (pa + n // 4) % 4
            x_src = n % 4
            source = x_src * 32 + at(part, a_src, pb, core)
            which = jnp.where(first[0, 2 * source + 1] >> 7 == goal, 1, 0)
            if begin == 0:
                back[part * 64 + b2 * 16 + n] = across[which * 8 + part * 4 + x_src]
            else:
                back[part * 64 + b2 * 16 + n] = lines[part * 32 + a_src * 8 + which * 4 + x_src]
            return 0

        lax.fori_loop(begin, end, one, 0, unroll=4)
        src = back.at[pl.ds(part * 64 + b2 * 16 + begin, end - begin)]
        dst = got.at[pl.ds((pb * 2 + core) * 16 + begin, end - begin)]
        if j:
            send(src, dst, bs, br, plane, at(part, pa, b2, part))
        else:

            @pl.when(core == part)
            def _():
                pltpu.make_async_copy(src, dst, ls).start()

            @pl.when(core != part)
            def _():
                send(src, dst, bs, br, plane, owner + 1 - 2 * core)

    drain(recv[0], 7, s2r.at[0])
    transform(0)
    forward()
    resist(0)
    backward()
    finish(0)
    to_planes(0)
    drain(recv[1], 7, s2r.at[1])
    transform(1)
    forward()
    to_line(0)
    resist(1)
    backward()
    finish(1)
    to_planes(1)
    to_line(1)
    for begin, end in ((0, 4), (4, 16)):
        if begin:
            drain(lines, 24, gr.at[0])
            drain(lines, 24, gr.at[1])
        for j in (2, 1, 3, 0):
            for part in range(2):
                to_owners(j, part, begin, end)
    drain(out, 24, s1s)
    drain(mid, 14, s2s)
    drain(grads, 12, xs)
    drain(lines, 48, gs)
    drain(back, 112, bs)
    drain(got, 16, ls)
    drain(got, 112, br)


def sum_kernel(first, losses, got, out, loss, held, total, rows, ins, outs):
    owner = lax.axis_index("owner")
    chip = owner // 2
    core = owner % 2
    here = (owner >> 3) + core * (((owner >> 1) & 3) - (owner >> 3))
    loads = [pltpu.make_async_copy(got.at[pl.ds(16 * n, 16)], held.at[pl.ds(16 * n, 16)], ins.at[n]) for n in range(8)]
    for load in loads:
        load.start()
    total[...] = jnp.zeros(total.shape, f32)

    def step(s, _):
        line = ((s >> 2) + here) & 3
        source = (s & 3) * 32 + line * (8 - 6 * core) + (s >> 5) * (2 + 6 * core) + ((s >> 4) & 1)
        near = first[0, 2 * source]
        far = first[0, 2 * source + 1]
        mine = jnp.where(near >> 7 == chip, near, far)
        column = jnp.where(mine >> 7 == chip, jnp.minimum(mine & 63, 62), 64)
        for n in range(2):
            total[pl.ds(pl.multiple_of((column + n) * 40, 8), 32), :] += held[s, n].astype(f32)
        return 0

    for n in range(8):
        loads[n].wait()
        lax.fori_loop(16 * n, 16 * n + 16, step, 0, unroll=4)
    stores = []
    for t in range(8):
        for j in range(32):
            rows[8 * t : 8 * t + 8, 128 * j : 128 * j + 128] = total[pl.ds(320 * t + j, 8, stride=40), :]
        store = pltpu.make_async_copy(rows.at[pl.ds(8 * t, 8)], out.at[pl.ds(8 * t, 8)], outs.at[t])
        store.start()
        stores.append(store)
    for i in range(2):
        loss[i] = losses[i]
    for store in stores:
        store.wait()


def body(mask_tiles, correlation, target, socs_kernels, socs_weights):
    first = correlation.T
    Rb, RTb, T3, TB = tables()
    S = pl.BlockSpec(memory_space=pltpu.SMEM)
    A = pl.BlockSpec(memory_space=pl.ANY)
    D = pltpu.SemaphoreType.DMA
    got, losses = pl.pallas_call(
        functools.partial(step_kernel, 24),
        out_shape=(jax.ShapeDtypeStruct((128, 2, 32, TS), bf16), jax.ShapeDtypeStruct((2,), f32)),
        in_specs=[S, S] + [A] * 7,
        out_specs=(A, S),
        scratch_shapes=[
            pltpu.VMEM((64, TS * TS), bf16),
            pltpu.VMEM((64, PITCH, TS), f32),
            pltpu.VMEM((2, W * W), bf16),
            pltpu.VMEM((4 * W, TS), f32),
            pltpu.VMEM((NK, KS, 2, KS), f32),
            pltpu.VMEM((W, W), bf16),
            pltpu.VMEM((W, W), bf16),
            pltpu.VMEM((W, 48), bf16),
            pltpu.VMEM((128, W), f32),
            pltpu.VMEM((W, W), f32),
            pltpu.VMEM((32, 2, TS, TS), bf16),
            *[pltpu.VMEM((8, 2, TS, TS), bf16)] * 4,
            pltpu.VMEM((16, 2, TS, TS), bf16),
            *[pltpu.VMEM((8, 2, TS, TS), bf16)] * 2,
            pltpu.VMEM((16, 2, 32, TS), bf16),
            pltpu.VMEM((16, 2, 32, TS), bf16),
            pltpu.VMEM((64, 2, 32, TS), bf16),
            pltpu.VMEM((128, 2, 32, TS), bf16),
            pltpu.VMEM((CH, 16, 128), f32),
            pltpu.VMEM((CH, 48, W), bf16),
            pltpu.VMEM((CH, 4, HF, HF), f32),
            pltpu.VMEM((4, HF, HF), f32),
            pltpu.VMEM((4, HF, HF), f32),
            pltpu.VMEM((CH, W, W), f32),
            pltpu.VMEM((W, W), f32),
            *[pltpu.VMEM((CH, 1, W), f32)] * 3,
            D((10,)), D, D((4,)), D, D((2,)), D, D((2,)), D, D((2,)), D, D, D,
        ],
        compiler_params=pltpu.CompilerParams(vmem_limit_bytes=56 * 2**20, collective_id=0, has_side_effects=True),
    )(first, socs_weights, mask_tiles, target, socs_kernels.transpose(1, 2, 0, 3),
        jnp.asarray(Rb), jnp.asarray(RTb), jnp.asarray(T3), jnp.asarray(TB))
    return pl.pallas_call(sum_kernel,
        out_shape=(jax.ShapeDtypeStruct((64, 4096), f32), jax.ShapeDtypeStruct((2,), f32)),
        in_specs=[S, S, A], out_specs=(A, S),
        scratch_shapes=[pltpu.VMEM((128, 2, 32, TS), bf16), pltpu.VMEM((66 * 40, TS), f32), pltpu.VMEM((64, 4096), f32), D((8,)), D((8,))],
    )(first, losses, got)


def solution(mesh):
    placed = (P("owner", None), P(), P(("clip", "owner"), None), P(), P())
    return jax.shard_map(body, mesh=mesh, in_specs=placed,
        out_specs=(P("owner", "clip"), P(("clip", "owner"))), check_vma=False)
```

```python
import functools

import jax
import jax.numpy as jnp
import ml_dtypes
import numpy as np
from jax import lax
from jax.experimental import pallas as pl
from jax.experimental.pallas import tpu as pltpu
from jax.sharding import PartitionSpec as P

TS=128; W=256; HF=128; KS=15; AM=7; NK=12; CH=24
PITCH = 136
MESH = pl.DeviceIdType.MESH
f32=jnp.float32; bf16=jnp.bfloat16

def tables():
    u = np.arange(HF) + 0.5
    y = np.arange(W)
    ang = 2*np.pi*u[:,None]*y[None,:]/W
    R = np.concatenate([np.cos(ang), np.sin(ang)], 0)
    b = np.arange(KS)-AM
    ang2 = 2*np.pi*u[:,None]*b[None,:]/W
    T = np.concatenate([np.cos(ang2), np.sin(ang2)], 0)
    T16 = np.zeros((W,16)); T16[:,:KS]=T
    hi = T16.astype(np.float32).astype(ml_dtypes.bfloat16)
    lo = (T16-hi.astype(np.float64)).astype(np.float32).astype(ml_dtypes.bfloat16)
    T3 = np.concatenate([hi,hi,lo],1)
    TB = np.zeros((W, 128)); TB[:,:KS]=T
    TB = TB.T.astype(np.float32)
    Rb = R.astype(np.float32).astype(ml_dtypes.bfloat16)
    return Rb, np.ascontiguousarray(Rb.T), T3, TB

def dot(a,b):
    return jnp.dot(a,b,preferred_element_type=f32)


def quarters(s):
    return s[:HF, :HF], s[:HF, HF:], s[HF:, :HF], s[HF:, HF:]


def whole(cc, cs, sc, ss):
    return jnp.concatenate([jnp.concatenate([cc, cs], 1), jnp.concatenate([sc, ss], 1)], 0)


def step_kernel(unroll, first, sw, mask_in, target_in, taps_in, r_in, rt_in, t3_in, tb_in, got, loss,
        raw, mask, wide, target, taps, r, rt, t3, tb, rsum, out, held0, held1, held2, held3, mid, recv0, recv1, grads, across, line1, line2, line3, back, pad, taph, spec, sfreq, acc, field, inten, level, flow, amp,
        ins, s1s, s1r, s2s, s2r, xs, xr, gs, gr, bs, br, ls):
    held = (held0, held1, held2, held3)
    recv = (recv0, recv1)
    lines = (None, line1, line2, line3)
    plane = lax.axis_index("clip")
    owner = lax.axis_index("owner")
    me = plane * 32 + owner
    chip = owner // 2
    core = owner % 2
    y = chip % 4
    z = chip // 4

    def at(route, a, b, c):
        return a * (8 - 6 * route) + b * (2 + 6 * route) + c

    def drain(ref, count, sem):
        part = ref.at[pl.ds(0, count)]
        pltpu.make_async_copy(part, part, sem).wait()

    def send(src, dst, send_sem, recv_sem, p, to):
        pltpu.make_async_remote_copy(src_ref=src, dst_ref=dst, send_sem=send_sem, recv_sem=recv_sem,
            device_id=(p, to), device_id_type=MESH).start()

    barrier = pltpu.get_barrier_semaphore()
    partners = [(plane, owner + 1 - 2 * core)]
    for j in (1, 2, 3):
        partners.append(((plane + j) % 4, owner))
        for c in range(2):
            partners.append((plane, at(0, (z + j) % 4, y, c)))
            partners.append((plane, at(0, z, (y + j) % 4, c)))
    for to in partners:
        pl.semaphore_signal(barrier, inc=1, device_id=to, device_id_type=MESH)

    loads = [pltpu.make_async_copy(mask_in.at[pl.ds(16 * n, 16)], raw.at[pl.ds(16 * n, 16)], ins.at[n]) for n in range(4)]
    loads += [
        pltpu.make_async_copy(src, dst, ins.at[4 + n])
        for n, (src, dst) in enumerate(((taps_in, taps), (tb_in, tb), (t3_in, t3), (target_in, wide), (r_in, r), (rt_in, rt)))
    ]
    for load in loads:
        load.start()

    a = z + core * (y - z)
    b = y + core * (z - y)

    def pick(k):
        b2 = (b + 1 + k) % 4

        def one(n, _):
            a2 = (a + n // 2) % 4
            c = n % 2
            dest = plane * 32 + at(core, a2, b2, c)
            near = first[0, 2 * dest]
            far = first[0, 2 * dest + 1]
            column = jnp.minimum(jnp.where(near >> 7 == chip, near, far) & 63, 62)
            slot = a2 * 8 + b2 * 2 + c
            for n2 in range(2):
                out[slot, n2] = mask[column + n2, :TS].astype(bf16)
            return 0

        lax.fori_loop(0, 8, one, 0)

    def first_stage(k):
        b2 = (b + 1 + k) % 4
        for j in (2, 1, 3):
            a2 = (a + j) % 4
            send(out.at[pl.ds(a2 * 8 + b2 * 2, 2)], held[k].at[pl.ds(a * 2, 2)], s1s, s1r.at[k],
                plane, at(core, a2, b, core))
        for c in range(2):
            held[k][a * 2 + c] = out[a * 8 + b2 * 2 + c]

    def second_stage(k, i):
        if i == 0:
            drain(held[k], 6, s1r.at[k])
        b2 = (b + 1 + k) % 4
        if True:
            for c in range(2):
                dest = plane * 32 + at(core, a, b2, c)
                pair = first[0, 2 * dest + i] >> 7
                from_z = pair >> 2
                from_a = from_z + core * ((pair & 3) - from_z)
                mid[b2 * 4 + c * 2 + i] = held[k][from_a * 2 + c]
            if k < 3:
                for c in range(2):
                    send(mid.at[b2 * 4 + c * 2 + i], recv[i].at[core * 4 + b], s2s, s2r.at[i],
                        plane, at(core, a, b2, c))
            else:
                send(mid.at[b2 * 4 + (1 - core) * 2 + i], recv[i].at[core * 4 + b], s2s, s2r.at[i],
                    plane, owner + 1 - 2 * core)
                recv[i][core * 4 + b] = mid[b2 * 4 + core * 2 + i]

    flat = mask.reshape(64 * PITCH, TS)
    for n in range(4):
        loads[n].wait()

        def rows(j, _):
            v = raw[16 * n : 16 * n + 16, pl.ds(pl.multiple_of(j * TS, TS), TS)].astype(f32)
            flat[pl.ds(16 * n * PITCH + j, 8, stride=PITCH), :] = v[:8]
            flat[pl.ds((16 * n + 8) * PITCH + j, 8, stride=PITCH), :] = v[8:]
            return 0

        lax.fori_loop(0, TS, rows, 0, unroll=8)

    pick(0)
    pl.semaphore_wait(barrier, len(partners))
    first_stage(0)
    for k in (1, 2, 3):
        pick(k)
        first_stage(k)

    for load in loads[4:7]:
        load.wait()
    pad[...] = jnp.zeros(pad.shape, f32)
    for c in range(CH):
        pad[c, :KS, :KS] = taps[c % NK, :, c // NK, :]
        amp[c] = jnp.full((1, W), jnp.sqrt(sw[c % NK] * (1.0 / NK)))
    flow[...] = jnp.broadcast_to(
        jnp.sum(jnp.sum(pad[...], axis=1, keepdims=True), axis=2, keepdims=True), flow.shape)
    m = jnp.dot((pad[...] * amp[:, :, :128]).reshape(CH * 16, 128), tb[...], precision=lax.Precision.HIGHEST,
        preferred_element_type=f32).reshape(CH, 16, W)
    high = m.astype(bf16)
    taph[:, 0:16, :] = high
    taph[:, 16:32, :] = (m - high.astype(f32)).astype(bf16)
    taph[:, 32:48, :] = high

    def spectrum(c, _):
        cc, cs, sc, ss = quarters(dot(t3[...], taph[c]))
        spec[c, 0] = cc - ss
        spec[c, 1] = sc + cs
        spec[c, 2] = cc + ss
        spec[c, 3] = sc - cs
        return 0

    for k in range(4):
        second_stage(k, 0)
        if k < 3:
            lax.fori_loop(8 * k, 8 * k + 8, spectrum, 0, unroll=8)

    for k in range(4):
        second_stage(k, 1)
    for load in loads[7:]:
        load.wait()

    def widen(n, _):
        target[pl.ds(n, 2, stride=2 * W), :] = wide[:, pl.ds(pl.multiple_of(n * TS, TS), TS)].astype(f32)
        return 0

    lax.fori_loop(0, 2 * W, widen, 0, unroll=8)
    rsum[...] = dot(r[...], jnp.full((W, W), 1.0, bf16))

    def transform(i):
        pair = first[0, 2 * me + i] >> 7
        top = recv[i][pair & 3]
        low = recv[i][4 + (pair >> 2)]
        x = whole(top[0], top[1], low[0], low[1])
        sums = jnp.sum(x.astype(f32), axis=0, keepdims=True)
        rounded = sums.astype(bf16).astype(f32)
        t = (dot(r[...], x) - rsum[...] * (0.5 - (rounded - sums) * (1.0 / W))).astype(bf16)
        zero = flow[...] * jnp.sum(rounded)
        level[...] = amp[...] * (0.5 * flow[...] + (zero.astype(bf16).astype(f32) - zero) * (1.0 / (W * W)))
        cc, cs, sc, ss = quarters(dot(t, rt[...]) * (0.5 / (HF * HF)))
        sfreq[0] = cc - ss
        sfreq[1] = sc + cs
        sfreq[2] = cc + ss
        sfreq[3] = sc - cs

    def back_to_pixels(aa, bb, a2, b2):
        u = dot(whole(aa + a2, bb - b2, bb + b2, a2 - aa).astype(bf16), r[...]).astype(bf16)
        return dot(rt[...], u)

    def forward():
        inten[...] = jnp.zeros((W, W), f32)

        def channel(c, _):
            p, q, p2, q2 = (sfreq[j] for j in range(4))
            m, n, m2, n2 = (spec[c, j] for j in range(4))
            e = back_to_pixels(p * m - q * n, p * n + q * m, p2 * m2 - q2 * n2, p2 * n2 + q2 * m2) + level[c]
            field[c] = e
            inten[...] = inten[...] + e * e
            return 0

        lax.fori_loop(0, CH, channel, 0, unroll=unroll)

    def resist(i):
        row = lax.broadcasted_iota(jnp.int32, (W, W), 0)
        col = lax.broadcasted_iota(jnp.int32, (W, W), 1)
        inside = (row >= AM) & (row < W - AM) & (col >= AM) & (col < W - AM)
        level_at = 1.0 / (1.0 + jnp.exp(-10.0 * (inten[...] - 0.3)))
        goal = jnp.concatenate([target[pl.ds(i * 2 * W + n, W, stride=2), :] for n in range(2)], 1)
        miss = jnp.where(inside, level_at - goal, 0.0)
        loss[i] = jnp.sum(miss * miss) * (1.0 / ((W - 2 * AM) ** 2))
        inten[...] = 40.0 * miss * level_at * (1.0 - level_at)

    def backward():
        acc[...] = jnp.zeros(acc.shape, f32)

        def channel(c, _):
            g = (inten[...] * field[c]).astype(bf16)
            v = dot(g, rt[...]).astype(bf16)
            cc, cs, sc, ss = quarters(dot(r[...], v))
            p, q, p2, q2 = cc - ss, sc + cs, cc + ss, sc - cs
            m, n, m2, n2 = (spec[c, j] for j in range(4))
            acc[0] += p * m + q * n
            acc[1] += q * m - p * n
            acc[2] += p2 * m2 + q2 * n2
            acc[3] += q2 * m2 - p2 * n2
            return 0

        lax.fori_loop(0, CH, channel, 0, unroll=unroll)

    def finish(i):
        d = back_to_pixels(*(acc[j] * (0.5 / (HF * HF)) for j in range(4))).astype(bf16)
        for q in range(4):
            for part in range(2):
                for slot in range(2):
                    row = part * TS + q * 32
                    grads[i * 8 + q * 2 + part, slot] = d[row : row + 32, slot * TS : slot * TS + TS]

    def to_planes(i):
        for j in (1, 2, 3):
            p = (plane + j) % 4
            for part in range(2):
                send(grads.at[i * 8 + p * 2 + part], across.at[i * 8 + part * 4 + plane], xs, xr.at[i], p, owner)
        for part in range(2):
            across[i * 8 + part * 4 + plane] = grads[i * 8 + plane * 2 + part]

    def to_line(i):
        drain(across, 6, xr.at[i])
        for j in (1, 3, 2):
            for part in range(2):
                pa, pb = (z, y) if part == 0 else (y, z)
                here = across.at[pl.ds(i * 8 + part * 4, 4)]
                send(here, lines[j].at[pl.ds(part * 8 + i * 4, 4)], gs, gr.at[i * 4 + j],
                    plane, at(part, (pa + j) % 4, pb, core))

    def to_owners(j, part, step):
        pa, pb = (z, y) if part == 0 else (y, z)
        b2 = (pb + j) % 4
        goal = pa * 4 + b2 if part == 0 else b2 * 4 + pa

        def one(n, _):
            source = n * 32 + at(part, (pa - step) % 4, pb, core)
            which = jnp.where(first[0, 2 * source + 1] >> 7 == goal, 1, 0)
            place = part * 64 + b2 * 16 + step * 4 + n
            if step == 0:
                back[place] = across[which * 8 + part * 4 + n]
            else:
                back[place] = lines[step][part * 8 + which * 4 + n]
            return 0

        lax.fori_loop(0, 4, one, 0, unroll=4)
        src = back.at[pl.ds(part * 64 + b2 * 16 + step * 4, 4)]
        dst = got.at[pl.ds((pb * 2 + core) * 16 + step * 4, 4)]
        if j:
            send(src, dst, bs, br, plane, at(part, pa, b2, part))
        else:

            @pl.when(core == part)
            def _():
                pltpu.make_async_copy(src, dst, ls).start()

            @pl.when(core != part)
            def _():
                send(src, dst, bs, br, plane, owner + 1 - 2 * core)

    drain(recv[0], 7, s2r.at[0])
    transform(0)
    forward()
    resist(0)
    backward()
    finish(0)
    to_planes(0)
    drain(recv[1], 7, s2r.at[1])
    transform(1)
    forward()
    to_line(0)
    resist(1)
    backward()
    finish(1)
    to_planes(1)
    to_line(1)
    for step in (0, 1, 3, 2):
        if step:
            drain(lines[step], 8, gr.at[step])
            drain(lines[step], 8, gr.at[4 + step])
        for j in (2, 1, 3, 0):
            for part in range(2):
                to_owners(j, part, step)
    drain(out, 24, s1s)
    drain(mid, 14, s2s)
    drain(grads, 12, xs)
    drain(back, 48, gs)
    drain(back, 112, bs)
    drain(got, 16, ls)
    drain(got, 112, br)


def sum_kernel(first, losses, got, out, loss, held, t0, t1, t2, t3, rows, ins, outs):
    owner = lax.axis_index("owner")
    chip = owner // 2
    core = owner % 2
    here = (owner >> 3) + core * (((owner >> 1) & 3) - (owner >> 3))
    loads = [pltpu.make_async_copy(got.at[pl.ds(16 * n, 16)], held.at[pl.ds(16 * n, 16)], ins.at[n]) for n in range(8)]
    for load in loads:
        load.start()
    totals = (t0, t1, t2, t3)
    for total in totals:
        total[...] = jnp.zeros(total.shape, f32)

    def add(s, odd):
        line = (here - (s >> 2)) & 3
        source = (s & 3) * 32 + line * (8 - 6 * core) + (s >> 5) * (2 + 6 * core) + ((s >> 4) & 1)
        near = first[0, 2 * source]
        far = first[0, 2 * source + 1]
        mine = jnp.where(near >> 7 == chip, near, far)
        column = jnp.where(mine >> 7 == chip, jnp.minimum(mine & 63, 62), 64)
        for n in range(2):
            totals[2 * odd + n][pl.ds(pl.multiple_of((column + n) * 40, 8), 32), :] += held[s, n].astype(f32)

    def step(h, _):
        add(2 * h, 0)
        add(2 * h + 1, 1)
        return 0

    for n in range(8):
        loads[n].wait()
        lax.fori_loop(8 * n, 8 * n + 8, step, 0, unroll=4)
    stores = []
    for t in range(8):
        for j in range(32):
            rows[8 * t : 8 * t + 8, 128 * j : 128 * j + 128] = sum(
                total[pl.ds(320 * t + j, 8, stride=40), :] for total in totals)
        store = pltpu.make_async_copy(rows.at[pl.ds(8 * t, 8)], out.at[pl.ds(8 * t, 8)], outs.at[t])
        store.start()
        stores.append(store)
    for i in range(2):
        loss[i] = losses[i]
    for store in stores:
        store.wait()


def body(mask_tiles, correlation, target, socs_kernels, socs_weights):
    first = correlation.T
    Rb, RTb, T3, TB = tables()
    S = pl.BlockSpec(memory_space=pltpu.SMEM)
    A = pl.BlockSpec(memory_space=pl.ANY)
    D = pltpu.SemaphoreType.DMA
    got, losses = pl.pallas_call(
        functools.partial(step_kernel, 24),
        out_shape=(jax.ShapeDtypeStruct((128, 2, 32, TS), bf16), jax.ShapeDtypeStruct((2,), f32)),
        in_specs=[S, S] + [A] * 7,
        out_specs=(A, S),
        scratch_shapes=[
            pltpu.VMEM((64, TS * TS), bf16),
            pltpu.VMEM((64, PITCH, TS), f32),
            pltpu.VMEM((2, W * W), bf16),
            pltpu.VMEM((4 * W, TS), f32),
            pltpu.VMEM((NK, KS, 2, KS), f32),
            pltpu.VMEM((W, W), bf16),
            pltpu.VMEM((W, W), bf16),
            pltpu.VMEM((W, 48), bf16),
            pltpu.VMEM((128, W), f32),
            pltpu.VMEM((W, W), f32),
            pltpu.VMEM((32, 2, TS, TS), bf16),
            *[pltpu.VMEM((8, 2, TS, TS), bf16)] * 4,
            pltpu.VMEM((16, 2, TS, TS), bf16),
            *[pltpu.VMEM((8, 2, TS, TS), bf16)] * 2,
            pltpu.VMEM((16, 2, 32, TS), bf16),
            pltpu.VMEM((16, 2, 32, TS), bf16),
            *[pltpu.VMEM((16, 2, 32, TS), bf16)] * 3,
            pltpu.VMEM((128, 2, 32, TS), bf16),
            pltpu.VMEM((CH, 16, 128), f32),
            pltpu.VMEM((CH, 48, W), bf16),
            pltpu.VMEM((CH, 4, HF, HF), f32),
            pltpu.VMEM((4, HF, HF), f32),
            pltpu.VMEM((4, HF, HF), f32),
            pltpu.VMEM((CH, W, W), f32),
            pltpu.VMEM((W, W), f32),
            *[pltpu.VMEM((CH, 1, W), f32)] * 3,
            D((10,)), D, D((4,)), D, D((2,)), D, D((2,)), D, D((8,)), D, D, D,
        ],
        compiler_params=pltpu.CompilerParams(vmem_limit_bytes=56 * 2**20, collective_id=0, has_side_effects=True),
    )(first, socs_weights, mask_tiles, target, socs_kernels.transpose(1, 2, 0, 3),
        jnp.asarray(Rb), jnp.asarray(RTb), jnp.asarray(T3), jnp.asarray(TB))
    return pl.pallas_call(sum_kernel,
        out_shape=(jax.ShapeDtypeStruct((64, 4096), f32), jax.ShapeDtypeStruct((2,), f32)),
        in_specs=[S, S, A], out_specs=(A, S),
        scratch_shapes=[pltpu.VMEM((128, 2, 32, TS), bf16), *[pltpu.VMEM((66 * 40, TS), f32)] * 4, pltpu.VMEM((64, 4096), f32), D((8,)), D((8,))],
    )(first, losses, got)


def solution(mesh):
    placed = (P("owner", None), P(), P(("clip", "owner"), None), P(), P())
    return jax.shard_map(body, mesh=mesh, in_specs=placed,
        out_specs=(P("owner", "clip"), P(("clip", "owner"))), check_vma=False)
```

```python
import functools

import jax
import jax.numpy as jnp
import ml_dtypes
import numpy as np
from jax import lax
from jax.experimental import pallas as pl
from jax.experimental.pallas import tpu as pltpu
from jax.sharding import PartitionSpec as P

TS=128; W=256; HF=128; KS=15; AM=7; NK=12; CH=24
PITCH = 136
MESH = pl.DeviceIdType.MESH
f32=jnp.float32; bf16=jnp.bfloat16

def tables():
    u = np.arange(HF) + 0.5
    y = np.arange(W)
    ang = 2*np.pi*u[:,None]*y[None,:]/W
    R = np.concatenate([np.cos(ang), np.sin(ang)], 0)
    b = np.arange(KS)-AM
    ang2 = 2*np.pi*u[:,None]*b[None,:]/W
    T = np.concatenate([np.cos(ang2), np.sin(ang2)], 0)
    T16 = np.zeros((W,16)); T16[:,:KS]=T
    hi = T16.astype(np.float32).astype(ml_dtypes.bfloat16)
    lo = (T16-hi.astype(np.float64)).astype(np.float32).astype(ml_dtypes.bfloat16)
    T3 = np.concatenate([hi,hi,lo],1)
    TB = np.zeros((W, 128)); TB[:,:KS]=T
    TB = TB.T.astype(np.float32)
    Rb = R.astype(np.float32).astype(ml_dtypes.bfloat16)
    return Rb, np.ascontiguousarray(Rb.T), T3, TB

def dot(a,b):
    return jnp.dot(a,b,preferred_element_type=f32)


def quarters(s):
    return s[:HF, :HF], s[:HF, HF:], s[HF:, :HF], s[HF:, HF:]


def whole(cc, cs, sc, ss):
    return jnp.concatenate([jnp.concatenate([cc, cs], 1), jnp.concatenate([sc, ss], 1)], 0)


def step_kernel(unroll, first, sw, mask_in, target_in, taps_in, r_in, rt_in, t3_in, tb_in, got, loss,
        raw, mask, wide, target, taps, r, rt, t3, tb, rsum, out, held0, held1, held2, held3, mid, recv0, recv1, grads, across, lines, back, pad, taph, spec, sfreq, acc, field, inten, level, flow, amp,
        ins, s1s, s1r, s2s, s2r, xs, xr, gs, gr, bs, br, ls):
    held = (held0, held1, held2, held3)
    recv = (recv0, recv1)
    plane = lax.axis_index("clip")
    owner = lax.axis_index("owner")
    me = plane * 32 + owner
    chip = owner // 2
    core = owner % 2
    y = chip % 4
    z = chip // 4

    def at(route, a, b, c):
        return a * (8 - 6 * route) + b * (2 + 6 * route) + c

    def drain(ref, count, sem):
        part = ref.at[pl.ds(0, count)]
        pltpu.make_async_copy(part, part, sem).wait()

    def send(src, dst, send_sem, recv_sem, p, to):
        pltpu.make_async_remote_copy(src_ref=src, dst_ref=dst, send_sem=send_sem, recv_sem=recv_sem,
            device_id=(p, to), device_id_type=MESH).start()

    barrier = pltpu.get_barrier_semaphore()
    partners = [(plane, owner + 1 - 2 * core)]
    for j in (1, 2, 3):
        partners.append(((plane + j) % 4, owner))
        for c in range(2):
            partners.append((plane, at(0, (z + j) % 4, y, c)))
            partners.append((plane, at(0, z, (y + j) % 4, c)))
    for to in partners:
        pl.semaphore_signal(barrier, inc=1, device_id=to, device_id_type=MESH)

    loads = [pltpu.make_async_copy(mask_in.at[pl.ds(16 * n, 16)], raw.at[pl.ds(16 * n, 16)], ins.at[n]) for n in range(4)]
    loads += [
        pltpu.make_async_copy(src, dst, ins.at[4 + n])
        for n, (src, dst) in enumerate(((taps_in, taps), (tb_in, tb), (t3_in, t3), (target_in, wide), (r_in, r), (rt_in, rt)))
    ]
    for load in loads:
        load.start()

    a = z + core * (y - z)
    b = y + core * (z - y)

    def pick(k):
        b2 = (b + 1 + k) % 4

        def one(n, _):
            a2 = (a + n // 2) % 4
            c = n % 2
            dest = plane * 32 + at(core, a2, b2, c)
            near = first[0, 2 * dest]
            far = first[0, 2 * dest + 1]
            column = jnp.minimum(jnp.where(near >> 7 == chip, near, far) & 63, 62)
            slot = a2 * 8 + b2 * 2 + c
            for n2 in range(2):
                out[slot, n2] = mask[column + n2, :TS].astype(bf16)
            return 0

        lax.fori_loop(0, 8, one, 0)

    def first_stage(k):
        b2 = (b + 1 + k) % 4
        for j in (2, 1, 3):
            a2 = (a + j) % 4
            send(out.at[pl.ds(a2 * 8 + b2 * 2, 2)], held[k].at[pl.ds(a * 2, 2)], s1s, s1r.at[k],
                plane, at(core, a2, b, core))
        for c in range(2):
            held[k][a * 2 + c] = out[a * 8 + b2 * 2 + c]

    def second_stage(k, i):
        if i == 0:
            drain(held[k], 6, s1r.at[k])
        b2 = (b + 1 + k) % 4
        if True:
            for c in range(2):
                dest = plane * 32 + at(core, a, b2, c)
                pair = first[0, 2 * dest + i] >> 7
                from_z = pair >> 2
                from_a = from_z + core * ((pair & 3) - from_z)
                mid[b2 * 4 + c * 2 + i] = held[k][from_a * 2 + c]
            if k < 3:
                for c in range(2):
                    send(mid.at[b2 * 4 + c * 2 + i], recv[i].at[core * 4 + b], s2s, s2r.at[i],
                        plane, at(core, a, b2, c))
            else:
                send(mid.at[b2 * 4 + (1 - core) * 2 + i], recv[i].at[core * 4 + b], s2s, s2r.at[i],
                    plane, owner + 1 - 2 * core)
                recv[i][core * 4 + b] = mid[b2 * 4 + core * 2 + i]

    flat = mask.reshape(64 * PITCH, TS)
    for n in range(4):
        loads[n].wait()

        def rows(j, _):
            v = raw[16 * n : 16 * n + 16, pl.ds(pl.multiple_of(j * TS, TS), TS)].astype(f32)
            flat[pl.ds(16 * n * PITCH + j, 8, stride=PITCH), :] = v[:8]
            flat[pl.ds((16 * n + 8) * PITCH + j, 8, stride=PITCH), :] = v[8:]
            return 0

        lax.fori_loop(0, TS, rows, 0, unroll=8)

    pick(0)
    pl.semaphore_wait(barrier, len(partners))
    first_stage(0)
    for k in (1, 2, 3):
        pick(k)
        first_stage(k)

    for load in loads[4:7]:
        load.wait()
    pad[...] = jnp.zeros(pad.shape, f32)
    for c in range(CH):
        pad[c, :KS, :KS] = taps[c % NK, :, c // NK, :]
        amp[c] = jnp.full((1, W), jnp.sqrt(sw[c % NK] * (1.0 / NK)))
    flow[...] = jnp.broadcast_to(
        jnp.sum(jnp.sum(pad[...], axis=1, keepdims=True), axis=2, keepdims=True), flow.shape)
    m = jnp.dot((pad[...] * amp[:, :, :128]).reshape(CH * 16, 128), tb[...], precision=lax.Precision.HIGHEST,
        preferred_element_type=f32).reshape(CH, 16, W)
    high = m.astype(bf16)
    taph[:, 0:16, :] = high
    taph[:, 16:32, :] = (m - high.astype(f32)).astype(bf16)
    taph[:, 32:48, :] = high

    def spectrum(c, _):
        cc, cs, sc, ss = quarters(dot(t3[...], taph[c]))
        spec[c, 0] = cc - ss
        spec[c, 1] = sc + cs
        spec[c, 2] = cc + ss
        spec[c, 3] = sc - cs
        return 0

    for k in range(4):
        second_stage(k, 0)
        if k < 3:
            lax.fori_loop(8 * k, 8 * k + 8, spectrum, 0, unroll=8)

    for k in range(4):
        second_stage(k, 1)
    for load in loads[7:]:
        load.wait()

    def widen(n, _):
        target[pl.ds(n, 2, stride=2 * W), :] = wide[:, pl.ds(pl.multiple_of(n * TS, TS), TS)].astype(f32)
        return 0

    lax.fori_loop(0, 2 * W, widen, 0, unroll=8)
    rsum[...] = dot(r[...], jnp.full((W, W), 1.0, bf16))

    def transform(i):
        pair = first[0, 2 * me + i] >> 7
        top = recv[i][pair & 3]
        low = recv[i][4 + (pair >> 2)]
        x = whole(top[0], top[1], low[0], low[1])
        sums = jnp.sum(x.astype(f32), axis=0, keepdims=True)
        rounded = sums.astype(bf16).astype(f32)
        t = (dot(r[...], x) - rsum[...] * (0.5 - (rounded - sums) * (1.0 / W))).astype(bf16)
        zero = flow[...] * jnp.sum(rounded)
        level[...] = amp[...] * (0.5 * flow[...] + (zero.astype(bf16).astype(f32) - zero) * (1.0 / (W * W)))
        cc, cs, sc, ss = quarters(dot(t, rt[...]) * (0.5 / (HF * HF)))
        sfreq[0] = cc - ss
        sfreq[1] = sc + cs
        sfreq[2] = cc + ss
        sfreq[3] = sc - cs

    def back_to_pixels(aa, bb, a2, b2):
        u = dot(whole(aa + a2, bb - b2, bb + b2, a2 - aa).astype(bf16), r[...]).astype(bf16)
        return dot(rt[...], u)

    def forward():
        inten[...] = jnp.zeros((W, W), f32)

        def channel(c, _):
            p, q, p2, q2 = (sfreq[j] for j in range(4))
            m, n, m2, n2 = (spec[c, j] for j in range(4))
            e = back_to_pixels(p * m - q * n, p * n + q * m, p2 * m2 - q2 * n2, p2 * n2 + q2 * m2) + level[c]
            field[c] = e
            inten[...] = inten[...] + e * e
            return 0

        lax.fori_loop(0, CH, channel, 0, unroll=unroll)

    def resist(i):
        row = lax.broadcasted_iota(jnp.int32, (W, W), 0)
        col = lax.broadcasted_iota(jnp.int32, (W, W), 1)
        inside = (row >= AM) & (row < W - AM) & (col >= AM) & (col < W - AM)
        level_at = 1.0 / (1.0 + jnp.exp(-10.0 * (inten[...] - 0.3)))
        goal = jnp.concatenate([target[pl.ds(i * 2 * W + n, W, stride=2), :] for n in range(2)], 1)
        miss = jnp.where(inside, level_at - goal, 0.0)
        loss[i] = jnp.sum(miss * miss) * (1.0 / ((W - 2 * AM) ** 2))
        inten[...] = 40.0 * miss * level_at * (1.0 - level_at)

    def backward():
        acc[...] = jnp.zeros(acc.shape, f32)

        def channel(c, _):
            g = (inten[...] * field[c]).astype(bf16)
            v = dot(g, rt[...]).astype(bf16)
            cc, cs, sc, ss = quarters(dot(r[...], v))
            p, q, p2, q2 = cc - ss, sc + cs, cc + ss, sc - cs
            m, n, m2, n2 = (spec[c, j] for j in range(4))
            acc[0] += p * m + q * n
            acc[1] += q * m - p * n
            acc[2] += p2 * m2 + q2 * n2
            acc[3] += q2 * m2 - p2 * n2
            return 0

        lax.fori_loop(0, CH, channel, 0, unroll=unroll)

    def finish(i):
        d = back_to_pixels(*(acc[j] * (0.5 / (HF * HF)) for j in range(4))).astype(bf16)
        for q in range(4):
            for part in range(2):
                for slot in range(2):
                    row = part * TS + q * 32
                    grads[i * 8 + q * 2 + part, slot] = d[row : row + 32, slot * TS : slot * TS + TS]

    def to_planes(i):
        for j in (1, 2, 3):
            p = (plane + j) % 4
            for part in range(2):
                send(grads.at[i * 8 + p * 2 + part], across.at[i * 8 + part * 4 + plane], xs, xr.at[i], p, owner)
        for part in range(2):
            across[i * 8 + part * 4 + plane] = grads[i * 8 + plane * 2 + part]

    def to_line(i):
        drain(across, 6, xr.at[i])
        for j in (2, 1, 3):
            for part in range(2):
                pa, pb = (z, y) if part == 0 else (y, z)
                here = across.at[pl.ds(i * 8 + part * 4, 4)]
                send(here, lines.at[pl.ds(part * 32 + pa * 8 + i * 4, 4)], gs, gr.at[i],
                    plane, at(part, (pa + j) % 4, pb, core))

    def to_owners(j, part, begin, end):
        pa, pb = (z, y) if part == 0 else (y, z)
        b2 = (pb + j) % 4
        goal = pa * 4 + b2 if part == 0 else b2 * 4 + pa

        def one(n, _):
            a_src = (pa + n // 4) % 4
            x_src = n % 4
            source = x_src * 32 + at(part, a_src, pb, core)
            which = jnp.where(first[0, 2 * source + 1] >> 7 == goal, 1, 0)
            if begin == 0:
                back[part * 64 + b2 * 16 + n] = across[which * 8 + part * 4 + x_src]
            else:
                back[part * 64 + b2 * 16 + n] = lines[part * 32 + a_src * 8 + which * 4 + x_src]
            return 0

        lax.fori_loop(begin, end, one, 0, unroll=4)
        src = back.at[pl.ds(part * 64 + b2 * 16 + begin, end - begin)]
        dst = got.at[pl.ds((pb * 2 + core) * 16 + begin, end - begin)]
        if j:
            send(src, dst, bs, br, plane, at(part, pa, b2, part))
        else:

            @pl.when(core == part)
            def _():
                pltpu.make_async_copy(src, dst, ls).start()

            @pl.when(core != part)
            def _():
                send(src, dst, bs, br, plane, owner + 1 - 2 * core)

    drain(recv[0], 7, s2r.at[0])
    transform(0)
    forward()
    resist(0)
    backward()
    finish(0)
    to_planes(0)
    drain(recv[1], 7, s2r.at[1])
    transform(1)
    forward()
    to_line(0)
    resist(1)
    backward()
    finish(1)
    to_planes(1)
    to_line(1)
    for begin, end in ((0, 4), (4, 16)):
        if begin:
            drain(lines, 24, gr.at[0])
            drain(lines, 24, gr.at[1])
        for j in (2, 1, 3, 0):
            for part in range(2):
                to_owners(j, part, begin, end)
    drain(out, 24, s1s)
    drain(mid, 14, s2s)
    drain(grads, 12, xs)
    drain(lines, 48, gs)
    drain(back, 112, bs)
    drain(got, 16, ls)
    drain(got, 112, br)


def sum_kernel(first, losses, got, out, loss, total, rows, outs):
    owner = lax.axis_index("owner")
    chip = owner // 2
    core = owner % 2
    here = (owner >> 3) + core * (((owner >> 1) & 3) - (owner >> 3))
    total[...] = jnp.zeros(total.shape, f32)

    def step(s, _):
        line = ((s >> 2) + here) & 3
        source = (s & 3) * 32 + line * (8 - 6 * core) + (s >> 5) * (2 + 6 * core) + ((s >> 4) & 1)
        near = first[0, 2 * source]
        far = first[0, 2 * source + 1]
        mine = jnp.where(near >> 7 == chip, near, far)
        column = jnp.where(mine >> 7 == chip, jnp.minimum(mine & 63, 62), 64)
        for n in range(2):
            total[pl.ds(pl.multiple_of((column + n) * 40, 8), 32), :] += got[s, n].astype(f32)
        return 0

    lax.fori_loop(0, 128, step, 0, unroll=16)
    stores = []
    for t in range(8):
        for j in range(32):
            rows[8 * t : 8 * t + 8, 128 * j : 128 * j + 128] = total[pl.ds(320 * t + j, 8, stride=40), :]
        store = pltpu.make_async_copy(rows.at[pl.ds(8 * t, 8)], out.at[pl.ds(8 * t, 8)], outs.at[t])
        store.start()
        stores.append(store)
    for i in range(2):
        loss[i] = losses[i]
    for store in stores:
        store.wait()


def body(mask_tiles, correlation, target, socs_kernels, socs_weights):
    first = correlation.T
    Rb, RTb, T3, TB = tables()
    S = pl.BlockSpec(memory_space=pltpu.SMEM)
    A = pl.BlockSpec(memory_space=pl.ANY)
    H = pl.BlockSpec(memory_space=pltpu.HBM)
    V = pl.BlockSpec(memory_space=pltpu.VMEM)
    D = pltpu.SemaphoreType.DMA
    got, losses = pl.pallas_call(
        functools.partial(step_kernel, 24),
        out_shape=(jax.ShapeDtypeStruct((128, 2, 32, TS), bf16), jax.ShapeDtypeStruct((2,), f32)),
        in_specs=[S, S] + [H] * 7,
        out_specs=(A, S),
        scratch_shapes=[
            pltpu.VMEM((64, TS * TS), bf16),
            pltpu.VMEM((64, PITCH, TS), f32),
            pltpu.VMEM((2, W * W), bf16),
            pltpu.VMEM((4 * W, TS), f32),
            pltpu.VMEM((NK, KS, 2, KS), f32),
            pltpu.VMEM((W, W), bf16),
            pltpu.VMEM((W, W), bf16),
            pltpu.VMEM((W, 48), bf16),
            pltpu.VMEM((128, W), f32),
            pltpu.VMEM((W, W), f32),
            pltpu.VMEM((32, 2, TS, TS), bf16),
            *[pltpu.VMEM((8, 2, TS, TS), bf16)] * 4,
            pltpu.VMEM((16, 2, TS, TS), bf16),
            *[pltpu.VMEM((8, 2, TS, TS), bf16)] * 2,
            pltpu.VMEM((16, 2, 32, TS), bf16),
            pltpu.VMEM((16, 2, 32, TS), bf16),
            pltpu.VMEM((64, 2, 32, TS), bf16),
            pltpu.VMEM((128, 2, 32, TS), bf16),
            pltpu.VMEM((CH, 16, 128), f32),
            pltpu.VMEM((CH, 48, W), bf16),
            pltpu.VMEM((CH, 4, HF, HF), f32),
            pltpu.VMEM((4, HF, HF), f32),
            pltpu.VMEM((4, HF, HF), f32),
            pltpu.VMEM((CH, W, W), f32),
            pltpu.VMEM((W, W), f32),
            *[pltpu.VMEM((CH, 1, W), f32)] * 3,
            D((10,)), D, D((4,)), D, D((2,)), D, D((2,)), D, D((2,)), D, D, D,
        ],
        compiler_params=pltpu.CompilerParams(vmem_limit_bytes=34 * 2**20, collective_id=0, has_side_effects=True),
    )(first, socs_weights, mask_tiles, target, socs_kernels.transpose(1, 2, 0, 3),
        jnp.asarray(Rb), jnp.asarray(RTb), jnp.asarray(T3), jnp.asarray(TB))
    return pl.pallas_call(sum_kernel,
        out_shape=(jax.ShapeDtypeStruct((64, 4096), f32), jax.ShapeDtypeStruct((2,), f32)),
        in_specs=[S, S, V], out_specs=(A, S),
        scratch_shapes=[pltpu.VMEM((66 * 40, TS), f32), pltpu.VMEM((64, 4096), f32), D((8,))],
    )(first, losses, got)


def solution(mesh):
    placed = (P("owner", None), P(), P(("clip", "owner"), None), P(), P())
    return jax.shard_map(body, mesh=mesh, in_specs=placed,
        out_specs=(P("owner", "clip"), P(("clip", "owner"))), check_vma=False)
```

```python
import functools

import jax
import jax.numpy as jnp
import ml_dtypes
import numpy as np
from jax import lax
from jax.experimental import pallas as pl
from jax.experimental.pallas import tpu as pltpu
from jax.sharding import PartitionSpec as P

TS=128; W=256; HF=128; KS=15; AM=7; NK=12; CH=24
PITCH = 136
MESH = pl.DeviceIdType.MESH
f32=jnp.float32; bf16=jnp.bfloat16

def tables():
    u = np.arange(HF) + 0.5
    y = np.arange(W)
    ang = 2*np.pi*u[:,None]*y[None,:]/W
    R = np.concatenate([np.cos(ang), np.sin(ang)], 0)
    b = np.arange(KS)-AM
    ang2 = 2*np.pi*u[:,None]*b[None,:]/W
    T = np.concatenate([np.cos(ang2), np.sin(ang2)], 0)
    T16 = np.zeros((W,16)); T16[:,:KS]=T
    hi = T16.astype(np.float32).astype(ml_dtypes.bfloat16)
    lo = (T16-hi.astype(np.float64)).astype(np.float32).astype(ml_dtypes.bfloat16)
    T3 = np.concatenate([hi,hi,lo],1)
    TB = np.zeros((W, 128)); TB[:,:KS]=T
    TB = TB.T.astype(np.float32)
    Rb = R.astype(np.float32).astype(ml_dtypes.bfloat16)
    return Rb, np.ascontiguousarray(Rb.T), T3, TB

def dot(a,b):
    return jnp.dot(a,b,preferred_element_type=f32)


def quarters(s):
    return s[:HF, :HF], s[:HF, HF:], s[HF:, :HF], s[HF:, HF:]


def whole(cc, cs, sc, ss):
    return jnp.concatenate([jnp.concatenate([cc, cs], 1), jnp.concatenate([sc, ss], 1)], 0)


def step_kernel(unroll, first, sw, mask_in, target_in, taps_in, r_in, rt_in, t3_in, tb_in, got, loss,
        raw, mask, wide, target, taps, r, rt, t3, tb, rsum, out, held0, held1, held2, held3, mid, recv0, recv1, grads, across, line1, line2, line3, back, pad, taph, spec, sfreq, acc, field, inten, level, flow, amp,
        ins, s1s, s1r, s2s, s2r, xs, xr, gs, gr, bs, br, ls):
    held = (held0, held1, held2, held3)
    recv = (recv0, recv1)
    lines = (None, line1, line2, line3)
    plane = lax.axis_index("clip")
    owner = lax.axis_index("owner")
    me = plane * 32 + owner
    chip = owner // 2
    core = owner % 2
    y = chip % 4
    z = chip // 4

    def at(route, a, b, c):
        return a * (8 - 6 * route) + b * (2 + 6 * route) + c

    def drain(ref, count, sem):
        part = ref.at[pl.ds(0, count)]
        pltpu.make_async_copy(part, part, sem).wait()

    def send(src, dst, send_sem, recv_sem, p, to):
        pltpu.make_async_remote_copy(src_ref=src, dst_ref=dst, send_sem=send_sem, recv_sem=recv_sem,
            device_id=(p, to), device_id_type=MESH).start()

    barrier = pltpu.get_barrier_semaphore()
    partners = [(plane, owner + 1 - 2 * core)]
    for j in (1, 2, 3):
        partners.append(((plane + j) % 4, owner))
        for c in range(2):
            partners.append((plane, at(0, (z + j) % 4, y, c)))
            partners.append((plane, at(0, z, (y + j) % 4, c)))
    for j in (1, 2, 3):
        for p in (1, 2, 3):
            partners.append(((plane + p) % 4, at(0, (z + j) % 4, y, core)))
            partners.append(((plane + p) % 4, at(0, z, (y + j) % 4, core)))
    for to in partners:
        pl.semaphore_signal(barrier, inc=1, device_id=to, device_id_type=MESH)

    loads = [pltpu.make_async_copy(mask_in.at[pl.ds(16 * n, 16)], raw.at[pl.ds(16 * n, 16)], ins.at[n]) for n in range(4)]
    loads += [
        pltpu.make_async_copy(src, dst, ins.at[4 + n])
        for n, (src, dst) in enumerate(((taps_in, taps), (tb_in, tb), (t3_in, t3), (target_in, wide), (r_in, r), (rt_in, rt)))
    ]
    for load in loads:
        load.start()

    a = z + core * (y - z)
    b = y + core * (z - y)

    def pick(k):
        b2 = (b + 1 + k) % 4

        def one(n, _):
            a2 = (a + n // 2) % 4
            c = n % 2
            dest = plane * 32 + at(core, a2, b2, c)
            near = first[0, 2 * dest]
            far = first[0, 2 * dest + 1]
            column = jnp.minimum(jnp.where(near >> 7 == chip, near, far) & 63, 62)
            slot = a2 * 8 + b2 * 2 + c
            for n2 in range(2):
                out[slot, n2] = mask[column + n2, :TS].astype(bf16)
            return 0

        lax.fori_loop(0, 8, one, 0)

    def first_stage(k):
        b2 = (b + 1 + k) % 4
        for j in (2, 1, 3):
            a2 = (a + j) % 4
            send(out.at[pl.ds(a2 * 8 + b2 * 2, 2)], held[k].at[pl.ds(a * 2, 2)], s1s, s1r.at[k],
                plane, at(core, a2, b, core))
        for c in range(2):
            held[k][a * 2 + c] = out[a * 8 + b2 * 2 + c]

    def second_stage(k, i):
        if i == 0:
            drain(held[k], 6, s1r.at[k])
        b2 = (b + 1 + k) % 4
        if True:
            for c in range(2):
                dest = plane * 32 + at(core, a, b2, c)
                pair = first[0, 2 * dest + i] >> 7
                from_z = pair >> 2
                from_a = from_z + core * ((pair & 3) - from_z)
                mid[b2 * 4 + c * 2 + i] = held[k][from_a * 2 + c]
            if k < 3:
                for c in range(2):
                    send(mid.at[b2 * 4 + c * 2 + i], recv[i].at[core * 4 + b], s2s, s2r.at[i],
                        plane, at(core, a, b2, c))
            else:
                send(mid.at[b2 * 4 + (1 - core) * 2 + i], recv[i].at[core * 4 + b], s2s, s2r.at[i],
                    plane, owner + 1 - 2 * core)
                recv[i][core * 4 + b] = mid[b2 * 4 + core * 2 + i]

    flat = mask.reshape(64 * PITCH, TS)
    for n in range(4):
        loads[n].wait()

        def rows(j, _):
            v = raw[16 * n : 16 * n + 16, pl.ds(pl.multiple_of(j * TS, TS), TS)].astype(f32)
            flat[pl.ds(16 * n * PITCH + j, 8, stride=PITCH), :] = v[:8]
            flat[pl.ds((16 * n + 8) * PITCH + j, 8, stride=PITCH), :] = v[8:]
            return 0

        lax.fori_loop(0, TS, rows, 0, unroll=8)

    pick(0)
    pl.semaphore_wait(barrier, len(partners))
    first_stage(0)
    for k in (1, 2, 3):
        pick(k)
        first_stage(k)

    for load in loads[4:7]:
        load.wait()
    pad[...] = jnp.zeros(pad.shape, f32)
    for c in range(CH):
        pad[c, :KS, :KS] = taps[c % NK, :, c // NK, :]
        amp[c] = jnp.full((1, W), jnp.sqrt(sw[c % NK] * (1.0 / NK)))
    flow[...] = jnp.broadcast_to(
        jnp.sum(jnp.sum(pad[...], axis=1, keepdims=True), axis=2, keepdims=True), flow.shape)
    m = jnp.dot((pad[...] * amp[:, :, :128]).reshape(CH * 16, 128), tb[...], precision=lax.Precision.HIGHEST,
        preferred_element_type=f32).reshape(CH, 16, W)
    high = m.astype(bf16)
    taph[:, 0:16, :] = high
    taph[:, 16:32, :] = (m - high.astype(f32)).astype(bf16)
    taph[:, 32:48, :] = high

    def spectrum(c, _):
        cc, cs, sc, ss = quarters(dot(t3[...], taph[c]))
        spec[c, 0] = cc - ss
        spec[c, 1] = sc + cs
        spec[c, 2] = cc + ss
        spec[c, 3] = sc - cs
        return 0

    for k in range(4):
        second_stage(k, 0)
        if k < 3:
            lax.fori_loop(8 * k, 8 * k + 8, spectrum, 0, unroll=8)

    for k in range(4):
        second_stage(k, 1)
    for load in loads[7:]:
        load.wait()

    def widen(n, _):
        target[pl.ds(n, 2, stride=2 * W), :] = wide[:, pl.ds(pl.multiple_of(n * TS, TS), TS)].astype(f32)
        return 0

    lax.fori_loop(0, 2 * W, widen, 0, unroll=8)
    rsum[...] = dot(r[...], jnp.full((W, W), 1.0, bf16))

    def transform(i):
        pair = first[0, 2 * me + i] >> 7
        top = recv[i][pair & 3]
        low = recv[i][4 + (pair >> 2)]
        x = whole(top[0], top[1], low[0], low[1])
        sums = jnp.sum(x.astype(f32), axis=0, keepdims=True)
        rounded = sums.astype(bf16).astype(f32)
        t = (dot(r[...], x) - rsum[...] * (0.5 - (rounded - sums) * (1.0 / W))).astype(bf16)
        zero = flow[...] * jnp.sum(rounded)
        level[...] = amp[...] * (0.5 * flow[...] + (zero.astype(bf16).astype(f32) - zero) * (1.0 / (W * W)))
        cc, cs, sc, ss = quarters(dot(t, rt[...]) * (0.5 / (HF * HF)))
        sfreq[0] = cc - ss
        sfreq[1] = sc + cs
        sfreq[2] = cc + ss
        sfreq[3] = sc - cs

    def back_to_pixels(aa, bb, a2, b2):
        u = dot(whole(aa + a2, bb - b2, bb + b2, a2 - aa).astype(bf16), r[...]).astype(bf16)
        return dot(rt[...], u)

    def forward():
        inten[...] = jnp.zeros((W, W), f32)

        def channel(c, _):
            p, q, p2, q2 = (sfreq[j] for j in range(4))
            m, n, m2, n2 = (spec[c, j] for j in range(4))
            e = back_to_pixels(p * m - q * n, p * n + q * m, p2 * m2 - q2 * n2, p2 * n2 + q2 * m2) + level[c]
            field[c] = e
            inten[...] = inten[...] + e * e
            return 0

        lax.fori_loop(0, CH, channel, 0, unroll=unroll)

    def resist(i):
        row = lax.broadcasted_iota(jnp.int32, (W, W), 0)
        col = lax.broadcasted_iota(jnp.int32, (W, W), 1)
        inside = (row >= AM) & (row < W - AM) & (col >= AM) & (col < W - AM)
        level_at = 1.0 / (1.0 + jnp.exp(-10.0 * (inten[...] - 0.3)))
        goal = jnp.concatenate([target[pl.ds(i * 2 * W + n, W, stride=2), :] for n in range(2)], 1)
        miss = jnp.where(inside, level_at - goal, 0.0)
        loss[i] = jnp.sum(miss * miss) * (1.0 / ((W - 2 * AM) ** 2))
        inten[...] = 40.0 * miss * level_at * (1.0 - level_at)

    def backward():
        acc[...] = jnp.zeros(acc.shape, f32)

        def channel(c, _):
            g = (inten[...] * field[c]).astype(bf16)
            v = dot(g, rt[...]).astype(bf16)
            cc, cs, sc, ss = quarters(dot(r[...], v))
            p, q, p2, q2 = cc - ss, sc + cs, cc + ss, sc - cs
            m, n, m2, n2 = (spec[c, j] for j in range(4))
            acc[0] += p * m + q * n
            acc[1] += q * m - p * n
            acc[2] += p2 * m2 + q2 * n2
            acc[3] += q2 * m2 - p2 * n2
            return 0

        lax.fori_loop(0, CH, channel, 0, unroll=unroll)

    def finish(i):
        d = back_to_pixels(*(acc[j] * (0.5 / (HF * HF)) for j in range(4))).astype(bf16)
        for q in range(4):
            for part in range(2):
                for slot in range(2):
                    row = part * TS + q * 32
                    grads[i * 8 + q * 2 + part, slot] = d[row : row + 32, slot * TS : slot * TS + TS]

    def to_planes(i):
        for j in (1, 2, 3):
            p = (plane + j) % 4
            for part in range(2):
                send(grads.at[i * 8 + p * 2 + part], across.at[i * 8 + part * 4 + plane], xs, xr.at[i], p, owner)
        for part in range(2):
            across[i * 8 + part * 4 + plane] = grads[i * 8 + plane * 2 + part]

    def to_line(i):
        drain(across, 6, xr.at[i])
        for j in (1, 3, 2):
            for part in range(2):
                pa, pb = (z, y) if part == 0 else (y, z)
                here = across.at[pl.ds(i * 8 + part * 4, 4)]
                send(here, lines[j].at[pl.ds(part * 8 + i * 4, 4)], gs, gr.at[i * 4 + j],
                    plane, at(part, (pa + j) % 4, pb, core))

    def to_planes_and_line(i):
        for j in (0, 1, 3, 2):
            for q in (1, 3, 2, 0):
                p = (plane + q) % 4
                for part in range(2):
                    pa, pb = (z, y) if part == 0 else (y, z)
                    src = grads.at[i * 8 + p * 2 + part]
                    if j:
                        send(src, lines[j].at[part * 8 + i * 4 + plane], gs, gr.at[i * 4 + j],
                            p, at(part, (pa + j) % 4, pb, core))
                    elif q:
                        send(src, across.at[i * 8 + part * 4 + plane], xs, xr.at[i], p, owner)
        for part in range(2):
            across[i * 8 + part * 4 + plane] = grads[i * 8 + plane * 2 + part]
        drain(across, 6, xr.at[i])

    def to_owners(j, part, step):
        pa, pb = (z, y) if part == 0 else (y, z)
        b2 = (pb + j) % 4
        goal = pa * 4 + b2 if part == 0 else b2 * 4 + pa

        def one(n, _):
            source = n * 32 + at(part, (pa - step) % 4, pb, core)
            which = jnp.where(first[0, 2 * source + 1] >> 7 == goal, 1, 0)
            place = part * 64 + b2 * 16 + step * 4 + n
            if step == 0:
                back[place] = across[which * 8 + part * 4 + n]
            else:
                back[place] = lines[step][part * 8 + which * 4 + n]
            return 0

        lax.fori_loop(0, 4, one, 0, unroll=4)
        src = back.at[pl.ds(part * 64 + b2 * 16 + step * 4, 4)]
        dst = got.at[pl.ds((pb * 2 + core) * 16 + step * 4, 4)]
        if j:
            send(src, dst, bs, br, plane, at(part, pa, b2, part))
        else:

            @pl.when(core == part)
            def _():
                pltpu.make_async_copy(src, dst, ls).start()

            @pl.when(core != part)
            def _():
                send(src, dst, bs, br, plane, owner + 1 - 2 * core)

    drain(recv[0], 7, s2r.at[0])
    transform(0)
    forward()
    resist(0)
    backward()
    finish(0)
    to_planes(0)
    drain(recv[1], 7, s2r.at[1])
    transform(1)
    forward()
    to_line(0)
    resist(1)
    backward()
    finish(1)
    to_planes_and_line(1)
    for step in (0, 1, 3, 2):
        if step:
            drain(lines[step], 8, gr.at[step])
            drain(lines[step], 8, gr.at[4 + step])
        for j in (2, 1, 3, 0):
            for part in range(2):
                to_owners(j, part, step)
    drain(out, 24, s1s)
    drain(mid, 14, s2s)
    drain(grads, 12, xs)
    drain(back, 48, gs)
    drain(back, 112, bs)
    drain(got, 16, ls)
    drain(got, 112, br)


def sum_kernel(first, losses, got, out, loss, held, total, rows, ins, outs):
    owner = lax.axis_index("owner")
    chip = owner // 2
    core = owner % 2
    here = (owner >> 3) + core * (((owner >> 1) & 3) - (owner >> 3))
    loads = [pltpu.make_async_copy(got.at[pl.ds(16 * n, 16)], held.at[pl.ds(16 * n, 16)], ins.at[n]) for n in range(8)]
    for load in loads:
        load.start()
    total[...] = jnp.zeros(total.shape, f32)

    def step(s, _):
        line = (here - (s >> 2)) & 3
        source = (s & 3) * 32 + line * (8 - 6 * core) + (s >> 5) * (2 + 6 * core) + ((s >> 4) & 1)
        near = first[0, 2 * source]
        far = first[0, 2 * source + 1]
        mine = jnp.where(near >> 7 == chip, near, far)
        column = jnp.where(mine >> 7 == chip, jnp.minimum(mine & 63, 62), 64)
        for n in range(2):
            total[pl.ds(pl.multiple_of((column + n) * 40, 8), 32), :] += held[s, n].astype(f32)
        return 0

    for n in range(8):
        loads[n].wait()
        lax.fori_loop(16 * n, 16 * n + 16, step, 0, unroll=16)
    stores = []
    for t in range(8):
        for j in range(32):
            rows[8 * t : 8 * t + 8, 128 * j : 128 * j + 128] = total[pl.ds(320 * t + j, 8, stride=40), :]
        store = pltpu.make_async_copy(rows.at[pl.ds(8 * t, 8)], out.at[pl.ds(8 * t, 8)], outs.at[t])
        store.start()
        stores.append(store)
    for i in range(2):
        loss[i] = losses[i]
    for store in stores:
        store.wait()


def body(mask_tiles, correlation, target, socs_kernels, socs_weights):
    first = correlation.T
    Rb, RTb, T3, TB = tables()
    S = pl.BlockSpec(memory_space=pltpu.SMEM)
    A = pl.BlockSpec(memory_space=pl.ANY)
    D = pltpu.SemaphoreType.DMA
    got, losses = pl.pallas_call(
        functools.partial(step_kernel, 24),
        out_shape=(jax.ShapeDtypeStruct((128, 2, 32, TS), bf16), jax.ShapeDtypeStruct((2,), f32)),
        in_specs=[S, S] + [A] * 7,
        out_specs=(A, S),
        scratch_shapes=[
            pltpu.VMEM((64, TS * TS), bf16),
            pltpu.VMEM((64, PITCH, TS), f32),
            pltpu.VMEM((2, W * W), bf16),
            pltpu.VMEM((4 * W, TS), f32),
            pltpu.VMEM((NK, KS, 2, KS), f32),
            pltpu.VMEM((W, W), bf16),
            pltpu.VMEM((W, W), bf16),
            pltpu.VMEM((W, 48), bf16),
            pltpu.VMEM((128, W), f32),
            pltpu.VMEM((W, W), f32),
            pltpu.VMEM((32, 2, TS, TS), bf16),
            *[pltpu.VMEM((8, 2, TS, TS), bf16)] * 4,
            pltpu.VMEM((16, 2, TS, TS), bf16),
            *[pltpu.VMEM((8, 2, TS, TS), bf16)] * 2,
            pltpu.VMEM((16, 2, 32, TS), bf16),
            pltpu.VMEM((16, 2, 32, TS), bf16),
            *[pltpu.VMEM((16, 2, 32, TS), bf16)] * 3,
            pltpu.VMEM((128, 2, 32, TS), bf16),
            pltpu.VMEM((CH, 16, 128), f32),
            pltpu.VMEM((CH, 48, W), bf16),
            pltpu.VMEM((CH, 4, HF, HF), f32),
            pltpu.VMEM((4, HF, HF), f32),
            pltpu.VMEM((4, HF, HF), f32),
            pltpu.VMEM((CH, W, W), f32),
            pltpu.VMEM((W, W), f32),
            *[pltpu.VMEM((CH, 1, W), f32)] * 3,
            D((10,)), D, D((4,)), D, D((2,)), D, D((2,)), D, D((8,)), D, D, D,
        ],
        compiler_params=pltpu.CompilerParams(vmem_limit_bytes=56 * 2**20, collective_id=0, has_side_effects=True),
    )(first, socs_weights, mask_tiles, target, socs_kernels.transpose(1, 2, 0, 3),
        jnp.asarray(Rb), jnp.asarray(RTb), jnp.asarray(T3), jnp.asarray(TB))
    return pl.pallas_call(sum_kernel,
        out_shape=(jax.ShapeDtypeStruct((64, 4096), f32), jax.ShapeDtypeStruct((2,), f32)),
        in_specs=[S, S, A], out_specs=(A, S),
        scratch_shapes=[pltpu.VMEM((128, 2, 32, TS), bf16), pltpu.VMEM((66 * 40, TS), f32), pltpu.VMEM((64, 4096), f32), D((8,)), D((8,))],
    )(first, losses, got)


def solution(mesh):
    placed = (P("owner", None), P(), P(("clip", "owner"), None), P(), P())
    return jax.shard_map(body, mesh=mesh, in_specs=placed,
        out_specs=(P("owner", "clip"), P(("clip", "owner"))), check_vma=False)
```

```python
import functools

import jax
import jax.numpy as jnp
import ml_dtypes
import numpy as np
from jax import lax
from jax.experimental import pallas as pl
from jax.experimental.pallas import tpu as pltpu
from jax.sharding import PartitionSpec as P

TS=128; W=256; HF=128; KS=15; AM=7; NK=12; CH=24
PITCH = 136
MESH = pl.DeviceIdType.MESH
f32=jnp.float32; bf16=jnp.bfloat16

def tables():
    u = np.arange(HF) + 0.5
    y = np.arange(W)
    ang = 2*np.pi*u[:,None]*y[None,:]/W
    R = np.concatenate([np.cos(ang), np.sin(ang)], 0)
    b = np.arange(KS)-AM
    ang2 = 2*np.pi*u[:,None]*b[None,:]/W
    T = np.concatenate([np.cos(ang2), np.sin(ang2)], 0)
    T16 = np.zeros((W,16)); T16[:,:KS]=T
    hi = T16.astype(np.float32).astype(ml_dtypes.bfloat16)
    lo = (T16-hi.astype(np.float64)).astype(np.float32).astype(ml_dtypes.bfloat16)
    T3 = np.concatenate([hi,hi,lo],1)
    TB = np.zeros((W, 128)); TB[:,:KS]=T
    TB = TB.T.astype(np.float32)
    Rb = R.astype(np.float32).astype(ml_dtypes.bfloat16)
    return Rb, np.ascontiguousarray(Rb.T), T3, TB

def dot(a,b):
    return jnp.dot(a,b,preferred_element_type=f32)


def quarters(s):
    return s[:HF, :HF], s[:HF, HF:], s[HF:, :HF], s[HF:, HF:]


def whole(cc, cs, sc, ss):
    return jnp.concatenate([jnp.concatenate([cc, cs], 1), jnp.concatenate([sc, ss], 1)], 0)


def step_kernel(unroll, first, sw, mask_in, target_in, taps_in, r_in, rt_in, t3_in, tb_in, got, loss,
        raw, mask, wide, target, taps, r, rt, t3, tb, rsum, out, held0, held1, held2, held3, mid, recv0, recv1, grads, across, line1, line2, line3, back, pad, taph, spec, sfreq, acc, field, inten, level, flow, amp,
        ins, s1s, s1r, s2s, s2r, xs, xr, gs, gr, bs, br, ls):
    held = (held0, held1, held2, held3)
    recv = (recv0, recv1)
    lines = (None, line1, line2, line3)
    plane = lax.axis_index("clip")
    owner = lax.axis_index("owner")
    me = plane * 32 + owner
    chip = owner // 2
    core = owner % 2
    y = chip % 4
    z = chip // 4

    def at(route, a, b, c):
        return a * (8 - 6 * route) + b * (2 + 6 * route) + c

    def drain(ref, count, sem):
        part = ref.at[pl.ds(0, count)]
        pltpu.make_async_copy(part, part, sem).wait()

    def send(src, dst, send_sem, recv_sem, p, to):
        pltpu.make_async_remote_copy(src_ref=src, dst_ref=dst, send_sem=send_sem, recv_sem=recv_sem,
            device_id=(p, to), device_id_type=MESH).start()

    loads = [pltpu.make_async_copy(mask_in.at[pl.ds(16 * n, 16)], raw.at[pl.ds(16 * n, 16)], ins.at[n]) for n in range(4)]
    loads += [
        pltpu.make_async_copy(src, dst, ins.at[4 + n])
        for n, (src, dst) in enumerate(((taps_in, taps), (tb_in, tb), (t3_in, t3), (target_in, wide), (r_in, r), (rt_in, rt)))
    ]
    for load in loads:
        load.start()

    barrier = pltpu.get_barrier_semaphore()
    partners = [(plane, owner + 1 - 2 * core)]
    for j in (1, 2, 3):
        partners.append(((plane + j) % 4, owner))
        for c in range(2):
            partners.append((plane, at(0, (z + j) % 4, y, c)))
            partners.append((plane, at(0, z, (y + j) % 4, c)))
    for j in (1, 2, 3):
        for p in (1, 2, 3):
            partners.append(((plane + p) % 4, at(0, (z + j) % 4, y, core)))
            partners.append(((plane + p) % 4, at(0, z, (y + j) % 4, core)))
    for to in partners:
        pl.semaphore_signal(barrier, inc=1, device_id=to, device_id_type=MESH)

    a = z + core * (y - z)
    b = y + core * (z - y)

    def pick(k):
        b2 = (b + 1 + k) % 4

        def one(n, _):
            a2 = (a + n // 2) % 4
            c = n % 2
            dest = plane * 32 + at(core, a2, b2, c)
            near = first[0, 2 * dest]
            far = first[0, 2 * dest + 1]
            column = jnp.minimum(jnp.where(near >> 7 == chip, near, far) & 63, 62)
            slot = a2 * 8 + b2 * 2 + c
            for n2 in range(2):
                out[slot, n2] = mask[column + n2, :TS].astype(bf16)
            return 0

        lax.fori_loop(0, 8, one, 0)

    def first_stage(k):
        b2 = (b + 1 + k) % 4
        for j in (2, 1, 3):
            a2 = (a + j) % 4
            send(out.at[pl.ds(a2 * 8 + b2 * 2, 2)], held[k].at[pl.ds(a * 2, 2)], s1s, s1r.at[k],
                plane, at(core, a2, b, core))
        for c in range(2):
            held[k][a * 2 + c] = out[a * 8 + b2 * 2 + c]

    def second_stage(k, i):
        if i == 0:
            drain(held[k], 6, s1r.at[k])
        b2 = (b + 1 + k) % 4
        if True:
            for c in range(2):
                dest = plane * 32 + at(core, a, b2, c)
                pair = first[0, 2 * dest + i] >> 7
                from_z = pair >> 2
                from_a = from_z + core * ((pair & 3) - from_z)
                mid[b2 * 4 + c * 2 + i] = held[k][from_a * 2 + c]
            if k < 3:
                for c in range(2):
                    send(mid.at[b2 * 4 + c * 2 + i], recv[i].at[core * 4 + b], s2s, s2r.at[i],
                        plane, at(core, a, b2, c))
            else:
                send(mid.at[b2 * 4 + (1 - core) * 2 + i], recv[i].at[core * 4 + b], s2s, s2r.at[i],
                    plane, owner + 1 - 2 * core)
                recv[i][core * 4 + b] = mid[b2 * 4 + core * 2 + i]

    flat = mask.reshape(64 * PITCH, TS)
    for n in range(4):
        loads[n].wait()

        def rows(j, _):
            v = raw[16 * n : 16 * n + 16, pl.ds(pl.multiple_of(j * TS, TS), TS)].astype(f32)
            flat[pl.ds(16 * n * PITCH + j, 8, stride=PITCH), :] = v[:8]
            flat[pl.ds((16 * n + 8) * PITCH + j, 8, stride=PITCH), :] = v[8:]
            return 0

        lax.fori_loop(0, TS, rows, 0, unroll=32)

    pick(0)
    pl.semaphore_wait(barrier, len(partners))
    first_stage(0)
    for k in (1, 2, 3):
        pick(k)
        first_stage(k)

    for load in loads[4:7]:
        load.wait()
    pad[...] = jnp.zeros(pad.shape, f32)
    for c in range(CH):
        pad[c, :KS, :KS] = taps[c % NK, :, c // NK, :]
        amp[c] = jnp.full((1, W), jnp.sqrt(sw[c % NK] * (1.0 / NK)))
    flow[...] = jnp.broadcast_to(
        jnp.sum(jnp.sum(pad[...], axis=1, keepdims=True), axis=2, keepdims=True), flow.shape)
    m = jnp.dot((pad[...] * amp[:, :, :128]).reshape(CH * 16, 128), tb[...], precision=lax.Precision.HIGHEST,
        preferred_element_type=f32).reshape(CH, 16, W)
    high = m.astype(bf16)
    taph[:, 0:16, :] = high
    taph[:, 16:32, :] = (m - high.astype(f32)).astype(bf16)
    taph[:, 32:48, :] = high

    def spectrum(c, _):
        cc, cs, sc, ss = quarters(dot(t3[...], taph[c]))
        spec[c, 0] = cc - ss
        spec[c, 1] = sc + cs
        spec[c, 2] = cc + ss
        spec[c, 3] = sc - cs
        return 0

    for k in range(4):
        second_stage(k, 0)
        if k < 3:
            lax.fori_loop(8 * k, 8 * k + 8, spectrum, 0, unroll=8)

    for k in range(4):
        second_stage(k, 1)
    for load in loads[7:]:
        load.wait()

    def widen(n, _):
        target[pl.ds(n, 2, stride=2 * W), :] = wide[:, pl.ds(pl.multiple_of(n * TS, TS), TS)].astype(f32)
        return 0

    lax.fori_loop(0, 2 * W, widen, 0, unroll=8)
    rsum[...] = dot(r[...], jnp.full((W, W), 1.0, bf16))

    def transform(i):
        pair = first[0, 2 * me + i] >> 7
        top = recv[i][pair & 3]
        low = recv[i][4 + (pair >> 2)]
        x = whole(top[0], top[1], low[0], low[1])
        sums = jnp.sum(x.astype(f32), axis=0, keepdims=True)
        rounded = sums.astype(bf16).astype(f32)
        t = (dot(r[...], x) - rsum[...] * (0.5 - (rounded - sums) * (1.0 / W))).astype(bf16)
        zero = flow[...] * jnp.sum(rounded)
        level[CH * i : CH * i + CH] = amp[...] * (0.5 * flow[...] + (zero.astype(bf16).astype(f32) - zero) * (1.0 / (W * W)))
        cc, cs, sc, ss = quarters(dot(t, rt[...]) * (0.5 / (HF * HF)))
        sfreq[4 * i] = cc - ss
        sfreq[4 * i + 1] = sc + cs
        sfreq[4 * i + 2] = cc + ss
        sfreq[4 * i + 3] = sc - cs

    def back_to_pixels(aa, bb, a2, b2):
        u = dot(whole(aa + a2, bb - b2, bb + b2, a2 - aa).astype(bf16), r[...]).astype(bf16)
        return dot(rt[...], u)

    def forward(i):
        inten[...] = jnp.zeros((W, W), f32)

        def channel(c, _):
            p, q, p2, q2 = (sfreq[4 * i + j] for j in range(4))
            m, n, m2, n2 = (spec[c, j] for j in range(4))
            e = back_to_pixels(p * m - q * n, p * n + q * m, p2 * m2 - q2 * n2, p2 * n2 + q2 * m2) + level[CH * i + c]
            field[c] = e
            inten[...] = inten[...] + e * e
            return 0

        lax.fori_loop(0, CH, channel, 0, unroll=unroll)

    def resist(i):
        row = lax.broadcasted_iota(jnp.int32, (W, W), 0)
        col = lax.broadcasted_iota(jnp.int32, (W, W), 1)
        inside = (row >= AM) & (row < W - AM) & (col >= AM) & (col < W - AM)
        level_at = 1.0 / (1.0 + jnp.exp(-10.0 * (inten[...] - 0.3)))
        goal = jnp.concatenate([target[pl.ds(i * 2 * W + n, W, stride=2), :] for n in range(2)], 1)
        miss = jnp.where(inside, level_at - goal, 0.0)
        loss[i] = jnp.sum(miss * miss) * (1.0 / ((W - 2 * AM) ** 2))
        inten[...] = 40.0 * miss * level_at * (1.0 - level_at)

    def backward():
        acc[...] = jnp.zeros(acc.shape, f32)

        def channel(c, _):
            g = (inten[...] * field[c]).astype(bf16)
            v = dot(g, rt[...]).astype(bf16)
            cc, cs, sc, ss = quarters(dot(r[...], v))
            p, q, p2, q2 = cc - ss, sc + cs, cc + ss, sc - cs
            m, n, m2, n2 = (spec[c, j] for j in range(4))
            acc[0] += p * m + q * n
            acc[1] += q * m - p * n
            acc[2] += p2 * m2 + q2 * n2
            acc[3] += q2 * m2 - p2 * n2
            return 0

        lax.fori_loop(0, CH, channel, 0, unroll=unroll)

    def finish(i):
        d = back_to_pixels(*(acc[j] * (0.5 / (HF * HF)) for j in range(4))).astype(bf16)
        for q in range(4):
            for part in range(2):
                for slot in range(2):
                    row = part * TS + q * 32
                    grads[i * 8 + q * 2 + part, slot] = d[row : row + 32, slot * TS : slot * TS + TS]

    def to_planes(i):
        for j in (1, 2, 3):
            p = (plane + j) % 4
            for part in range(2):
                send(grads.at[i * 8 + p * 2 + part], across.at[i * 8 + part * 4 + plane], xs, xr.at[i], p, owner)
        for part in range(2):
            across[i * 8 + part * 4 + plane] = grads[i * 8 + plane * 2 + part]

    def to_line(i):
        drain(across, 6, xr.at[i])
        for j in (1, 3, 2):
            for part in range(2):
                pa, pb = (z, y) if part == 0 else (y, z)
                here = across.at[pl.ds(i * 8 + part * 4, 4)]
                send(here, lines[j].at[pl.ds(part * 8 + i * 4, 4)], gs, gr.at[i * 4 + j],
                    plane, at(part, (pa + j) % 4, pb, core))

    def to_planes_and_line(i):
        for j in (0, 1, 3, 2):
            for q in (1, 3, 2, 0):
                p = (plane + q) % 4
                for part in range(2):
                    pa, pb = (z, y) if part == 0 else (y, z)
                    src = grads.at[i * 8 + p * 2 + part]
                    if j:
                        send(src, lines[j].at[part * 8 + i * 4 + plane], gs, gr.at[i * 4 + j],
                            p, at(part, (pa + j) % 4, pb, core))
                    elif q:
                        send(src, across.at[i * 8 + part * 4 + plane], xs, xr.at[i], p, owner)
        for part in range(2):
            across[i * 8 + part * 4 + plane] = grads[i * 8 + plane * 2 + part]
        drain(across, 6, xr.at[i])

    def to_owners(j, part, step):
        pa, pb = (z, y) if part == 0 else (y, z)
        b2 = (pb + j) % 4
        goal = pa * 4 + b2 if part == 0 else b2 * 4 + pa

        def one(n, _):
            source = n * 32 + at(part, (pa - step) % 4, pb, core)
            which = jnp.where(first[0, 2 * source + 1] >> 7 == goal, 1, 0)
            place = part * 64 + b2 * 16 + step * 4 + n
            if step == 0:
                back[place] = across[which * 8 + part * 4 + n]
            else:
                back[place] = lines[step][part * 8 + which * 4 + n]
            return 0

        lax.fori_loop(0, 4, one, 0, unroll=4)
        src = back.at[pl.ds(part * 64 + b2 * 16 + step * 4, 4)]
        dst = got.at[pl.ds((pb * 2 + core) * 16 + step * 4, 4)]
        if j:
            send(src, dst, bs, br, plane, at(part, pa, b2, part))
        else:

            @pl.when(core == part)
            def _():
                pltpu.make_async_copy(src, dst, ls).start()

            @pl.when(core != part)
            def _():
                send(src, dst, bs, br, plane, owner + 1 - 2 * core)

    drain(recv[0], 7, s2r.at[0])
    transform(0)
    forward(0)
    resist(0)
    drain(recv[1], 7, s2r.at[1])
    transform(1)
    backward()
    finish(0)
    to_planes(0)
    forward(1)
    to_line(0)
    resist(1)
    backward()
    finish(1)
    to_planes_and_line(1)
    for step in (0, 1, 3, 2):
        if step:
            drain(lines[step], 8, gr.at[step])
            drain(lines[step], 8, gr.at[4 + step])
        for j in (2, 1, 3, 0):
            for part in range(2):
                to_owners(j, part, step)
    drain(out, 24, s1s)
    drain(mid, 14, s2s)
    drain(grads, 12, xs)
    drain(back, 48, gs)
    drain(back, 112, bs)
    drain(got, 16, ls)
    drain(got, 112, br)


def sum_kernel(first, losses, got, out, loss, held, total, rows, ins, outs):
    owner = lax.axis_index("owner")
    chip = owner // 2
    core = owner % 2
    here = (owner >> 3) + core * (((owner >> 1) & 3) - (owner >> 3))
    loads = [pltpu.make_async_copy(got.at[pl.ds(16 * n, 16)], held.at[pl.ds(16 * n, 16)], ins.at[n]) for n in range(8)]
    for load in loads:
        load.start()
    total[...] = jnp.zeros(total.shape, f32)

    def step(s, _):
        line = (here - (s >> 2)) & 3
        source = (s & 3) * 32 + line * (8 - 6 * core) + (s >> 5) * (2 + 6 * core) + ((s >> 4) & 1)
        near = first[0, 2 * source]
        far = first[0, 2 * source + 1]
        mine = jnp.where(near >> 7 == chip, near, far)
        column = jnp.where(mine >> 7 == chip, jnp.minimum(mine & 63, 62), 64)
        for n in range(2):
            total[pl.ds(pl.multiple_of((column + n) * 40, 8), 32), :] += held[s, n].astype(f32)
        return 0

    for n in range(8):
        loads[n].wait()
        lax.fori_loop(16 * n, 16 * n + 16, step, 0, unroll=16)
    stores = []
    for t in range(8):
        for j in range(32):
            rows[8 * t : 8 * t + 8, 128 * j : 128 * j + 128] = total[pl.ds(320 * t + j, 8, stride=40), :]
        store = pltpu.make_async_copy(rows.at[pl.ds(8 * t, 8)], out.at[pl.ds(8 * t, 8)], outs.at[t])
        store.start()
        stores.append(store)
    for i in range(2):
        loss[i] = losses[i]
    for store in stores:
        store.wait()


def body(mask_tiles, correlation, target, socs_kernels, socs_weights):
    first = correlation.T
    Rb, RTb, T3, TB = tables()
    S = pl.BlockSpec(memory_space=pltpu.SMEM)
    A = pl.BlockSpec(memory_space=pl.ANY)
    D = pltpu.SemaphoreType.DMA
    got, losses = pl.pallas_call(
        functools.partial(step_kernel, 24),
        out_shape=(jax.ShapeDtypeStruct((128, 2, 32, TS), bf16), jax.ShapeDtypeStruct((2,), f32)),
        in_specs=[S, S] + [A] * 7,
        out_specs=(A, S),
        scratch_shapes=[
            pltpu.VMEM((64, TS * TS), bf16),
            pltpu.VMEM((64, PITCH, TS), f32),
            pltpu.VMEM((2, W * W), bf16),
            pltpu.VMEM((4 * W, TS), f32),
            pltpu.VMEM((NK, KS, 2, KS), f32),
            pltpu.VMEM((W, W), bf16),
            pltpu.VMEM((W, W), bf16),
            pltpu.VMEM((W, 48), bf16),
            pltpu.VMEM((128, W), f32),
            pltpu.VMEM((W, W), f32),
            pltpu.VMEM((32, 2, TS, TS), bf16),
            *[pltpu.VMEM((8, 2, TS, TS), bf16)] * 4,
            pltpu.VMEM((16, 2, TS, TS), bf16),
            *[pltpu.VMEM((8, 2, TS, TS), bf16)] * 2,
            pltpu.VMEM((16, 2, 32, TS), bf16),
            pltpu.VMEM((16, 2, 32, TS), bf16),
            *[pltpu.VMEM((16, 2, 32, TS), bf16)] * 3,
            pltpu.VMEM((128, 2, 32, TS), bf16),
            pltpu.VMEM((CH, 16, 128), f32),
            pltpu.VMEM((CH, 48, W), bf16),
            pltpu.VMEM((CH, 4, HF, HF), f32),
            pltpu.VMEM((8, HF, HF), f32),
            pltpu.VMEM((4, HF, HF), f32),
            pltpu.VMEM((CH, W, W), f32),
            pltpu.VMEM((W, W), f32),
            pltpu.VMEM((2 * CH, 1, W), f32),
            *[pltpu.VMEM((CH, 1, W), f32)] * 2,
            D((10,)), D, D((4,)), D, D((2,)), D, D((2,)), D, D((8,)), D, D, D,
        ],
        compiler_params=pltpu.CompilerParams(vmem_limit_bytes=56 * 2**20, collective_id=0, has_side_effects=True),
    )(first, socs_weights, mask_tiles, target, socs_kernels.transpose(1, 2, 0, 3),
        jnp.asarray(Rb), jnp.asarray(RTb), jnp.asarray(T3), jnp.asarray(TB))
    return pl.pallas_call(sum_kernel,
        out_shape=(jax.ShapeDtypeStruct((64, 4096), f32), jax.ShapeDtypeStruct((2,), f32)),
        in_specs=[S, S, A], out_specs=(A, S),
        scratch_shapes=[pltpu.VMEM((128, 2, 32, TS), bf16), pltpu.VMEM((66 * 40, TS), f32), pltpu.VMEM((64, 4096), f32), D((8,)), D((8,))],
    )(first, losses, got)


def solution(mesh):
    placed = (P("owner", None), P(), P(("clip", "owner"), None), P(), P())
    return jax.shard_map(body, mesh=mesh, in_specs=placed,
        out_specs=(P("owner", "clip"), P(("clip", "owner"))), check_vma=False)
```

```python
import functools

import jax
import jax.numpy as jnp
import ml_dtypes
import numpy as np
from jax import lax
from jax.experimental import pallas as pl
from jax.experimental.pallas import tpu as pltpu
from jax.sharding import PartitionSpec as P

TS=128; W=256; HF=128; KS=15; AM=7; NK=12; CH=24
PITCH = 136
MESH = pl.DeviceIdType.MESH
f32=jnp.float32; bf16=jnp.bfloat16

def tables():
    u = np.arange(HF) + 0.5
    y = np.arange(W)
    ang = 2*np.pi*u[:,None]*y[None,:]/W
    R = np.concatenate([np.cos(ang), np.sin(ang)], 0)
    b = np.arange(KS)-AM
    ang2 = 2*np.pi*u[:,None]*b[None,:]/W
    T = np.concatenate([np.cos(ang2), np.sin(ang2)], 0)
    T16 = np.zeros((W,16)); T16[:,:KS]=T
    hi = T16.astype(np.float32).astype(ml_dtypes.bfloat16)
    lo = (T16-hi.astype(np.float64)).astype(np.float32).astype(ml_dtypes.bfloat16)
    T3 = np.concatenate([hi,hi,lo],1)
    TB = np.zeros((W, 128)); TB[:,:KS]=T
    TB = TB.T.astype(np.float32)
    Rb = R.astype(np.float32).astype(ml_dtypes.bfloat16)
    return Rb, np.ascontiguousarray(Rb.T), T3, TB

def dot(a,b):
    return jnp.dot(a,b,preferred_element_type=f32)


def quarters(s):
    return s[:HF, :HF], s[:HF, HF:], s[HF:, :HF], s[HF:, HF:]


def whole(cc, cs, sc, ss):
    return jnp.concatenate([jnp.concatenate([cc, cs], 1), jnp.concatenate([sc, ss], 1)], 0)


def step_kernel(unroll, first, sw, mask_in, target_in, taps_in, r_in, rt_in, t3_in, tb_in, got, loss,
        raw, mask, wide, target, taps, r, rt, t3, tb, rsum, out, held0, held1, held2, held3, mid, recv0, recv1, grads, across, line1, line2, line3, back, pad, taph, spec, sfreq, acc, field, inten, level, flow, amp,
        ins, s1s, s1r, s2s, s2r, xs, xr, gs, gr, bs, br, ls):
    held = (held0, held1, held2, held3)
    recv = (recv0, recv1)
    lines = (None, line1, line2, line3)
    plane = lax.axis_index("clip")
    owner = lax.axis_index("owner")
    me = plane * 32 + owner
    chip = owner // 2
    core = owner % 2
    y = chip % 4
    z = chip // 4

    def at(route, a, b, c):
        return a * (8 - 6 * route) + b * (2 + 6 * route) + c

    def drain(ref, count, sem):
        part = ref.at[pl.ds(0, count)]
        pltpu.make_async_copy(part, part, sem).wait()

    def send(src, dst, send_sem, recv_sem, p, to):
        pltpu.make_async_remote_copy(src_ref=src, dst_ref=dst, send_sem=send_sem, recv_sem=recv_sem,
            device_id=(p, to), device_id_type=MESH).start()

    loads = [pltpu.make_async_copy(mask_in.at[pl.ds(16 * n, 16)], raw.at[pl.ds(16 * n, 16)], ins.at[n]) for n in range(4)]
    loads += [
        pltpu.make_async_copy(src, dst, ins.at[4 + n])
        for n, (src, dst) in enumerate(((taps_in, taps), (tb_in, tb), (t3_in, t3), (target_in, wide), (r_in, r), (rt_in, rt)))
    ]
    for load in loads:
        load.start()

    barrier = pltpu.get_barrier_semaphore()
    partners = [(plane, owner + 1 - 2 * core)]
    for j in (1, 2, 3):
        partners.append(((plane + j) % 4, owner))
        for c in range(2):
            partners.append((plane, at(0, (z + j) % 4, y, c)))
            partners.append((plane, at(0, z, (y + j) % 4, c)))
    for j in (1, 2, 3):
        for p in (1, 2, 3):
            partners.append(((plane + p) % 4, at(0, (z + j) % 4, y, core)))
            partners.append(((plane + p) % 4, at(0, z, (y + j) % 4, core)))
    for to in partners:
        pl.semaphore_signal(barrier, inc=1, device_id=to, device_id_type=MESH)

    a = z + core * (y - z)
    b = y + core * (z - y)

    def pick(k):
        b2 = (b + 1 + k) % 4

        def one(n, _):
            a2 = (a + n // 2) % 4
            c = n % 2
            dest = plane * 32 + at(core, a2, b2, c)
            near = first[0, 2 * dest]
            far = first[0, 2 * dest + 1]
            column = jnp.minimum(jnp.where(near >> 7 == chip, near, far) & 63, 62)
            slot = a2 * 8 + b2 * 2 + c
            for n2 in range(2):
                out[slot, n2] = mask[column + n2, :TS].astype(bf16)
            return 0

        lax.fori_loop(0, 8, one, 0)

    def first_stage(k):
        b2 = (b + 1 + k) % 4
        for j in (2, 1, 3):
            a2 = (a + j) % 4
            send(out.at[pl.ds(a2 * 8 + b2 * 2, 2)], held[k].at[pl.ds(a * 2, 2)], s1s, s1r.at[k],
                plane, at(core, a2, b, core))
        for c in range(2):
            held[k][a * 2 + c] = out[a * 8 + b2 * 2 + c]

    def second_stage(k, i):
        if i == 0:
            drain(held[k], 6, s1r.at[k])
        b2 = (b + 1 + k) % 4
        if True:
            for c in range(2):
                dest = plane * 32 + at(core, a, b2, c)
                pair = first[0, 2 * dest + i] >> 7
                from_z = pair >> 2
                from_a = from_z + core * ((pair & 3) - from_z)
                mid[b2 * 4 + c * 2 + i] = held[k][from_a * 2 + c]
            if k < 3:
                for c in range(2):
                    send(mid.at[b2 * 4 + c * 2 + i], recv[i].at[core * 4 + b], s2s, s2r.at[i],
                        plane, at(core, a, b2, c))
            else:
                send(mid.at[b2 * 4 + (1 - core) * 2 + i], recv[i].at[core * 4 + b], s2s, s2r.at[i],
                    plane, owner + 1 - 2 * core)
                recv[i][core * 4 + b] = mid[b2 * 4 + core * 2 + i]

    flat = mask.reshape(64 * PITCH, TS)
    for n in range(4):
        loads[n].wait()

        def rows(j, _):
            v = raw[16 * n : 16 * n + 16, pl.ds(pl.multiple_of(j * TS, TS), TS)].astype(f32)
            flat[pl.ds(16 * n * PITCH + j, 8, stride=PITCH), :] = v[:8]
            flat[pl.ds((16 * n + 8) * PITCH + j, 8, stride=PITCH), :] = v[8:]
            return 0

        lax.fori_loop(0, TS, rows, 0, unroll=8)

    pick(0)
    pl.semaphore_wait(barrier, len(partners))
    first_stage(0)
    for k in (1, 2, 3):
        pick(k)
        first_stage(k)

    for load in loads[4:7]:
        load.wait()
    pad[...] = jnp.zeros(pad.shape, f32)
    for c in range(CH):
        pad[c, :KS, :KS] = taps[c % NK, :, c // NK, :]
        amp[c] = jnp.full((1, W), jnp.sqrt(sw[c % NK] * (1.0 / NK)))
    flow[...] = jnp.broadcast_to(
        jnp.sum(jnp.sum(pad[...], axis=1, keepdims=True), axis=2, keepdims=True), flow.shape)
    m = jnp.dot((pad[...] * amp[:, :, :128]).reshape(CH * 16, 128), tb[...], precision=lax.Precision.HIGHEST,
        preferred_element_type=f32).reshape(CH, 16, W)
    high = m.astype(bf16)
    taph[:, 0:16, :] = high
    taph[:, 16:32, :] = (m - high.astype(f32)).astype(bf16)
    taph[:, 32:48, :] = high

    def spectrum(c, _):
        cc, cs, sc, ss = quarters(dot(t3[...], taph[c]))
        spec[c, 0] = cc - ss
        spec[c, 1] = sc + cs
        spec[c, 2] = cc + ss
        spec[c, 3] = sc - cs
        return 0

    for k in range(4):
        second_stage(k, 0)
        if k < 3:
            lax.fori_loop(8 * k, 8 * k + 8, spectrum, 0, unroll=8)

    for k in range(4):
        second_stage(k, 1)
    for load in loads[7:]:
        load.wait()

    def widen(n, _):
        target[pl.ds(n, 2, stride=2 * W), :] = wide[:, pl.ds(pl.multiple_of(n * TS, TS), TS)].astype(f32)
        return 0

    lax.fori_loop(0, 2 * W, widen, 0, unroll=8)
    rsum[...] = dot(r[...], jnp.full((W, W), 1.0, bf16))

    def transform(i):
        pair = first[0, 2 * me + i] >> 7
        top = recv[i][pair & 3]
        low = recv[i][4 + (pair >> 2)]
        x = whole(top[0], top[1], low[0], low[1])
        sums = jnp.sum(x.astype(f32), axis=0, keepdims=True)
        rounded = sums.astype(bf16).astype(f32)
        t = (dot(r[...], x) - rsum[...] * (0.5 - (rounded - sums) * (1.0 / W))).astype(bf16)
        zero = flow[...] * jnp.sum(rounded)
        level[...] = amp[...] * (0.5 * flow[...] + (zero.astype(bf16).astype(f32) - zero) * (1.0 / (W * W)))
        cc, cs, sc, ss = quarters(dot(t, rt[...]) * (0.5 / (HF * HF)))
        sfreq[0] = cc - ss
        sfreq[1] = sc + cs
        sfreq[2] = cc + ss
        sfreq[3] = sc - cs

    def back_to_pixels(aa, bb, a2, b2):
        u = dot(whole(aa + a2, bb - b2, bb + b2, a2 - aa).astype(bf16), r[...]).astype(bf16)
        return dot(rt[...], u)

    def forward():
        inten[...] = jnp.zeros((W, W), f32)

        def channel(c, _):
            p, q, p2, q2 = (sfreq[j] for j in range(4))
            m, n, m2, n2 = (spec[c, j] for j in range(4))
            e = back_to_pixels(p * m - q * n, p * n + q * m, p2 * m2 - q2 * n2, p2 * n2 + q2 * m2) + level[c]
            field[c] = e
            inten[...] = inten[...] + e * e
            return 0

        lax.fori_loop(0, CH, channel, 0, unroll=unroll)

    def resist(i):
        row = lax.broadcasted_iota(jnp.int32, (W, W), 0)
        col = lax.broadcasted_iota(jnp.int32, (W, W), 1)
        inside = (row >= AM) & (row < W - AM) & (col >= AM) & (col < W - AM)
        level_at = 1.0 / (1.0 + jnp.exp(-10.0 * (inten[...] - 0.3)))
        goal = jnp.concatenate([target[pl.ds(i * 2 * W + n, W, stride=2), :] for n in range(2)], 1)
        miss = jnp.where(inside, level_at - goal, 0.0)
        loss[i] = jnp.sum(miss * miss) * (1.0 / ((W - 2 * AM) ** 2))
        inten[...] = 40.0 * miss * level_at * (1.0 - level_at)

    def backward():
        acc[...] = jnp.zeros(acc.shape, f32)

        def channel(c, _):
            g = (inten[...] * field[c]).astype(bf16)
            v = dot(g, rt[...]).astype(bf16)
            cc, cs, sc, ss = quarters(dot(r[...], v))
            p, q, p2, q2 = cc - ss, sc + cs, cc + ss, sc - cs
            m, n, m2, n2 = (spec[c, j] for j in range(4))
            acc[0] += p * m + q * n
            acc[1] += q * m - p * n
            acc[2] += p2 * m2 + q2 * n2
            acc[3] += q2 * m2 - p2 * n2
            return 0

        lax.fori_loop(0, CH, channel, 0, unroll=unroll)

    def finish(i):
        d = back_to_pixels(*(acc[j] * (0.5 / (HF * HF)) for j in range(4))).astype(bf16)
        for q in range(4):
            for part in range(2):
                for slot in range(2):
                    row = part * TS + q * 32
                    grads[i * 8 + q * 2 + part, slot] = d[row : row + 32, slot * TS : slot * TS + TS]

    def to_planes(i):
        for j in (1, 2, 3):
            p = (plane + j) % 4
            for part in range(2):
                send(grads.at[i * 8 + p * 2 + part], across.at[i * 8 + part * 4 + plane], xs, xr.at[i], p, owner)
        for part in range(2):
            across[i * 8 + part * 4 + plane] = grads[i * 8 + plane * 2 + part]

    def to_line(i):
        drain(across, 6, xr.at[i])
        for j in (1, 3, 2):
            for part in range(2):
                pa, pb = (z, y) if part == 0 else (y, z)
                here = across.at[pl.ds(i * 8 + part * 4, 4)]
                send(here, lines[j].at[pl.ds(part * 8 + i * 4, 4)], gs, gr.at[i * 4 + j],
                    plane, at(part, (pa + j) % 4, pb, core))

    def to_planes_and_line(i):
        for j in (0, 1, 3, 2):
            for q in (1, 3, 2, 0):
                p = (plane + q) % 4
                for part in range(2):
                    pa, pb = (z, y) if part == 0 else (y, z)
                    src = grads.at[i * 8 + p * 2 + part]
                    if j:
                        send(src, lines[j].at[part * 8 + i * 4 + plane], gs, gr.at[i * 4 + j],
                            p, at(part, (pa + j) % 4, pb, core))
                    elif q:
                        send(src, across.at[i * 8 + part * 4 + plane], xs, xr.at[i], p, owner)
        for part in range(2):
            across[i * 8 + part * 4 + plane] = grads[i * 8 + plane * 2 + part]
        drain(across, 6, xr.at[i])

    def to_owners(j, part, step):
        pa, pb = (z, y) if part == 0 else (y, z)
        b2 = (pb + j) % 4
        goal = pa * 4 + b2 if part == 0 else b2 * 4 + pa

        def one(n, _):
            source = n * 32 + at(part, (pa - step) % 4, pb, core)
            which = jnp.where(first[0, 2 * source + 1] >> 7 == goal, 1, 0)
            place = part * 64 + b2 * 16 + step * 4 + n
            if step == 0:
                back[place] = across[which * 8 + part * 4 + n]
            else:
                back[place] = lines[step][part * 8 + which * 4 + n]
            return 0

        lax.fori_loop(0, 4, one, 0, unroll=4)
        src = back.at[pl.ds(part * 64 + b2 * 16 + step * 4, 4)]
        dst = got.at[pl.ds((pb * 2 + core) * 16 + step * 4, 4)]
        if j:
            send(src, dst, bs, br, plane, at(part, pa, b2, part))
        else:

            @pl.when(core == part)
            def _():
                pltpu.make_async_copy(src, dst, ls).start()

            @pl.when(core != part)
            def _():
                send(src, dst, bs, br, plane, owner + 1 - 2 * core)

    drain(recv[0], 7, s2r.at[0])
    transform(0)
    forward()
    resist(0)
    backward()
    finish(0)
    to_planes(0)
    drain(recv[1], 7, s2r.at[1])
    transform(1)
    forward()
    to_line(0)
    resist(1)
    backward()
    finish(1)
    to_planes_and_line(1)
    for step in (0, 1, 3, 2):
        if step:
            drain(lines[step], 8, gr.at[step])
            drain(lines[step], 8, gr.at[4 + step])
        for j in (2, 1, 3, 0):
            for part in range(2):
                to_owners(j, part, step)
    drain(out, 24, s1s)
    drain(mid, 14, s2s)
    drain(grads, 12, xs)
    drain(back, 48, gs)
    drain(back, 112, bs)
    drain(got, 16, ls)
    drain(got, 112, br)


def sum_kernel(first, losses, got, out, loss, held, total, rows, ins, outs):
    owner = lax.axis_index("owner")
    chip = owner // 2
    core = owner % 2
    here = (owner >> 3) + core * (((owner >> 1) & 3) - (owner >> 3))
    loads = [pltpu.make_async_copy(got.at[pl.ds(16 * n, 16)], held.at[pl.ds(16 * n, 16)], ins.at[n]) for n in range(8)]
    for load in loads:
        load.start()
    total[...] = jnp.zeros(total.shape, f32)

    def step(s, _):
        line = (here - (s >> 2)) & 3
        source = (s & 3) * 32 + line * (8 - 6 * core) + (s >> 5) * (2 + 6 * core) + ((s >> 4) & 1)
        near = first[0, 2 * source]
        far = first[0, 2 * source + 1]
        mine = jnp.where(near >> 7 == chip, near, far)
        column = jnp.where(mine >> 7 == chip, jnp.minimum(mine & 63, 62), 64)
        for n in range(2):
            total[pl.ds(pl.multiple_of((column + n) * 40, 8), 32), :] += held[s, n].astype(f32)
        return 0

    for n in range(8):
        loads[n].wait()
        lax.fori_loop(16 * n, 16 * n + 16, step, 0, unroll=16)
    stores = []
    for t in range(8):
        for j in range(32):
            rows[8 * t : 8 * t + 8, 128 * j : 128 * j + 128] = total[pl.ds(320 * t + j, 8, stride=40), :]
        store = pltpu.make_async_copy(rows.at[pl.ds(8 * t, 8)], out.at[pl.ds(8 * t, 8)], outs.at[t])
        store.start()
        stores.append(store)
    for i in range(2):
        loss[i] = losses[i]
    for store in stores:
        store.wait()


def body(mask_tiles, correlation, target, socs_kernels, socs_weights):
    first = correlation.T
    Rb, RTb, T3, TB = tables()
    S = pl.BlockSpec(memory_space=pltpu.SMEM)
    A = pl.BlockSpec(memory_space=pl.ANY)
    D = pltpu.SemaphoreType.DMA
    got, losses = pl.pallas_call(
        functools.partial(step_kernel, 24),
        out_shape=(jax.ShapeDtypeStruct((128, 2, 32, TS), bf16), jax.ShapeDtypeStruct((2,), f32)),
        in_specs=[S, S] + [A] * 7,
        out_specs=(A, S),
        scratch_shapes=[
            pltpu.VMEM((64, TS * TS), bf16),
            pltpu.VMEM((64, PITCH, TS), f32),
            pltpu.VMEM((2, W * W), bf16),
            pltpu.VMEM((4 * W, TS), f32),
            pltpu.VMEM((NK, KS, 2, KS), f32),
            pltpu.VMEM((W, W), bf16),
            pltpu.VMEM((W, W), bf16),
            pltpu.VMEM((W, 48), bf16),
            pltpu.VMEM((128, W), f32),
            pltpu.VMEM((W, W), f32),
            pltpu.VMEM((32, 2, TS, TS), bf16),
            *[pltpu.VMEM((8, 2, TS, TS), bf16)] * 4,
            pltpu.VMEM((16, 2, TS, TS), bf16),
            *[pltpu.VMEM((8, 2, TS, TS), bf16)] * 2,
            pltpu.VMEM((16, 2, 32, TS), bf16),
            pltpu.VMEM((16, 2, 32, TS), bf16),
            *[pltpu.VMEM((16, 2, 32, TS), bf16)] * 3,
            pltpu.VMEM((128, 2, 32, TS), bf16),
            pltpu.VMEM((CH, 16, 128), f32),
            pltpu.VMEM((CH, 48, W), bf16),
            pltpu.VMEM((CH, 4, HF, HF), f32),
            pltpu.VMEM((4, HF, HF), f32),
            pltpu.VMEM((4, HF, HF), f32),
            pltpu.VMEM((CH, W, W), f32),
            pltpu.VMEM((W, W), f32),
            *[pltpu.VMEM((CH, 1, W), f32)] * 3,
            D((10,)), D, D((4,)), D, D((2,)), D, D((2,)), D, D((8,)), D, D, D,
        ],
        compiler_params=pltpu.CompilerParams(vmem_limit_bytes=56 * 2**20, collective_id=0, has_side_effects=True),
    )(first, socs_weights, mask_tiles, target, socs_kernels.transpose(1, 2, 0, 3),
        jnp.asarray(Rb), jnp.asarray(RTb), jnp.asarray(T3), jnp.asarray(TB))
    return pl.pallas_call(sum_kernel,
        out_shape=(jax.ShapeDtypeStruct((64, 4096), f32), jax.ShapeDtypeStruct((2,), f32)),
        in_specs=[S, S, A], out_specs=(A, S),
        scratch_shapes=[pltpu.VMEM((128, 2, 32, TS), bf16), pltpu.VMEM((66 * 40, TS), f32), pltpu.VMEM((64, 4096), f32), D((8,)), D((8,))],
    )(first, losses, got)


def solution(mesh):
    placed = (P("owner", None), P(), P(("clip", "owner"), None), P(), P())
    return jax.shard_map(body, mesh=mesh, in_specs=placed,
        out_specs=(P("owner", "clip"), P(("clip", "owner"))), check_vma=False)
```
